32 devices in a mesh: dp: 8 (over z, x), tp: 4 (over y, core).
Axes of the slice: x: 2, y: 2, z: 4, core: 2. Of those that a mesh axis runs over, the one named last changes fastest.
Arguments:
- block_input: bfloat16 [2, 16384, 1152], P(None, ('dp', 'tp')), may hold values from -6 to 6
- segment_ids: int32 [2, 16384], P(None, 'dp'), may hold values from 0 to 3, as said below
- conditioning: bfloat16 [2, 64, 1152], P(None, 'dp'), may hold values from -6 to 6
- w_qkv: bfloat16 [3, 1152, 1152], P(None, 'dp', 'tp'), may hold values from -0.1875 to 0.1875
- qv_bias: bfloat16 [2, 1152], replicated, may hold values from -3 to 3
- w_out: bfloat16 [1152, 1152], P('tp', 'dp'), may hold values from -1.5 to 1.5
- out_bias: bfloat16 [1152], replicated, may hold values from -3 to 3
- w_fc1: bfloat16 [1152, 4608], P('dp', 'tp'), may hold values from -0.1875 to 0.1875
- fc1_bias: bfloat16 [4608], replicated, may hold values from -3 to 3
- w_fc2: bfloat16 [4608, 1152], P('tp', 'dp'), may hold values from -0.09375 to 0.09375
- fc2_bias: bfloat16 [1152], replicated, may hold values from -3 to 3
- w_ada: bfloat16 [1152, 6912], P('dp', 'tp'), may hold values from -0.1875 to 0.1875
- ada_bias: bfloat16 [6912], replicated, may hold values from -3 to 3
- cotangent: bfloat16 [2, 16384, 1152], P(None, ('dp', 'tp')), may hold values from -6 to 6
Outputs:
- block_output: bfloat16 [2, 16384, 1152], P(None, ('dp', 'tp'))
- input_grad: bfloat16 [2, 16384, 1152], P(None, ('dp', 'tp'))
- w_qkv_grad: float32 [3, 1152, 1152], P(None, 'dp', 'tp')
- qv_bias_grad: float32 [2, 1152], replicated
- w_out_grad: float32 [1152, 1152], P('tp', 'dp')
- out_bias_grad: float32 [1152], replicated
- w_fc1_grad: float32 [1152, 4608], P('dp', 'tp')
- fc1_bias_grad: float32 [4608], replicated
- w_fc2_grad: float32 [4608, 1152], P('tp', 'dp')
- fc2_bias_grad: float32 [1152], replicated
- w_ada_grad: float32 [1152, 6912], P('dp', 'tp')
- ada_bias_grad: float32 [6912], replicated
The draws below stay inside these ranges and needn't reach their ends.
Inputs may be any that keep to these rules, and one draw needn't show every extreme that they name: `segment_ids`: within each packed row of 1024 tokens the ids never fall, and every image of the row holds at least one token.
All inputs are finite; a program needn't handle non-finite values.
Results may differ from the reference program's by a relative error of at most 0.02.
The reference program's roundings to bfloat16 on the way count: a program that leaves them out, or rounds other values in their place, can miss the bound.
Values may be sent and summed in bfloat16 or wider, within the bound.
No kernel may reach another device: no remote copies, remote signals or barrier semaphores. Data moves between devices by JAX's collectives and lax.ppermute only.
A program may use at most 320 MiB of HBM per device.

```python
import math
import jax
import jax.numpy as jnp
from jax import lax

D = 1152
HEADS = 16
HD = 72
FF = 4608
COND = 1152
PACK = 1024
IMG_ROW = 4
MICRO = 2
TOKENS = 16384
IMAGES = 64
N_TP = 4


def draw_segment_ids(key, part):
    key = jax.random.fold_in(key, 11)
    row_total = MICRO * TOKENS // PACK
    spread = PACK // 16
    offsets = jax.random.randint(key, (row_total, IMG_ROW - 1), -spread, spread + 1)
    lengths = PACK // IMG_ROW + offsets
    bounds = jnp.cumsum(lengths, axis=1)
    positions = jnp.arange(PACK, dtype=jnp.int32)
    segment_rows = jnp.sum((positions[None, None, :] >= bounds[:, :, None]).astype(jnp.int32), axis=1)
    return segment_rows.reshape(MICRO, TOKENS).astype(jnp.int32)


def levels(own_key, shape, pieces, smallest, high):
    gain = 1.0
    for position, blocks in pieces:
        heights = jax.random.uniform(jax.random.fold_in(jax.random.fold_in(own_key, 6), position), (blocks,), jnp.float32, smallest / len(pieces), high / len(pieces))
        gain = gain * jnp.repeat(jnp.exp(heights), shape[position] // blocks).reshape((-1,) + (1,) * (len(shape) - 1 - position))
    return gain


def bell_draw(key, extent, width, limit, pieces=(), kind=jnp.bfloat16):
    entries = width * jax.random.normal(key, extent, jnp.float32)
    if pieces:
        entries = entries * levels(key, extent, pieces, -0.22, 0.18)
    return jnp.clip(entries, -limit, limit).astype(kind)


def setup_inputs(seed: int = 0) -> dict:
    splits = jax.random.split(jax.random.key(seed), 15)
    block_input = bell_draw(splits[0], (MICRO, TOKENS, D), 1.0, 6.0, ((1, 32),))
    segment_ids = draw_segment_ids(jax.random.fold_in(splits[14], 71), 0)
    conditioning = bell_draw(splits[2], (MICRO, IMAGES, COND), 1.0, 6.0, ((1, 8),))
    w_qkv = bell_draw(splits[3], (3, D, D), D ** -0.5, 0.1875, ((1, 8), (2, 4)))
    qv_bias = bell_draw(splits[4], (2, D), 0.5, 3.0)
    w_out = bell_draw(splits[5], (D, D), (D // 64) ** -0.5, 1.5, ((0, 4), (1, 8)))
    out_bias = bell_draw(splits[6], (D,), 0.5, 3.0)
    w_fc1 = bell_draw(splits[7], (D, FF), D ** -0.5, 0.1875, ((0, 8), (1, 4)))
    fc1_bias = bell_draw(splits[8], (FF,), 0.5, 3.0)
    w_fc2 = bell_draw(splits[9], (FF, D), FF ** -0.5, 0.09375, ((0, 4), (1, 8)))
    fc2_bias = bell_draw(splits[10], (D,), 0.5, 3.0)
    w_ada = bell_draw(splits[11], (COND, 6 * D), COND ** -0.5, 0.1875, ((0, 8), (1, 4)))
    ada_bias = bell_draw(splits[12], (6 * D,), 0.5, 3.0)
    cotangent = bell_draw(splits[13], (MICRO, TOKENS, D), 1.0, 6.0, ((1, 32),))
    return {"block_input": block_input, "segment_ids": segment_ids, "conditioning": conditioning, "w_qkv": w_qkv, "qv_bias": qv_bias, "w_out": w_out, "out_bias": out_bias, "w_fc1": w_fc1, "fc1_bias": fc1_bias, "w_fc2": w_fc2, "fc2_bias": fc2_bias, "w_ada": w_ada, "ada_bias": ada_bias, "cotangent": cotangent}


highest = lax.Precision.HIGHEST
epsilon = 1e-06
masked_score = -1e+30

@jax.custom_vjp
def low(v):
    return lax.optimization_barrier(v.astype(jnp.bfloat16)).astype(jnp.float32)

@jax.custom_vjp
def low_back(v):
    return v

def low_keep(v):
    return (low(v), None)

def low_pass(kept, grad):
    return (grad,)

def back_keep(v):
    return (v, None)

def back_low(kept, grad):
    return (low(grad),)
low.defvjp(low_keep, low_pass)
low_back.defvjp(back_keep, back_low)

def round_both(values):
    return low(low_back(values))

def layer_norm(values):
    centred = values - lax.optimization_barrier(jnp.mean(values, axis=-1, keepdims=True))
    return centred * lax.rsqrt(lax.optimization_barrier(jnp.mean(centred * centred, axis=-1, keepdims=True)) + epsilon)

def gelu_tanh(values):
    return 0.5 * values * (1.0 + jnp.tanh(0.7978845608028654 * (values + 0.044715 * values * values * values)))

def smooth_gate(values):
    return values / (1.0 + jnp.exp(-values))

def grouped_product(values, weights, groups):
    row_count, inner_width = values.shape
    partials = jnp.einsum('pgk,gkd->gpd', values.reshape(row_count, groups, inner_width // groups), weights.reshape(groups, inner_width // groups, weights.shape[1]), precision=highest)
    return lax.optimization_barrier(jnp.sum(low(partials), axis=0))

def block_forward(params, inputs, segment_row, cond_row):
    w_qkv, qv_bias, w_out, out_bias, w_fc1, fc1_bias, w_fc2, fc2_bias, w_ada, ada_bias = params
    lifted = low(smooth_gate(cond_row))
    modulation = jnp.dot(lifted, w_ada, precision=highest) + ada_bias
    onehot = (segment_row[:, None] == jnp.arange(IMG_ROW)[None, :]).astype(jnp.float32)
    token_mod = jnp.dot(onehot, modulation, precision=highest)
    shift_one, scale_one, gate_one, shift_two, scale_two, gate_two = jnp.split(token_mod, 6, axis=1)
    normed_one = layer_norm(inputs)
    attn_in = low(normed_one * (1.0 + scale_one) + shift_one)
    query_rows = round_both(jnp.dot(attn_in, w_qkv[0], precision=highest) + qv_bias[0]).reshape(PACK, HEADS, HD)
    key_rows = round_both(jnp.dot(attn_in, w_qkv[1], precision=highest)).reshape(PACK, HEADS, HD)
    value_rows = round_both(jnp.dot(attn_in, w_qkv[2], precision=highest) + qv_bias[1]).reshape(PACK, HEADS, HD)
    scores = low_back(jnp.einsum('qhe,khe->hqk', query_rows, key_rows, precision=highest) / math.sqrt(HD))
    same_image = segment_row[:, None] == segment_row[None, :]
    scores = jnp.where(same_image[None], scores, masked_score)
    exponents = jnp.exp(scores - lax.optimization_barrier(jnp.max(scores, axis=-1, keepdims=True)))
    attn_probs = low(exponents / lax.optimization_barrier(jnp.sum(exponents, axis=-1, keepdims=True)))
    attended = round_both(jnp.einsum('hqk,khe->qhe', attn_probs, value_rows, precision=highest)).reshape(PACK, D)
    branch_one = low_back(grouped_product(attended, w_out, N_TP))
    hidden = inputs + gate_one * (branch_one + out_bias)
    normed_two = layer_norm(hidden)
    mlp_in = low(normed_two * (1.0 + scale_two) + shift_two)
    activated = low(gelu_tanh(low_back(jnp.dot(mlp_in, w_fc1, precision=highest) + fc1_bias)))
    branch_two = low_back(grouped_product(activated, w_fc2, N_TP))
    return hidden + gate_two * (branch_two + fc2_bias)

def reference(block_input, segment_ids, conditioning, w_qkv, qv_bias, w_out, out_bias, w_fc1, fc1_bias, w_fc2, fc2_bias, w_ada, ada_bias, cotangent):
    params = tuple((item_array.astype(jnp.float32) for item_array in (w_qkv, qv_bias, w_out, out_bias, w_fc1, fc1_bias, w_fc2, fc2_bias, w_ada, ada_bias)))
    row_total = MICRO * TOKENS // PACK
    inputs_all = block_input.astype(jnp.float32).reshape(row_total, PACK, D)
    segments_all = segment_ids.reshape(row_total, PACK)
    conds_all = conditioning.astype(jnp.float32).reshape(row_total, IMG_ROW, COND)
    cots_all = cotangent.astype(jnp.float32).reshape(row_total, PACK, D)

    def scan_step(totals, row_items):
        inputs, segment_row, cond_row, cot_row = row_items

        def forward_row(param_set, values):
            return block_forward(param_set, values, segment_row, cond_row)
        result, pull_back = jax.vjp(forward_row, params, inputs)
        grad_params, grad_inputs = pull_back(cot_row)
        totals = jax.tree.map(jnp.add, totals, grad_params)
        return (totals, (result.astype(jnp.bfloat16), grad_inputs.astype(jnp.bfloat16)))
    zero_grads = jax.tree.map(jnp.zeros_like, params)
    totals, (results, input_grads) = lax.scan(scan_step, zero_grads, (inputs_all, segments_all, conds_all, cots_all))
    return (results.reshape(MICRO, TOKENS, D), input_grads.reshape(MICRO, TOKENS, D), totals[0], totals[1], totals[2], totals[3], totals[4], totals[5], totals[6], totals[7], totals[8], totals[9])
```

```python
import math

import jax
import jax.numpy as jnp
from jax import lax
from jax.experimental import pallas as pl
from jax.experimental.pallas import tpu as pltpu
from jax.sharding import PartitionSpec as P

HD = 72
PACK = 1024
IMG_ROW = 4


highest = lax.Precision.HIGHEST
epsilon = 1e-06
masked_score = -1e30


def layer_norm(values):
    centred = values - jnp.mean(values, axis=-1, keepdims=True)
    return centred * lax.rsqrt(jnp.mean(centred * centred, axis=-1, keepdims=True) + epsilon)


def gelu_tanh(values):
    return (
        0.5
        * values
        * (1.0 + jnp.tanh(0.7978845608028654 * (values + 0.044715 * values * values * values)))
    )


def smooth_gate(values):
    return values / (1.0 + jnp.exp(-values))


def to_blocks(values, local_heads):
    shaped = values.reshape(values.shape[0] // PACK, PACK, local_heads, HD)
    return shaped.transpose(0, 2, 1, 3).reshape(-1, PACK, HD)


def from_blocks(blocks, local_heads):
    shaped = blocks.reshape(-1, local_heads, PACK, HD).transpose(0, 2, 1, 3)
    return shaped.reshape(-1, local_heads * HD)


def block_segments(segment_group, local_heads):
    shaped = segment_group.reshape(-1, 1, PACK)
    return jnp.broadcast_to(shaped, (shaped.shape[0], local_heads, PACK)).reshape(-1, PACK)


def project_heads(activations, full_qkv, bias_pair):
    projected = jnp.einsum("gd,cde->cge", activations, full_qkv, preferred_element_type=jnp.float32)
    bias_rows = jnp.stack([bias_pair[0], jnp.zeros_like(bias_pair[0]), bias_pair[1]])
    return (projected + bias_rows[:, None, :]).astype(jnp.bfloat16)


def masked_scores(query_rows, key_rows, segment_row):
    raw_scores = lax.dot_general(
        query_rows, key_rows, (((1,), (1,)), ((), ())), preferred_element_type=jnp.float32
    ) / math.sqrt(HD)
    same_image = segment_row[:, None] == segment_row[None, :]
    return (same_image, jnp.where(same_image, raw_scores, masked_score))


def attend_forward(block_items):
    query_rows, key_rows, value_rows, segment_row = block_items
    same_image, scores = masked_scores(query_rows, key_rows, segment_row)
    row_max = jnp.max(scores, axis=-1, keepdims=True)
    exponents = jnp.exp(scores - row_max)
    row_sums = jnp.sum(exponents, axis=-1, keepdims=True)
    probs_low = (exponents / row_sums).astype(jnp.bfloat16)
    attended = jnp.dot(probs_low, value_rows, preferred_element_type=jnp.float32).astype(
        jnp.bfloat16
    )
    return (attended, (row_max + jnp.log(row_sums))[:, 0])


def attend_backward(block_items):
    query_rows, key_rows, value_rows, segment_row, log_total, attended_grad = block_items
    same_image, scores = masked_scores(query_rows, key_rows, segment_row)
    attn_probs = jnp.where(same_image, jnp.exp(scores - log_total[:, None]), 0.0)
    value_grad = lax.dot_general(
        attn_probs.astype(jnp.bfloat16),
        attended_grad,
        (((0,), (0,)), ((), ())),
        preferred_element_type=jnp.float32,
    )
    probs_grad = lax.dot_general(
        attended_grad, value_rows, (((1,), (1,)), ((), ())), preferred_element_type=jnp.float32
    )
    centred = probs_grad - jnp.sum(attn_probs * probs_grad, axis=-1, keepdims=True)
    scores_grad = (attn_probs * centred).astype(jnp.bfloat16)
    query_grad = jnp.dot(scores_grad, key_rows, preferred_element_type=jnp.float32) / math.sqrt(HD)
    key_grad = lax.dot_general(
        scores_grad, query_rows, (((0,), (0,)), ((), ())), preferred_element_type=jnp.float32
    ) / math.sqrt(HD)
    return (
        query_grad.astype(jnp.bfloat16),
        key_grad.astype(jnp.bfloat16),
        value_grad.astype(jnp.bfloat16),
    )


def general_body(
    block_input,
    segment_ids,
    conditioning,
    w_qkv,
    qv_bias,
    w_out,
    out_bias,
    w_fc1,
    fc1_bias,
    w_fc2,
    fc2_bias,
    w_ada,
    ada_bias,
    cotangent,
):
    micro_count, tok_dev, model_width = block_input.shape
    tp_size = lax.axis_size("tp")
    tp_rank = lax.axis_index("tp")
    heads_dev = w_qkv.shape[2]
    hidden_dev = w_fc1.shape[1]
    mod_dev = w_ada.shape[1]
    cond_width = conditioning.shape[2]
    images = conditioning.shape[1]
    local_heads = heads_dev // HD
    qv_local = lax.dynamic_slice_in_dim(
        qv_bias.astype(jnp.float32), tp_rank * heads_dev, heads_dev, 1
    )
    fc1_local = lax.dynamic_slice_in_dim(
        fc1_bias.astype(jnp.float32), tp_rank * hidden_dev, hidden_dev, 0
    )
    ada_local = lax.dynamic_slice_in_dim(
        ada_bias.astype(jnp.float32), tp_rank * mod_dev, mod_dev, 0
    )
    out_bias_f = out_bias.astype(jnp.float32)
    fc2_bias_f = fc2_bias.astype(jnp.float32)
    positions = tp_rank * tok_dev + jnp.arange(tok_dev, dtype=jnp.int32)
    grad_qkv = jnp.zeros((3, model_width, heads_dev), jnp.float32)
    grad_out_w = jnp.zeros((heads_dev, model_width), jnp.float32)
    grad_fc1 = jnp.zeros((model_width, hidden_dev), jnp.float32)
    grad_fc2 = jnp.zeros((hidden_dev, model_width), jnp.float32)
    grad_ada = jnp.zeros((cond_width, mod_dev), jnp.float32)
    sum_qv = jnp.zeros((2, heads_dev), jnp.float32)
    sum_out_bias = jnp.zeros((model_width,), jnp.float32)
    sum_fc1 = jnp.zeros((hidden_dev,), jnp.float32)
    sum_fc2 = jnp.zeros((model_width,), jnp.float32)
    sum_ada = jnp.zeros((mod_dev,), jnp.float32)
    outputs = []
    input_grads = []
    for micro_step in range(micro_count):
        full_qkv, full_out, full_fc1, full_fc2, full_ada = (
            lax.all_gather(w_qkv, "dp", axis=1, tiled=True),
            lax.all_gather(w_out, "dp", axis=1, tiled=True),
            lax.all_gather(w_fc1, "dp", axis=0, tiled=True),
            lax.all_gather(w_fc2, "dp", axis=1, tiled=True),
            lax.all_gather(w_ada, "dp", axis=0, tiled=True),
        )
        lifted = smooth_gate(conditioning[micro_step].astype(jnp.float32)).astype(jnp.bfloat16)
        mod_part = jnp.dot(lifted, full_ada, preferred_element_type=jnp.float32) + ada_local
        modulation = lax.all_gather(mod_part, "tp", axis=1, tiled=True)
        segment_group = segment_ids[micro_step]
        segment_local = lax.dynamic_slice_in_dim(segment_group, tp_rank * tok_dev, tok_dev, 0)
        image_index = positions // PACK * IMG_ROW + segment_local
        onehot = (image_index[:, None] == jnp.arange(images, dtype=jnp.int32)[None, :]).astype(
            jnp.float32
        )
        token_mod = jnp.dot(onehot, modulation, precision=highest)
        shift_one, scale_one, gate_one, shift_two, scale_two, gate_two = jnp.split(
            token_mod, 6, axis=1
        )
        inputs = block_input[micro_step].astype(jnp.float32)
        normed_one = layer_norm(inputs)
        attn_in = (normed_one * (1.0 + scale_one) + shift_one).astype(jnp.bfloat16)
        attn_full = lax.all_gather(attn_in, "tp", axis=0, tiled=True)
        projected = project_heads(attn_full, full_qkv, qv_local)
        segment_blocks = block_segments(segment_group, local_heads)
        attended_blocks, log_totals = lax.map(
            attend_forward,
            (
                to_blocks(projected[0], local_heads),
                to_blocks(projected[1], local_heads),
                to_blocks(projected[2], local_heads),
                segment_blocks,
            ),
        )
        attended = from_blocks(attended_blocks, local_heads)
        branch_one = lax.psum_scatter(
            jnp.dot(attended, full_out, preferred_element_type=jnp.float32).astype(jnp.bfloat16),
            "tp",
            scatter_dimension=0,
            tiled=True,
        ).astype(jnp.float32)
        hidden = inputs + gate_one * (branch_one + out_bias_f)
        normed_two = layer_norm(hidden)
        mlp_in = (normed_two * (1.0 + scale_two) + shift_two).astype(jnp.bfloat16)
        mlp_full = lax.all_gather(mlp_in, "tp", axis=0, tiled=True)
        pre_act = jnp.dot(mlp_full, full_fc1, preferred_element_type=jnp.float32) + fc1_local
        activated = gelu_tanh(pre_act).astype(jnp.bfloat16)
        branch_two = lax.psum_scatter(
            jnp.dot(activated, full_fc2, preferred_element_type=jnp.float32).astype(jnp.bfloat16),
            "tp",
            scatter_dimension=0,
            tiled=True,
        ).astype(jnp.float32)
        outputs.append((hidden + gate_two * (branch_two + fc2_bias_f)).astype(jnp.bfloat16))
        grad_y = cotangent[micro_step].astype(jnp.float32)
        sum_fc2 = sum_fc2 + jnp.sum(gate_two * grad_y, axis=0)
        grad_gate_two = grad_y * (branch_two + fc2_bias_f)
        grad_branch_two = (gate_two * grad_y).astype(jnp.bfloat16)
        grad_two_full = lax.all_gather(grad_branch_two, "tp", axis=0, tiled=True)
        attn_back, mlp_back = (
            lax.all_gather(attn_in, "tp", axis=0, tiled=True),
            lax.all_gather(mlp_in, "tp", axis=0, tiled=True),
        )
        proj_back = project_heads(attn_back, full_qkv, qv_local)
        pre_back = jnp.dot(mlp_back, full_fc1, preferred_element_type=jnp.float32) + fc1_local
        act_back, gelu_pull = jax.vjp(gelu_tanh, pre_back)
        grad_fc2 = grad_fc2 + lax.dot_general(
            act_back.astype(jnp.bfloat16),
            grad_two_full,
            (((0,), (0,)), ((), ())),
            preferred_element_type=jnp.float32,
        )
        grad_act = lax.dot_general(
            grad_two_full, full_fc2, (((1,), (1,)), ((), ())), preferred_element_type=jnp.float32
        )
        grad_pre = gelu_pull(grad_act)[0].astype(jnp.bfloat16)
        sum_fc1 = sum_fc1 + jnp.sum(grad_pre.astype(jnp.float32), axis=0)
        grad_fc1 = grad_fc1 + lax.dot_general(
            mlp_back, grad_pre, (((0,), (0,)), ((), ())), preferred_element_type=jnp.float32
        )
        grad_mlp_in = lax.psum_scatter(
            lax.dot_general(
                grad_pre, full_fc1, (((1,), (1,)), ((), ())), preferred_element_type=jnp.float32
            ).astype(jnp.bfloat16),
            "tp",
            scatter_dimension=0,
            tiled=True,
        ).astype(jnp.float32)
        norm_two_pull = jax.vjp(layer_norm, hidden)[1]
        grad_hidden = grad_y + norm_two_pull(grad_mlp_in * (1.0 + scale_two))[0]
        sum_out_bias = sum_out_bias + jnp.sum(gate_one * grad_hidden, axis=0)
        grad_gate_one = grad_hidden * (branch_one + out_bias_f)
        grad_branch_one = (gate_one * grad_hidden).astype(jnp.bfloat16)
        grad_one_full = lax.all_gather(grad_branch_one, "tp", axis=0, tiled=True)
        grad_out_w = grad_out_w + lax.dot_general(
            attended, grad_one_full, (((0,), (0,)), ((), ())), preferred_element_type=jnp.float32
        )
        grad_attended = lax.dot_general(
            grad_one_full, full_out, (((1,), (1,)), ((), ())), preferred_element_type=jnp.float32
        ).astype(jnp.bfloat16)
        query_blocks, key_blocks, value_blocks = lax.map(
            attend_backward,
            (
                to_blocks(proj_back[0], local_heads),
                to_blocks(proj_back[1], local_heads),
                to_blocks(proj_back[2], local_heads),
                segment_blocks,
                log_totals,
                to_blocks(grad_attended, local_heads),
            ),
        )
        grad_proj = jnp.stack(
            [
                from_blocks(query_blocks, local_heads),
                from_blocks(key_blocks, local_heads),
                from_blocks(value_blocks, local_heads),
            ]
        )
        sum_qv = sum_qv + jnp.stack(
            [
                jnp.sum(grad_proj[0].astype(jnp.float32), axis=0),
                jnp.sum(grad_proj[2].astype(jnp.float32), axis=0),
            ]
        )
        grad_qkv = grad_qkv + jnp.einsum(
            "gd,cge->cde", attn_back, grad_proj, preferred_element_type=jnp.float32
        )
        grad_attn_in = lax.psum_scatter(
            jnp.einsum(
                "cge,cde->gd", grad_proj, full_qkv, preferred_element_type=jnp.float32
            ).astype(jnp.bfloat16),
            "tp",
            scatter_dimension=0,
            tiled=True,
        ).astype(jnp.float32)
        norm_one_pull = jax.vjp(layer_norm, inputs)[1]
        input_grads.append(
            (grad_hidden + norm_one_pull(grad_attn_in * (1.0 + scale_one))[0]).astype(jnp.bfloat16)
        )
        grad_token_mod = jnp.concatenate(
            [
                grad_attn_in,
                grad_attn_in * normed_one,
                grad_gate_one,
                grad_mlp_in,
                grad_mlp_in * normed_two,
                grad_gate_two,
            ],
            axis=1,
        )
        mod_grad_part = lax.dot_general(
            onehot, grad_token_mod, (((0,), (0,)), ((), ())), precision=highest
        )
        grad_mod = lax.psum_scatter(
            mod_grad_part.astype(jnp.bfloat16), "tp", scatter_dimension=1, tiled=True
        ).astype(jnp.float32)
        sum_ada = sum_ada + jnp.sum(grad_mod, axis=0)
        grad_ada = grad_ada + lax.dot_general(
            lifted.astype(jnp.float32), grad_mod, (((0,), (0,)), ((), ())), precision=highest
        )
    qkv_shard, out_shard, fc1_shard, fc2_shard, ada_shard = (
        lax.psum_scatter(
            grad_qkv.astype(jnp.bfloat16), "dp", scatter_dimension=1, tiled=True
        ).astype(jnp.float32),
        lax.psum_scatter(
            grad_out_w.astype(jnp.bfloat16), "dp", scatter_dimension=1, tiled=True
        ).astype(jnp.float32),
        lax.psum_scatter(
            grad_fc1.astype(jnp.bfloat16), "dp", scatter_dimension=0, tiled=True
        ).astype(jnp.float32),
        lax.psum_scatter(
            grad_fc2.astype(jnp.bfloat16), "dp", scatter_dimension=1, tiled=True
        ).astype(jnp.float32),
        lax.psum_scatter(
            grad_ada.astype(jnp.bfloat16), "dp", scatter_dimension=0, tiled=True
        ).astype(jnp.float32),
    )
    qv_full = lax.dynamic_update_slice_in_dim(
        jnp.zeros((2, model_width), jnp.float32), sum_qv, tp_rank * heads_dev, 1
    )
    fc1_full = lax.dynamic_update_slice_in_dim(
        jnp.zeros((hidden_dev * tp_size,), jnp.float32), sum_fc1, tp_rank * hidden_dev, 0
    )
    ada_full = lax.dynamic_update_slice_in_dim(
        jnp.zeros((mod_dev * tp_size,), jnp.float32), sum_ada, tp_rank * mod_dev, 0
    )
    qv_total, out_total, fc1_total, fc2_total, ada_total = lax.psum(
        (qv_full, sum_out_bias, fc1_full, sum_fc2, ada_full), ("dp", "tp")
    )
    return (
        jnp.stack(outputs),
        jnp.stack(input_grads),
        qkv_shard,
        qv_total,
        out_shard,
        out_total,
        fc1_shard,
        fc1_total,
        fc2_shard,
        fc2_total,
        ada_shard,
        ada_total,
    )


f32, bf16 = jnp.float32, jnp.bfloat16
AXES = ("dp", "tp")
CORE, CHIP = 1, 2
ROWS = 144
QT = 256
ET = 128
LOG2E = 1.4426950408889634
GELU_A = 0.7978845608028654
GELU_B = 0.7978845608028654 * 0.044715
VMEM_BYTES = 56 * 2**20
NN = (((1,), (0,)), ((), ()))
NT = (((1,), (1,)), ((), ()))
SMEM_SPEC = pl.BlockSpec(memory_space=pltpu.SMEM)
VMEM_SPEC = pl.BlockSpec(memory_space=pltpu.VMEM)
ANY_SPEC = pl.BlockSpec(memory_space=pl.ANY)


def dot(left, right, dims=NN):
    return lax.dot_general(left, right, dims, preferred_element_type=f32)


def compiler_params():
    return pltpu.CompilerParams(vmem_limit_bytes=VMEM_BYTES)


def swap(values, dp_mask, tp_mask):
    pairs = [(d * 4 + t, (d ^ dp_mask) * 4 + (t ^ tp_mask)) for d in range(8) for t in range(4)]
    return lax.ppermute(values, AXES, pairs)


def across(values, tp_mask):
    return swap(values, 0, tp_mask)


def tie(values, after):
    count = len(values)
    return pl.pallas_call(
        lambda *refs: None,
        in_specs=[ANY_SPEC] * (count + len(after)),
        out_specs=[ANY_SPEC] * count,
        out_shape=[jax.ShapeDtypeStruct(v.shape, v.dtype) for v in values],
        input_output_aliases={i: i for i in range(count)},
    )(*values, *after)


def fetch(whole_ref, block, column, out_ref, sem):
    width = out_ref.shape[1]
    return [
        pltpu.make_async_copy(
            whole_ref.at[d * 4 + block, :, pl.ds(column, width)],
            out_ref.at[pl.ds(d * ROWS, ROWS), :],
            sem.at[d],
        )
        for d in range(8)
    ]


def send_pieces(stage, place_ref, first, count, outs, sem):
    for q in range(count):
        source = stage.at[pl.ds(q * ROWS, ROWS), :]
        spot = place_ref[first + q]

        @pl.when(spot < 4)
        def _():
            pltpu.make_async_copy(source, outs[0].at[spot], sem.at[q]).start()

        @pl.when(spot >= 4)
        def _():
            pltpu.make_async_copy(source, outs[1].at[spot - 4], sem.at[q]).start()


def wait_pieces(stage, count, outs, sem):
    for q in range(count):
        pltpu.make_async_copy(stage.at[pl.ds(q * ROWS, ROWS), :], outs[0].at[0], sem.at[q]).wait()


def mlp_body(added, waits, tok_steps, *refs):
    block_ref, x_ref, g_ref, xt_ref, gt_ref, whole_ref, b_ref = refs[:7]
    init_ref = refs[7] if added else None
    b2_ref, dm_ref, db_ref, dw_ref, w1_ref, w2_ref, act_s, slope_s, sem = refs[7 + added + waits :]
    step = pl.program_id(0)
    rows = x_ref.shape[0]
    ff = w1_ref.shape[1]

    @pl.when(step == 0)
    def _():
        copies = fetch(whole_ref, block_ref[0], 0, w1_ref, sem.at[0])
        copies += fetch(whole_ref, block_ref[0], ff, w2_ref, sem.at[1])
        for copy in copies:
            copy.start()
        for copy in copies:
            copy.wait()

    @pl.when(step < tok_steps)
    def _():
        pre = dot(x_ref[...], w1_ref[...]) + b_ref[...]
        act_grad = dot(g_ref[...], w2_ref[...])
        square = pre * pre
        bend = jnp.tanh(pre * (GELU_A + GELU_B * square))
        half = 0.5 + 0.5 * bend
        act = (pre * half).astype(bf16)
        slope = half + pre * (half * (1.0 - bend)) * (GELU_A + (3 * GELU_B) * square)
        pre_grad = (act_grad * slope).astype(bf16)
        b2_ref[...] = dot(act, w2_ref[...], NT).astype(bf16)
        dm_ref[...] = dot(pre_grad, w1_ref[...], NT).astype(bf16)
        here = pl.ds(pl.multiple_of(step * rows, rows), rows)
        act_s[here, :] = act
        slope_s[here, :] = pre_grad
        sums = jnp.sum(pre_grad.astype(f32), axis=0, keepdims=True)

        @pl.when(step == 0)
        def _():
            db_ref[...] = sums

        @pl.when(step > 0)
        def _():
            db_ref[...] += sums

    @pl.when(step >= tok_steps)
    def _():
        grad1 = dot(xt_ref[...], slope_s[...])
        grad2 = dot(gt_ref[...], act_s[...])
        if added:
            grad1 += init_ref[:, :ff].astype(f32)
            grad2 += init_ref[:, ff:].astype(f32)
        dw_ref[:, :ff] = grad1.astype(bf16)
        dw_ref[:, ff:] = grad2.astype(bf16)


def mlp_block(x, g, xt, gt, whole, block, bias, init=None, waits=(), tok_steps=4, row_steps=4):
    n, d = x.shape
    ff = whole.shape[2] // 2
    added = init is not None
    tok_rows, dim_rows = n // tok_steps, d // row_steps

    def tok(s):
        return (jnp.minimum(s, tok_steps - 1), 0)

    def row(s):
        return (jnp.maximum(s - tok_steps, 0), 0)

    in_specs = [
        SMEM_SPEC,
        pl.BlockSpec((tok_rows, d), tok),
        pl.BlockSpec((tok_rows, d), tok),
        pl.BlockSpec((dim_rows, n), row),
        pl.BlockSpec((dim_rows, n), row),
        ANY_SPEC,
        pl.BlockSpec((1, ff), lambda s: (0, 0)),
    ]
    operands = [block, x, g, xt, gt, whole, bias]
    if added:
        in_specs.append(pl.BlockSpec((dim_rows, 2 * ff), row))
        operands.append(init)
    return pl.pallas_call(
        lambda *refs: mlp_body(added, len(waits), tok_steps, *refs),
        grid=(tok_steps + row_steps,),
        in_specs=in_specs + [ANY_SPEC] * len(waits),
        out_specs=[
            pl.BlockSpec((tok_rows, d), tok),
            pl.BlockSpec((tok_rows, d), tok),
            pl.BlockSpec((1, ff), lambda s: (0, 0)),
            pl.BlockSpec((dim_rows, 2 * ff), row),
        ],
        out_shape=[
            jax.ShapeDtypeStruct((n, d), bf16),
            jax.ShapeDtypeStruct((n, d), bf16),
            jax.ShapeDtypeStruct((1, ff), f32),
            jax.ShapeDtypeStruct((d, 2 * ff), bf16),
        ],
        scratch_shapes=[
            pltpu.VMEM((d, ff), bf16),
            pltpu.VMEM((d, ff), bf16),
            pltpu.VMEM((n, ff), bf16),
            pltpu.VMEM((n, ff), bf16),
            pltpu.SemaphoreType.DMA((2, 8)),
        ],
        compiler_params=compiler_params(),
        cost_estimate=pl.CostEstimate(
            flops=12 * n * d * ff, bytes_accessed=30 << 20, transcendentals=n * ff
        ),
    )(*operands, *waits)


def attend_fwd_body(
    heads, lo_ref, hi_ref, block_ref, x_ref, whole_ref, b_ref, sc_ref, sr_ref, *refs
):
    qkv_ref, att_ref, lse_ref, part_ref, w_ref, qt_s, k_s, vt_s, ot_s, m_s, l_s, acc_s, sem = refs[-13:]
    copies = fetch(whole_ref, block_ref[0], 0, w_ref, sem)
    for copy in copies:
        copy.start()
    for copy in copies:
        copy.wait()
    n = x_ref.shape[0]
    e = heads * HD
    c = LOG2E / math.sqrt(HD)
    qkv = dot(x_ref[...], w_ref[:, : 3 * e]) + b_ref[...]
    qkv_ref[...] = qkv.astype(bf16)
    qt = qkv[:, :e].T
    vt = qkv[:, 2 * e :].T
    for h in range(heads):
        qt_s[h] = qt[h * HD : (h + 1) * HD].astype(bf16)
        vt_s[h] = vt[h * HD : (h + 1) * HD].astype(bf16)
        k_s[h] = qkv[:, e + h * HD : e + (h + 1) * HD].astype(bf16)

    @pl.loop(0, n // QT)
    def _(i):
        qi = pl.ds(pl.multiple_of(i * QT, QT), QT)
        m_s[...] = jnp.full(m_s.shape, masked_score, f32)
        l_s[...] = jnp.zeros(l_s.shape, f32)
        acc_s[...] = jnp.zeros(acc_s.shape, f32)
        seg_row = sr_ref[:1, qi]

        @pl.loop(lo_ref[i], hi_ref[i])
        def _(j):
            kj = pl.ds(pl.multiple_of(j * QT, QT), QT)
            same = sc_ref[kj, :1] == seg_row
            for h in range(heads):
                scores = jnp.where(same, dot(k_s[h, kj, :], qt_s[h, :, qi]), masked_score)
                old = m_s[h]
                top = jnp.maximum(old, jnp.max(scores, axis=0, keepdims=True))
                fade = jnp.exp2((old - top) * c)
                p = jnp.exp2((scores - top) * c)
                l_s[h] = l_s[h] * fade + jnp.sum(p, axis=0, keepdims=True)
                acc_s[h] = acc_s[h] * fade + dot(vt_s[h, :, kj], p.astype(bf16))
                m_s[h] = top

        for h in range(heads):
            total = l_s[h]
            ot_s[h * HD : (h + 1) * HD, qi] = acc_s[h] / total
            lse_ref[h : h + 1, qi] = m_s[h] * c + jnp.log(total) * LOG2E

    att = ot_s[...].T.astype(bf16)
    att_ref[...] = att
    part_ref[...] = dot(att, w_ref[:, 3 * e :], NT).astype(bf16)


def attend_fwd(x, whole, block, bias, lo, hi, seg_col, seg_row, waits=()):
    n, d = x.shape
    e = whole.shape[2] // 4
    heads = e // HD
    return pl.pallas_call(
        lambda *refs: attend_fwd_body(heads, *refs),
        in_specs=[SMEM_SPEC] * 3
        + [VMEM_SPEC, ANY_SPEC]
        + [VMEM_SPEC] * 3
        + [ANY_SPEC] * len(waits),
        out_specs=[VMEM_SPEC] * 4,
        out_shape=[
            jax.ShapeDtypeStruct((n, 3 * e), bf16),
            jax.ShapeDtypeStruct((n, e), bf16),
            jax.ShapeDtypeStruct((8, n), f32),
            jax.ShapeDtypeStruct((n, d), bf16),
        ],
        scratch_shapes=[
            pltpu.VMEM((d, 4 * e), bf16),
            pltpu.VMEM((heads, HD, n), bf16),
            pltpu.VMEM((heads, n, HD), bf16),
            pltpu.VMEM((heads, HD, n), bf16),
            pltpu.VMEM((e, n), f32),
            pltpu.VMEM((heads, 1, QT), f32),
            pltpu.VMEM((heads, 1, QT), f32),
            pltpu.VMEM((heads, HD, QT), f32),
            pltpu.SemaphoreType.DMA((8,)),
        ],
        compiler_params=compiler_params(),
        cost_estimate=pl.CostEstimate(
            flops=8 * n * d * e * 3, bytes_accessed=12 << 20, transcendentals=heads * n * n
        ),
    )(lo, hi, block, x, whole, bias, seg_col, seg_row, *waits)


def attend_bwd_body(final, waits, heads, *refs):
    (lo_ref, hi_ref, block_ref, place_ref, qkv_ref, att_ref, g_ref, gt_ref, xt_ref, whole_ref, lse_ref, sc_ref, sr_ref) = refs[:13]
    init_ref = refs[13] if final else None
    refs = refs[13 + final + waits :]
    if final:
        dx_ref, db_ref = refs[:2]
        outs, (stage, sem) = refs[2:4], refs[-2:]
        refs = refs[4:-2]
    else:
        dx_ref, db_ref, stage = refs[:3]
        refs = refs[3:]
    qt_s, q_s, k_s, kt_s, v_s, do_s, dot_s, delta_s, dqt_s, dk_s, dv_s, w_ref, w_sem = refs
    copies = fetch(whole_ref, block_ref[0], 0, w_ref, w_sem)
    for copy in copies:
        copy.start()
    for copy in copies:
        copy.wait()
    n = g_ref.shape[0]
    e = heads * HD
    c = LOG2E / math.sqrt(HD)
    scale = 1.0 / math.sqrt(HD)
    out_grad = dot(g_ref[...], w_ref[:, 3 * e :]).astype(bf16).astype(f32)
    out_grad_t = out_grad.T
    qkv = qkv_ref[...].astype(f32)
    qt = qkv[:, :e].T
    kt = qkv[:, e : 2 * e].T
    att = att_ref[...]
    products = out_grad_t * att.astype(f32).T
    for h in range(heads):
        s = slice(h * HD, (h + 1) * HD)
        qt_s[h] = qt[s].astype(bf16)
        kt_s[h] = kt[s].astype(bf16)
        dot_s[h] = out_grad_t[s].astype(bf16)
        delta_s[h] = jnp.sum(products[s], axis=0, keepdims=True)
        q_s[h] = qkv[:, h * HD : (h + 1) * HD].astype(bf16)
        k_s[h] = qkv[:, e + h * HD : e + (h + 1) * HD].astype(bf16)
        v_s[h] = qkv[:, 2 * e + h * HD : 2 * e + (h + 1) * HD].astype(bf16)
        do_s[h] = out_grad[:, s].astype(bf16)
    dqt_s[...] = jnp.zeros(dqt_s.shape, f32)
    dk_s[...] = jnp.zeros(dk_s.shape, f32)
    dv_s[...] = jnp.zeros(dv_s.shape, f32)

    @pl.loop(0, n // QT)
    def _(j):
        kj = pl.ds(pl.multiple_of(j * QT, QT), QT)
        seg_col = sc_ref[kj, :1]

        @pl.loop(lo_ref[j], hi_ref[j])
        def _(i):
            qi = pl.ds(pl.multiple_of(i * QT, QT), QT)
            same = seg_col == sr_ref[:1, qi]
            for h in range(heads):
                scores = dot(k_s[h, kj, :], qt_s[h, :, qi])
                p = jnp.where(same, jnp.exp2(scores * c - lse_ref[h : h + 1, qi]), 0.0)
                p_grad = dot(v_s[h, kj, :], dot_s[h, :, qi])
                s_grad = (p * (p_grad - delta_s[h, :, qi])).astype(bf16)
                dv_s[h, kj, :] += dot(p.astype(bf16), do_s[h, qi, :])
                dk_s[h, kj, :] += dot(s_grad, q_s[h, qi, :])
                dqt_s[h, :, qi] += dot(kt_s[h, :, kj], s_grad)

    dq = jnp.concatenate([dqt_s[h] for h in range(heads)], axis=0).T * scale
    dk = [dk_s[h] * scale for h in range(heads)]
    dv = [dv_s[h] for h in range(heads)]
    grads = jnp.concatenate([dq] + dk + dv, axis=1).astype(bf16)
    db_ref[...] = jnp.sum(grads.astype(f32), axis=0, keepdims=True)
    dx_ref[...] = dot(grads, w_ref[:, : 3 * e], NT).astype(bf16)
    dw = jnp.concatenate([dot(xt_ref[...], grads), dot(gt_ref[...], att)], axis=1)
    if not final:
        stage[...] = dw.astype(bf16)
    else:
        stage[...] = (dw + init_ref[...].astype(f32)).astype(bf16)
        send_pieces(stage, place_ref, 0, 8, outs, sem)
        wait_pieces(stage, 8, outs, sem)


def attend_bwd(
    qkv, att, g, gt, xt, whole, block, lse, lo, hi, seg_col, seg_row, place, init=None, waits=()
):
    n, d = g.shape
    e = whole.shape[2] // 4
    heads = e // HD
    final = init is not None
    operands = [lo, hi, block, place, qkv, att, g, gt, xt, whole, lse, seg_col, seg_row]
    in_specs = [SMEM_SPEC] * 4 + [VMEM_SPEC] * 5 + [ANY_SPEC] + [VMEM_SPEC] * 3
    out_shape = [jax.ShapeDtypeStruct((n, d), bf16), jax.ShapeDtypeStruct((1, 3 * e), f32)]
    out_specs = [VMEM_SPEC, VMEM_SPEC]
    tall, wide = (heads, n, HD), (heads, HD, n)
    scratch = [pltpu.VMEM(s, bf16) for s in (wide, tall, tall, wide, tall, tall, wide)]
    scratch += [pltpu.VMEM((heads, 1, n), f32)] + [pltpu.VMEM(s, f32) for s in (wide, tall, tall)]
    scratch += [pltpu.VMEM((d, 4 * e), bf16), pltpu.SemaphoreType.DMA((8,))]
    if final:
        operands.append(init)
        in_specs.append(VMEM_SPEC)
        out_shape += [jax.ShapeDtypeStruct((4, ROWS, 4 * e), bf16)] * 2
        out_specs += [ANY_SPEC] * 2
        scratch += [pltpu.VMEM((d, 4 * e), bf16), pltpu.SemaphoreType.DMA((8,))]
    else:
        out_shape.append(jax.ShapeDtypeStruct((d, 4 * e), bf16))
        out_specs.append(VMEM_SPEC)
    in_specs += [ANY_SPEC] * len(waits)
    operands += waits
    return pl.pallas_call(
        lambda *refs: attend_bwd_body(final, len(waits), heads, *refs),
        in_specs=in_specs,
        out_specs=out_specs,
        out_shape=out_shape,
        scratch_shapes=scratch,
        compiler_params=compiler_params(),
        cost_estimate=pl.CostEstimate(
            flops=16 * n * d * e * 3, bytes_accessed=20 << 20, transcendentals=heads * n * n
        ),
    )(*operands)


def token_rows(mod_ref, block, sc_ref):
    d = mod_ref.shape[1] // 6
    seg = sc_ref[:, :1]
    rows = mod_ref[:, block * d : (block + 1) * d]
    value = jnp.where(seg == 0, rows[0:1], rows[1:2])
    value = jnp.where(seg == 2, rows[2:3], value)
    return jnp.where(seg == 3, rows[3:4], value)


def normalize(values):
    centred = values - jnp.mean(values, axis=-1, keepdims=True)
    inverse = lax.rsqrt(jnp.mean(centred * centred, axis=-1, keepdims=True) + epsilon)
    return centred * inverse, inverse


def norm_back(normed, inverse, grad):
    mean = jnp.mean(grad, axis=-1, keepdims=True)
    along = jnp.mean(grad * normed, axis=-1, keepdims=True)
    return inverse * (grad - mean - normed * along)


def add_images(acc_ref, first_ref, last_ref, sc_ref, columns):
    step = pl.program_id(0)
    seg = sc_ref[:, :1]

    @pl.when(step == 0)
    def _():
        acc_ref[...] = jnp.zeros(acc_ref.shape, f32)

    @pl.loop(first_ref[step], last_ref[step] + 1)
    def _(image):
        mine = seg == image
        for i, values in enumerate(columns):
            d = values.shape[1]
            part = jnp.sum(jnp.where(mine, values, 0.0), axis=0, keepdims=True)
            acc_ref[pl.ds(image, 1), i * d : (i + 1) * d] += part


def add_rows(acc_ref, values):
    part = jnp.sum(values, axis=0, keepdims=True)

    @pl.when(pl.program_id(0) == 0)
    def _():
        acc_ref[...] = part

    @pl.when(pl.program_id(0) > 0)
    def _():
        acc_ref[...] += part


def enter_body(x_ref, g_ref, mod_ref, sc_ref, a_ref, at_ref, bg_ref, bgt_ref, sum_ref):
    normed, _ = normalize(x_ref[...].astype(f32))
    a = normed * (1.0 + token_rows(mod_ref, 1, sc_ref)) + token_rows(mod_ref, 0, sc_ref)
    a_ref[...] = a.astype(bf16)
    at_ref[...] = a.T.astype(bf16)
    bg = token_rows(mod_ref, 5, sc_ref) * g_ref[...].astype(f32)
    bg_ref[...] = bg.astype(bf16)
    bgt_ref[...] = bg.T.astype(bf16)
    add_rows(sum_ref, bg)


def middle_body(x_ref, p0, p1, p2, p3, mod_ref, sc_ref, ob_ref, hid_ref, br_ref, m_ref, mt_ref):
    branch = p0[...].astype(f32) + p1[...].astype(f32) + p2[...].astype(f32) + p3[...].astype(f32)
    branch = branch + ob_ref[...]
    br_ref[...] = branch
    hidden = x_ref[...].astype(f32) + token_rows(mod_ref, 2, sc_ref) * branch
    hid_ref[...] = hidden
    normed, _ = normalize(hidden)
    m = normed * (1.0 + token_rows(mod_ref, 4, sc_ref)) + token_rows(mod_ref, 3, sc_ref)
    m_ref[...] = m.astype(bf16)
    mt_ref[...] = m.T.astype(bf16)


def turn_body(
    first_ref, last_ref, hid_ref, br_ref, g_ref, b0, b1, b2, b3, d0, d1, d2, d3, mod_ref, sc_ref, fb_ref,
    out_ref, hg_ref, bg_ref, bgt_ref, sum_ref, img_ref,
):
    hidden, g = hid_ref[...], g_ref[...].astype(f32)
    branch = b0[...].astype(f32) + b1[...].astype(f32) + b2[...].astype(f32) + b3[...].astype(f32)
    branch = branch + fb_ref[...]
    out_ref[...] = (hidden + token_rows(mod_ref, 5, sc_ref) * branch).astype(bf16)
    m_grad = d0[...].astype(f32) + d1[...].astype(f32) + d2[...].astype(f32) + d3[...].astype(f32)
    normed, inverse = normalize(hidden)
    hidden_grad = g + norm_back(normed, inverse, m_grad * (1.0 + token_rows(mod_ref, 4, sc_ref)))
    hg_ref[...] = hidden_grad
    bg = token_rows(mod_ref, 2, sc_ref) * hidden_grad
    bg_ref[...] = bg.astype(bf16)
    bgt_ref[...] = bg.T.astype(bf16)
    add_rows(sum_ref, bg)
    add_images(
        img_ref, first_ref, last_ref, sc_ref,
        (hidden_grad * br_ref[...], m_grad, m_grad * normed, g * branch),
    )


def leave_body(first_ref, last_ref, x_ref, hg_ref, d0, d1, d2, d3, mod_ref, sc_ref, out_ref, img_ref):
    a_grad = d0[...].astype(f32) + d1[...].astype(f32) + d2[...].astype(f32) + d3[...].astype(f32)
    normed, inverse = normalize(x_ref[...].astype(f32))
    back = norm_back(normed, inverse, a_grad * (1.0 + token_rows(mod_ref, 1, sc_ref)))
    out_ref[...] = (hg_ref[...] + back).astype(bf16)
    add_images(img_ref, first_ref, last_ref, sc_ref, (a_grad, a_grad * normed))


def by_rows(body_fn, scalars, operands, outs, waits=(), carried=()):
    def spec(kind, shape):
        if kind == "t":
            return pl.BlockSpec((ET, shape[1]), lambda s: (s, 0))
        if kind == "T":
            return pl.BlockSpec((shape[0], ET), lambda s: (0, s))
        return pl.BlockSpec(shape, lambda s: (0, 0))

    n = operands[0][1].shape[0]
    own_in, own_out = len(scalars) + len(operands), len(outs)
    idle = len(waits) + len(carried)

    def body(*refs):
        body_fn(*refs[:own_in], *refs[own_in + idle : own_in + idle + own_out])

    return pl.pallas_call(
        body,
        grid=(n // ET,),
        in_specs=[SMEM_SPEC] * len(scalars)
        + [spec(k, v.shape) for k, v in operands]
        + [ANY_SPEC] * idle,
        out_specs=[spec(k, s) for k, s, _ in outs] + [ANY_SPEC] * len(carried),
        out_shape=[jax.ShapeDtypeStruct(s, t) for _, s, t in outs]
        + [jax.ShapeDtypeStruct(v.shape, v.dtype) for v in carried],
        input_output_aliases={
            own_in + len(waits) + i: own_out + i for i in range(len(carried))
        },
        compiler_params=compiler_params(),
        cost_estimate=pl.CostEstimate(
            flops=100 * n * 1152, bytes_accessed=24 << 20, transcendentals=n
        ),
    )(*scalars, *[v for _, v in operands], *waits, *carried)


def trade_rows(values, core):
    own = lax.dynamic_index_in_dim(values, core, 0, keepdims=False)
    got = across(lax.dynamic_index_in_dim(values, 1 - core, 0, keepdims=False), CORE)
    first = core == 0
    return jnp.concatenate([jnp.where(first, own, got), jnp.where(first, got, own)])


def trade_back(row, core):
    half = row.shape[0] // 2
    own = lax.dynamic_slice_in_dim(row, core * half, half, 0)
    got = across(lax.dynamic_slice_in_dim(row, (1 - core) * half, half, 0), CORE)
    first = core == 0
    return jnp.stack([jnp.where(first, own, got), jnp.where(first, got, own)])


def add_pieces(*terms):
    return sum(t.astype(f32) for t in terms)


class Scatter:
    def __init__(self, low, high):
        self.low, self.got = low, swap(high, 1, 0)

    def turn(self):
        sums = [add_pieces(self.low[i], self.got[i]) for i in range(4)]
        self.low = sums[0]
        self.got = [swap(sums[i].astype(bf16), 2 * i, 0) for i in range(1, 4)]

    def total(self):
        return add_pieces(self.low, *self.got)


def gather_all(values, dp_rank, tp_rank):
    order = dp_rank * 4 + tp_rank + jnp.zeros((1,), jnp.int32)
    for dp_mask, tp_mask in ((1, 0), (2, 0), (6, 0), (0, CHIP), (0, CORE)):
        values = jnp.concatenate([values, swap(values, dp_mask, tp_mask)])
        order = jnp.concatenate([order, order ^ (dp_mask * 4 + tp_mask)])
    return values, order


def row_body(
    block_input,
    segment_ids,
    conditioning,
    w_qkv,
    qv_bias,
    w_out,
    out_bias,
    w_fc1,
    fc1_bias,
    w_fc2,
    fc2_bias,
    w_ada,
    ada_bias,
    cotangent,
):
    dp_rank, tp_rank = lax.axis_index("dp"), lax.axis_index("tp")
    core, chip = tp_rank & 1, tp_rank >> 1
    d = block_input.shape[2]
    e, ff, mod_dev = w_qkv.shape[2], w_fc1.shape[1], w_ada.shape[1]
    flips = jnp.arange(8, dtype=jnp.int32) ^ dp_rank
    place = (flips & 1) * 4 + (flips >> 1)
    blocks = [(tp_rank ^ k).reshape(1) for k in range(4)]
    att_shard = jnp.concatenate([w_qkv[0], w_qkv[1], w_qkv[2], w_out.T], axis=1)
    mlp_shard = jnp.concatenate([w_fc1, w_fc2.T], axis=1)
    att_w = lax.all_gather(att_shard, AXES)
    mlp_w = lax.all_gather(mlp_shard, AXES)
    x = trade_rows(block_input, core)
    g = trade_rows(cotangent, core)
    seg = lax.dynamic_slice(segment_ids, (core, chip * PACK), (1, PACK))[0]
    seg_col = jnp.broadcast_to(seg[:, None], (PACK, 128))
    seg_row = jnp.broadcast_to(seg[None, :], (8, PACK))
    tiles = seg.reshape(-1, QT)
    lo = jnp.sum((tiles[None, :, -1] < tiles[:, None, 0]).astype(jnp.int32), axis=1)
    hi = jnp.sum((tiles[None, :, 0] <= tiles[:, None, -1]).astype(jnp.int32), axis=1)
    small = seg.reshape(-1, ET)
    first, last = small[:, 0], small[:, -1]
    lifted = smooth_gate(conditioning.astype(f32)).astype(bf16).reshape(-1, 8, w_ada.shape[0])
    lifted = lax.all_to_all(lifted.transpose(1, 0, 2), "dp", 0, 0)
    lifted = lifted.reshape(8, 2, 2, IMG_ROW, -1).transpose(0, 2, 1, 3, 4).reshape(32 * IMG_ROW, -1)
    mod_part = dot(lifted, w_ada).reshape(32, IMG_ROW, mod_dev)
    mod_part = lax.all_to_all(mod_part, AXES, 0, 0).reshape(8, 4, IMG_ROW, mod_dev)
    modulation = jnp.sum(mod_part, axis=0).transpose(1, 0, 2).reshape(IMG_ROW, -1)
    modulation = modulation + ada_bias.astype(f32)
    row_f, row_b = ((PACK, d), f32), ((PACK, d), bf16)
    turned = ((d, PACK), bf16)
    a, a_t, bg2, bg2_t, fc2_sum = by_rows(
        enter_body,
        (),
        [("t", x), ("t", g), ("w", modulation), ("t", seg_col)],
        [("t", *row_b), ("T", *turned), ("t", *row_b), ("T", *turned), ("w", (1, d), f32)],
    )
    qkv_bias = jnp.stack([qv_bias[0], jnp.zeros_like(qv_bias[0]), qv_bias[1]]).astype(f32)
    kept = {}

    def forward(k, waits):
        bias = lax.dynamic_slice_in_dim(qkv_bias, (tp_rank ^ k) * e, e, 1).reshape(1, 3 * e)
        kept[k] = attend_fwd(a, att_w, blocks[k], bias, lo, hi, seg_col, seg_row, waits)
        return (kept[k][2],)

    after = ()
    for k in range(4):
        after = forward(k, after)
    hidden, branch1, m, m_t = by_rows(
        middle_body,
        (),
        [("t", x)]
        + [("t", kept[k][3]) for k in range(4)]
        + [("w", modulation), ("t", seg_col), ("w", out_bias.astype(f32)[None])],
        [("t", *row_f), ("t", *row_f), ("t", *row_b), ("T", *turned)],
    )
    done = {}
    fc1_f = fc1_bias.astype(f32)[None]

    def feed_forward(k, init, waits):
        bias = lax.dynamic_slice_in_dim(fc1_f, (tp_rank ^ k) * ff, ff, 1)
        done[k] = mlp_block(m, bg2, m_t, bg2_t, mlp_w, blocks[k], bias, init, waits)
        return (done[k][2],)

    after = feed_forward(1, None, ())
    init = across(done[1][3], CORE)
    after = feed_forward(3, None, after)
    after = feed_forward(0, init, after)
    init = across(done[3][3], CORE)
    mlp_sum = {0: lax.psum_scatter(done[0][3], "dp", scatter_dimension=0, tiled=True)}
    after = feed_forward(2, init, after)
    mlp_sum[2] = lax.psum_scatter(done[2][3], "dp", scatter_dimension=0, tiled=True)
    block_output, hidden_grad, bg1, bg1_t, out_sum, img_late = by_rows(
        turn_body,
        (first, last),
        [("t", hidden), ("t", branch1), ("t", g)]
        + [("t", done[k][0]) for k in range(4)]
        + [("t", done[k][1]) for k in range(4)]
        + [("w", modulation), ("t", seg_col), ("w", fc2_bias.astype(f32)[None])],
        [("t", *row_b), ("t", *row_f), ("t", *row_b), ("T", *turned), ("w", (1, d), f32), ("w", (IMG_ROW, 4 * d), f32)],
        waits=after,
    )
    fc1_sum = jnp.zeros((1, 4 * ff), f32)
    for k in range(4):
        fc1_sum = lax.dynamic_update_slice_in_dim(fc1_sum, done[k][2], (tp_rank ^ k) * ff, 1)
    late = jnp.concatenate([jnp.zeros((IMG_ROW, 2 * d), f32), img_late], axis=1)
    late = late.reshape(IMG_ROW, 4, mod_dev).transpose(1, 0, 2).reshape(4, IMG_ROW * mod_dev)
    sums = jnp.concatenate([jnp.sum(img_late, axis=0, keepdims=True), fc1_sum, fc2_sum, out_sum], axis=1)
    late = jnp.concatenate([late, jnp.broadcast_to(sums, (4, sums.shape[1]))], axis=1)
    late = lax.all_to_all(jnp.concatenate([late] * 8), AXES, 0, 0, tiled=True)
    back = {}

    def backward(k, init, waits):
        qkv, att, lse, _ = kept[k]
        back[k] = attend_bwd(
            qkv, att, bg1, bg1_t, a_t, att_w, blocks[k], lse, lo, hi, seg_col, seg_row, place, init, waits
        )
        return (back[k][1],)

    block_output = trade_back(block_output, core)
    after = backward(1, None, ())
    init = across(back[1][2], CORE)
    (block_output,) = tie([block_output], after)
    after = backward(3, None, after + (block_output,))
    (late,) = tie([late], after)
    after = backward(0, init, after + (late,))
    init = across(back[3][2], CORE)
    near = Scatter(*back[0][2:])
    after = backward(2, init, after + (mlp_sum[0],))
    (near.got,) = tie([near.got], after)
    near.turn()
    far = Scatter(*back[2][2:])
    input_grad, img_early = by_rows(
        leave_body,
        (first, last),
        [("t", x), ("t", hidden_grad)]
        + [("t", back[k][0]) for k in range(4)]
        + [("w", modulation), ("t", seg_col)],
        [("t", *row_b), ("w", (IMG_ROW, 2 * d), f32)],
        waits=(near.low,),
    )
    mlp_total = mlp_sum[0].astype(f32) + across(mlp_sum[2], CHIP).astype(f32)
    far.got, *near.got = tie([far.got] + near.got, (img_early,))
    far.turn()
    att_total = near.total() + across(far.total().astype(bf16), CHIP).astype(f32)
    qv_sum = jnp.zeros((2, 4 * e), f32)
    for k in range(4):
        grads = back[k][1].reshape(3, e)
        qv_sum = lax.dynamic_update_slice_in_dim(
            qv_sum, jnp.stack([grads[0], grads[2]]), (tp_rank ^ k) * e, 1
        )
    all_b = jnp.concatenate([img_early.reshape(1, -1), qv_sum.reshape(1, -1)], axis=1)
    all_b, order = gather_all(all_b, dp_rank, tp_rank)
    early = 2 * d * IMG_ROW
    own = IMG_ROW * mod_dev
    late_bias, fc1_total, fc2_total, out_total = jnp.split(
        jnp.sum(late[:, own:], axis=0), [4 * d, 4 * d + 4 * ff, 5 * d + 4 * ff]
    )
    qv_total = jnp.sum(all_b[:, early:], axis=0).reshape(2, -1)
    all_b = all_b[:, :early].reshape(32 * IMG_ROW, 2 * d)
    ada_total = jnp.concatenate([jnp.sum(all_b, axis=0), late_bias])
    grad_b = lax.dynamic_slice_in_dim(
        jnp.pad(all_b, ((0, 0), (0, 4 * d))), tp_rank * mod_dev, mod_dev, 1
    )
    lifted = lifted.astype(f32)
    lifted_b = jnp.take(lifted.reshape(32, -1), order, axis=0).reshape(lifted.shape)
    ada_grad = jnp.zeros((), f32)
    for rows, grad in ((lifted, late[:, :own].reshape(32 * IMG_ROW, mod_dev)), (lifted_b, grad_b)):
        ada_grad += lax.dot_general(rows, grad, (((0,), (0,)), ((), ())), precision=highest)
    return (
        block_output,
        trade_back(input_grad, core),
        jnp.stack([att_total[:, i * e : (i + 1) * e] for i in range(3)]),
        qv_total,
        att_total[:, 3 * e :].T,
        out_total,
        mlp_total[:, :ff],
        fc1_total,
        mlp_total[:, ff:].T,
        fc2_total,
        ada_grad,
        ada_total,
    )


def body(*arrays):
    block_input, w_qkv, w_fc1 = arrays[0], arrays[3], arrays[7]
    micro, tokens, width = block_input.shape
    heads_dev, rows = w_qkv.shape[2], w_fc1.shape[0]
    if (
        lax.axis_size("dp") == 8
        and lax.axis_size("tp") == 4
        and micro == 2
        and micro * tokens == PACK
        and rows == ROWS
        and rows * 8 == width
        and heads_dev * 4 == width
        and w_fc1.shape[1] % 384 == 0
    ):
        return row_body(*arrays)
    return general_body(*arrays)


def solution(mesh):
    placed = (
        P(None, ("dp", "tp"), None),
        P(None, "dp"),
        P(None, "dp", None),
        P(None, "dp", "tp"),
        P(),
        P("tp", "dp"),
        P(),
        P("dp", "tp"),
        P(),
        P("tp", "dp"),
        P(),
        P("dp", "tp"),
        P(),
        P(None, ("dp", "tp"), None),
    )
    return jax.shard_map(
        body,
        mesh=mesh,
        in_specs=placed,
        out_specs=(
            P(None, ("dp", "tp"), None),
            P(None, ("dp", "tp"), None),
            P(None, "dp", "tp"),
            P(),
            P("tp", "dp"),
            P(),
            P("dp", "tp"),
            P(),
            P("tp", "dp"),
            P(),
            P("dp", "tp"),
            P(),
        ),
        check_vma=False,
    )
```

```python
import math

import jax
import jax.numpy as jnp
from jax import lax
from jax.experimental import pallas as pl
from jax.experimental.pallas import tpu as pltpu
from jax.sharding import PartitionSpec as P

HD = 72
PACK = 1024
IMG_ROW = 4


highest = lax.Precision.HIGHEST
epsilon = 1e-06
masked_score = -1e30


def layer_norm(values):
    centred = values - jnp.mean(values, axis=-1, keepdims=True)
    return centred * lax.rsqrt(jnp.mean(centred * centred, axis=-1, keepdims=True) + epsilon)


def gelu_tanh(values):
    return (
        0.5
        * values
        * (1.0 + jnp.tanh(0.7978845608028654 * (values + 0.044715 * values * values * values)))
    )


def smooth_gate(values):
    return values / (1.0 + jnp.exp(-values))


def to_blocks(values, local_heads):
    shaped = values.reshape(values.shape[0] // PACK, PACK, local_heads, HD)
    return shaped.transpose(0, 2, 1, 3).reshape(-1, PACK, HD)


def from_blocks(blocks, local_heads):
    shaped = blocks.reshape(-1, local_heads, PACK, HD).transpose(0, 2, 1, 3)
    return shaped.reshape(-1, local_heads * HD)


def block_segments(segment_group, local_heads):
    shaped = segment_group.reshape(-1, 1, PACK)
    return jnp.broadcast_to(shaped, (shaped.shape[0], local_heads, PACK)).reshape(-1, PACK)


def project_heads(activations, full_qkv, bias_pair):
    projected = jnp.einsum("gd,cde->cge", activations, full_qkv, preferred_element_type=jnp.float32)
    bias_rows = jnp.stack([bias_pair[0], jnp.zeros_like(bias_pair[0]), bias_pair[1]])
    return (projected + bias_rows[:, None, :]).astype(jnp.bfloat16)


def masked_scores(query_rows, key_rows, segment_row):
    raw_scores = lax.dot_general(
        query_rows, key_rows, (((1,), (1,)), ((), ())), preferred_element_type=jnp.float32
    ) / math.sqrt(HD)
    same_image = segment_row[:, None] == segment_row[None, :]
    return (same_image, jnp.where(same_image, raw_scores, masked_score))


def attend_forward(block_items):
    query_rows, key_rows, value_rows, segment_row = block_items
    same_image, scores = masked_scores(query_rows, key_rows, segment_row)
    row_max = jnp.max(scores, axis=-1, keepdims=True)
    exponents = jnp.exp(scores - row_max)
    row_sums = jnp.sum(exponents, axis=-1, keepdims=True)
    probs_low = (exponents / row_sums).astype(jnp.bfloat16)
    attended = jnp.dot(probs_low, value_rows, preferred_element_type=jnp.float32).astype(
        jnp.bfloat16
    )
    return (attended, (row_max + jnp.log(row_sums))[:, 0])


def attend_backward(block_items):
    query_rows, key_rows, value_rows, segment_row, log_total, attended_grad = block_items
    same_image, scores = masked_scores(query_rows, key_rows, segment_row)
    attn_probs = jnp.where(same_image, jnp.exp(scores - log_total[:, None]), 0.0)
    value_grad = lax.dot_general(
        attn_probs.astype(jnp.bfloat16),
        attended_grad,
        (((0,), (0,)), ((), ())),
        preferred_element_type=jnp.float32,
    )
    probs_grad = lax.dot_general(
        attended_grad, value_rows, (((1,), (1,)), ((), ())), preferred_element_type=jnp.float32
    )
    centred = probs_grad - jnp.sum(attn_probs * probs_grad, axis=-1, keepdims=True)
    scores_grad = (attn_probs * centred).astype(jnp.bfloat16)
    query_grad = jnp.dot(scores_grad, key_rows, preferred_element_type=jnp.float32) / math.sqrt(HD)
    key_grad = lax.dot_general(
        scores_grad, query_rows, (((0,), (0,)), ((), ())), preferred_element_type=jnp.float32
    ) / math.sqrt(HD)
    return (
        query_grad.astype(jnp.bfloat16),
        key_grad.astype(jnp.bfloat16),
        value_grad.astype(jnp.bfloat16),
    )


def general_body(
    block_input,
    segment_ids,
    conditioning,
    w_qkv,
    qv_bias,
    w_out,
    out_bias,
    w_fc1,
    fc1_bias,
    w_fc2,
    fc2_bias,
    w_ada,
    ada_bias,
    cotangent,
):
    micro_count, tok_dev, model_width = block_input.shape
    tp_size = lax.axis_size("tp")
    tp_rank = lax.axis_index("tp")
    heads_dev = w_qkv.shape[2]
    hidden_dev = w_fc1.shape[1]
    mod_dev = w_ada.shape[1]
    cond_width = conditioning.shape[2]
    images = conditioning.shape[1]
    local_heads = heads_dev // HD
    qv_local = lax.dynamic_slice_in_dim(
        qv_bias.astype(jnp.float32), tp_rank * heads_dev, heads_dev, 1
    )
    fc1_local = lax.dynamic_slice_in_dim(
        fc1_bias.astype(jnp.float32), tp_rank * hidden_dev, hidden_dev, 0
    )
    ada_local = lax.dynamic_slice_in_dim(
        ada_bias.astype(jnp.float32), tp_rank * mod_dev, mod_dev, 0
    )
    out_bias_f = out_bias.astype(jnp.float32)
    fc2_bias_f = fc2_bias.astype(jnp.float32)
    positions = tp_rank * tok_dev + jnp.arange(tok_dev, dtype=jnp.int32)
    grad_qkv = jnp.zeros((3, model_width, heads_dev), jnp.float32)
    grad_out_w = jnp.zeros((heads_dev, model_width), jnp.float32)
    grad_fc1 = jnp.zeros((model_width, hidden_dev), jnp.float32)
    grad_fc2 = jnp.zeros((hidden_dev, model_width), jnp.float32)
    grad_ada = jnp.zeros((cond_width, mod_dev), jnp.float32)
    sum_qv = jnp.zeros((2, heads_dev), jnp.float32)
    sum_out_bias = jnp.zeros((model_width,), jnp.float32)
    sum_fc1 = jnp.zeros((hidden_dev,), jnp.float32)
    sum_fc2 = jnp.zeros((model_width,), jnp.float32)
    sum_ada = jnp.zeros((mod_dev,), jnp.float32)
    outputs = []
    input_grads = []
    for micro_step in range(micro_count):
        full_qkv, full_out, full_fc1, full_fc2, full_ada = (
            lax.all_gather(w_qkv, "dp", axis=1, tiled=True),
            lax.all_gather(w_out, "dp", axis=1, tiled=True),
            lax.all_gather(w_fc1, "dp", axis=0, tiled=True),
            lax.all_gather(w_fc2, "dp", axis=1, tiled=True),
            lax.all_gather(w_ada, "dp", axis=0, tiled=True),
        )
        lifted = smooth_gate(conditioning[micro_step].astype(jnp.float32)).astype(jnp.bfloat16)
        mod_part = jnp.dot(lifted, full_ada, preferred_element_type=jnp.float32) + ada_local
        modulation = lax.all_gather(mod_part, "tp", axis=1, tiled=True)
        segment_group = segment_ids[micro_step]
        segment_local = lax.dynamic_slice_in_dim(segment_group, tp_rank * tok_dev, tok_dev, 0)
        image_index = positions // PACK * IMG_ROW + segment_local
        onehot = (image_index[:, None] == jnp.arange(images, dtype=jnp.int32)[None, :]).astype(
            jnp.float32
        )
        token_mod = jnp.dot(onehot, modulation, precision=highest)
        shift_one, scale_one, gate_one, shift_two, scale_two, gate_two = jnp.split(
            token_mod, 6, axis=1
        )
        inputs = block_input[micro_step].astype(jnp.float32)
        normed_one = layer_norm(inputs)
        attn_in = (normed_one * (1.0 + scale_one) + shift_one).astype(jnp.bfloat16)
        attn_full = lax.all_gather(attn_in, "tp", axis=0, tiled=True)
        projected = project_heads(attn_full, full_qkv, qv_local)
        segment_blocks = block_segments(segment_group, local_heads)
        attended_blocks, log_totals = lax.map(
            attend_forward,
            (
                to_blocks(projected[0], local_heads),
                to_blocks(projected[1], local_heads),
                to_blocks(projected[2], local_heads),
                segment_blocks,
            ),
        )
        attended = from_blocks(attended_blocks, local_heads)
        branch_one = lax.psum_scatter(
            jnp.dot(attended, full_out, preferred_element_type=jnp.float32).astype(jnp.bfloat16),
            "tp",
            scatter_dimension=0,
            tiled=True,
        ).astype(jnp.float32)
        hidden = inputs + gate_one * (branch_one + out_bias_f)
        normed_two = layer_norm(hidden)
        mlp_in = (normed_two * (1.0 + scale_two) + shift_two).astype(jnp.bfloat16)
        mlp_full = lax.all_gather(mlp_in, "tp", axis=0, tiled=True)
        pre_act = jnp.dot(mlp_full, full_fc1, preferred_element_type=jnp.float32) + fc1_local
        activated = gelu_tanh(pre_act).astype(jnp.bfloat16)
        branch_two = lax.psum_scatter(
            jnp.dot(activated, full_fc2, preferred_element_type=jnp.float32).astype(jnp.bfloat16),
            "tp",
            scatter_dimension=0,
            tiled=True,
        ).astype(jnp.float32)
        outputs.append((hidden + gate_two * (branch_two + fc2_bias_f)).astype(jnp.bfloat16))
        grad_y = cotangent[micro_step].astype(jnp.float32)
        sum_fc2 = sum_fc2 + jnp.sum(gate_two * grad_y, axis=0)
        grad_gate_two = grad_y * (branch_two + fc2_bias_f)
        grad_branch_two = (gate_two * grad_y).astype(jnp.bfloat16)
        grad_two_full = lax.all_gather(grad_branch_two, "tp", axis=0, tiled=True)
        attn_back, mlp_back = (
            lax.all_gather(attn_in, "tp", axis=0, tiled=True),
            lax.all_gather(mlp_in, "tp", axis=0, tiled=True),
        )
        proj_back = project_heads(attn_back, full_qkv, qv_local)
        pre_back = jnp.dot(mlp_back, full_fc1, preferred_element_type=jnp.float32) + fc1_local
        act_back, gelu_pull = jax.vjp(gelu_tanh, pre_back)
        grad_fc2 = grad_fc2 + lax.dot_general(
            act_back.astype(jnp.bfloat16),
            grad_two_full,
            (((0,), (0,)), ((), ())),
            preferred_element_type=jnp.float32,
        )
        grad_act = lax.dot_general(
            grad_two_full, full_fc2, (((1,), (1,)), ((), ())), preferred_element_type=jnp.float32
        )
        grad_pre = gelu_pull(grad_act)[0].astype(jnp.bfloat16)
        sum_fc1 = sum_fc1 + jnp.sum(grad_pre.astype(jnp.float32), axis=0)
        grad_fc1 = grad_fc1 + lax.dot_general(
            mlp_back, grad_pre, (((0,), (0,)), ((), ())), preferred_element_type=jnp.float32
        )
        grad_mlp_in = lax.psum_scatter(
            lax.dot_general(
                grad_pre, full_fc1, (((1,), (1,)), ((), ())), preferred_element_type=jnp.float32
            ).astype(jnp.bfloat16),
            "tp",
            scatter_dimension=0,
            tiled=True,
        ).astype(jnp.float32)
        norm_two_pull = jax.vjp(layer_norm, hidden)[1]
        grad_hidden = grad_y + norm_two_pull(grad_mlp_in * (1.0 + scale_two))[0]
        sum_out_bias = sum_out_bias + jnp.sum(gate_one * grad_hidden, axis=0)
        grad_gate_one = grad_hidden * (branch_one + out_bias_f)
        grad_branch_one = (gate_one * grad_hidden).astype(jnp.bfloat16)
        grad_one_full = lax.all_gather(grad_branch_one, "tp", axis=0, tiled=True)
        grad_out_w = grad_out_w + lax.dot_general(
            attended, grad_one_full, (((0,), (0,)), ((), ())), preferred_element_type=jnp.float32
        )
        grad_attended = lax.dot_general(
            grad_one_full, full_out, (((1,), (1,)), ((), ())), preferred_element_type=jnp.float32
        ).astype(jnp.bfloat16)
        query_blocks, key_blocks, value_blocks = lax.map(
            attend_backward,
            (
                to_blocks(proj_back[0], local_heads),
                to_blocks(proj_back[1], local_heads),
                to_blocks(proj_back[2], local_heads),
                segment_blocks,
                log_totals,
                to_blocks(grad_attended, local_heads),
            ),
        )
        grad_proj = jnp.stack(
            [
                from_blocks(query_blocks, local_heads),
                from_blocks(key_blocks, local_heads),
                from_blocks(value_blocks, local_heads),
            ]
        )
        sum_qv = sum_qv + jnp.stack(
            [
                jnp.sum(grad_proj[0].astype(jnp.float32), axis=0),
                jnp.sum(grad_proj[2].astype(jnp.float32), axis=0),
            ]
        )
        grad_qkv = grad_qkv + jnp.einsum(
            "gd,cge->cde", attn_back, grad_proj, preferred_element_type=jnp.float32
        )
        grad_attn_in = lax.psum_scatter(
            jnp.einsum(
                "cge,cde->gd", grad_proj, full_qkv, preferred_element_type=jnp.float32
            ).astype(jnp.bfloat16),
            "tp",
            scatter_dimension=0,
            tiled=True,
        ).astype(jnp.float32)
        norm_one_pull = jax.vjp(layer_norm, inputs)[1]
        input_grads.append(
            (grad_hidden + norm_one_pull(grad_attn_in * (1.0 + scale_one))[0]).astype(jnp.bfloat16)
        )
        grad_token_mod = jnp.concatenate(
            [
                grad_attn_in,
                grad_attn_in * normed_one,
                grad_gate_one,
                grad_mlp_in,
                grad_mlp_in * normed_two,
                grad_gate_two,
            ],
            axis=1,
        )
        mod_grad_part = lax.dot_general(
            onehot, grad_token_mod, (((0,), (0,)), ((), ())), precision=highest
        )
        grad_mod = lax.psum_scatter(
            mod_grad_part.astype(jnp.bfloat16), "tp", scatter_dimension=1, tiled=True
        ).astype(jnp.float32)
        sum_ada = sum_ada + jnp.sum(grad_mod, axis=0)
        grad_ada = grad_ada + lax.dot_general(
            lifted.astype(jnp.float32), grad_mod, (((0,), (0,)), ((), ())), precision=highest
        )
    qkv_shard, out_shard, fc1_shard, fc2_shard, ada_shard = (
        lax.psum_scatter(
            grad_qkv.astype(jnp.bfloat16), "dp", scatter_dimension=1, tiled=True
        ).astype(jnp.float32),
        lax.psum_scatter(
            grad_out_w.astype(jnp.bfloat16), "dp", scatter_dimension=1, tiled=True
        ).astype(jnp.float32),
        lax.psum_scatter(
            grad_fc1.astype(jnp.bfloat16), "dp", scatter_dimension=0, tiled=True
        ).astype(jnp.float32),
        lax.psum_scatter(
            grad_fc2.astype(jnp.bfloat16), "dp", scatter_dimension=1, tiled=True
        ).astype(jnp.float32),
        lax.psum_scatter(
            grad_ada.astype(jnp.bfloat16), "dp", scatter_dimension=0, tiled=True
        ).astype(jnp.float32),
    )
    qv_full = lax.dynamic_update_slice_in_dim(
        jnp.zeros((2, model_width), jnp.float32), sum_qv, tp_rank * heads_dev, 1
    )
    fc1_full = lax.dynamic_update_slice_in_dim(
        jnp.zeros((hidden_dev * tp_size,), jnp.float32), sum_fc1, tp_rank * hidden_dev, 0
    )
    ada_full = lax.dynamic_update_slice_in_dim(
        jnp.zeros((mod_dev * tp_size,), jnp.float32), sum_ada, tp_rank * mod_dev, 0
    )
    qv_total, out_total, fc1_total, fc2_total, ada_total = lax.psum(
        (qv_full, sum_out_bias, fc1_full, sum_fc2, ada_full), ("dp", "tp")
    )
    return (
        jnp.stack(outputs),
        jnp.stack(input_grads),
        qkv_shard,
        qv_total,
        out_shard,
        out_total,
        fc1_shard,
        fc1_total,
        fc2_shard,
        fc2_total,
        ada_shard,
        ada_total,
    )


f32, bf16 = jnp.float32, jnp.bfloat16
AXES = ("dp", "tp")
CORE, CHIP = 1, 2
ROWS = 144
QT = 256
ET = 128
LOG2E = 1.4426950408889634
GELU_A = 0.7978845608028654
GELU_B = 0.7978845608028654 * 0.044715
VMEM_BYTES = 56 * 2**20
NN = (((1,), (0,)), ((), ()))
NT = (((1,), (1,)), ((), ()))
SMEM_SPEC = pl.BlockSpec(memory_space=pltpu.SMEM)
VMEM_SPEC = pl.BlockSpec(memory_space=pltpu.VMEM)
ANY_SPEC = pl.BlockSpec(memory_space=pl.ANY)


def cost(micros):
    return pl.CostEstimate(flops=int(4 * micros * 1.15e9), bytes_accessed=0, transcendentals=0)


def dot(left, right, dims=NN):
    return lax.dot_general(left, right, dims, preferred_element_type=f32)


def compiler_params():
    return pltpu.CompilerParams(vmem_limit_bytes=VMEM_BYTES)


def swap(values, dp_mask, tp_mask):
    pairs = [(d * 4 + t, (d ^ dp_mask) * 4 + (t ^ tp_mask)) for d in range(8) for t in range(4)]
    return lax.ppermute(values, AXES, pairs)


def across(values, tp_mask):
    return swap(values, 0, tp_mask)


def tie(values, after):
    count = len(values)
    return pl.pallas_call(
        lambda *refs: None,
        in_specs=[ANY_SPEC] * (count + len(after)),
        out_specs=[ANY_SPEC] * count,
        out_shape=[jax.ShapeDtypeStruct(v.shape, v.dtype) for v in values],
        input_output_aliases={i: i for i in range(count)},
    )(*values, *after)


def piece_copies(stage, place_ref, parts, outs, sem, start):
    for q in range(8):
        column = 0
        for i, width in enumerate(parts):
            source = stage.at[pl.ds(q * ROWS, ROWS), pl.ds(column, width)]
            column += width
            low, high, done = outs[2 * i], outs[2 * i + 1], sem.at[len(parts) * q + i]
            if not start:
                pltpu.make_async_copy(source, low.at[0], done).wait()
                continue
            spot = place_ref[q]

            @pl.when(spot < 4)
            def _():
                pltpu.make_async_copy(source, low.at[spot], done).start()

            @pl.when(spot >= 4)
            def _():
                pltpu.make_async_copy(source, high.at[spot - 4], done).start()


def mlp_tokens(x_ref, g_ref, w1_ref, w2_ref, b_ref, b2_ref, dm_ref, db_ref):
    pre = dot(x_ref[...], w1_ref[...]) + b_ref[...]
    act_grad = dot(g_ref[...], w2_ref[...])
    square = pre * pre
    bend = jnp.tanh(pre * (GELU_A + GELU_B * square))
    half = 0.5 + 0.5 * bend
    act = (pre * half).astype(bf16)
    slope = half + pre * (half * (1.0 - bend)) * (GELU_A + (3 * GELU_B) * square)
    pre_grad = (act_grad * slope).astype(bf16)
    b2_ref[...] = dot(act, w2_ref[...], NT).astype(bf16)
    dm_ref[...] = dot(pre_grad, w1_ref[...], NT).astype(bf16)
    add_rows(db_ref, pre_grad.astype(f32))
    return act, pre_grad


def mlp_whole_body(waits, tok_steps, x_ref, g_ref, xt_ref, gt_ref, w1_ref, w2_ref, b_ref, *refs):
    b2_ref, dm_ref, db_ref, dw_ref, act_s, slope_s = refs[waits:]
    step = pl.program_id(0)
    rows = x_ref.shape[0]
    ff = w1_ref.shape[1]

    @pl.when(step < tok_steps)
    def _():
        act, pre_grad = mlp_tokens(x_ref, g_ref, w1_ref, w2_ref, b_ref, b2_ref, dm_ref, db_ref)
        here = pl.ds(pl.multiple_of(step * rows, rows), rows)
        act_s[here, :] = act
        slope_s[here, :] = pre_grad

    @pl.when(step >= tok_steps)
    def _():
        dw_ref[:, :ff] = dot(xt_ref[...], slope_s[...]).astype(bf16)
        dw_ref[:, ff:] = dot(gt_ref[...], act_s[...]).astype(bf16)


def mlp_first_body(waits, x_ref, g_ref, w1_ref, w2_ref, b_ref, *refs):
    b2_ref, dm_ref, db_ref, act_ref, slope_ref = refs[waits:]
    act, pre_grad = mlp_tokens(x_ref, g_ref, w1_ref, w2_ref, b_ref, b2_ref, dm_ref, db_ref)
    act_ref[...] = act
    slope_ref[...] = pre_grad


def mlp_second_body(waits, xt_ref, gt_ref, act_ref, slope_ref, init_ref, *refs):
    (dw_ref,) = refs[waits:]
    ff = act_ref.shape[1]
    grad1 = dot(xt_ref[...], slope_ref[...]) + init_ref[:, :ff].astype(f32)
    dw_ref[:, :ff] = grad1.astype(bf16)
    grad2 = dot(gt_ref[...], act_ref[...]) + init_ref[:, ff:].astype(f32)
    dw_ref[:, ff:] = grad2.astype(bf16)


def mlp_call(body, steps, in_specs, operands, outs, scratch, waits, micros):
    n, d = operands[0].shape
    return pl.pallas_call(
        lambda *refs: body(len(waits), *refs),
        grid=(steps,),
        in_specs=in_specs + [ANY_SPEC] * len(waits),
        out_specs=[spec for spec, _, _ in outs],
        out_shape=[jax.ShapeDtypeStruct(shape, kind) for _, shape, kind in outs],
        scratch_shapes=scratch,
        compiler_params=compiler_params(),
        cost_estimate=cost(micros),
    )(*operands, *waits)


def columns(d, ff, block):
    return pl.BlockSpec((d, ff), lambda s: (0, block), pipeline_mode=pl.Buffered(1))


def mlp_weights(d, ff, weights):
    return [columns(d, ff, block) for _, block in weights] + [
        pl.BlockSpec((1, ff), lambda s: (0, 0))
    ]


def mlp_whole(x, g, xt, gt, weights, bias, waits=(), tok_steps=4, row_steps=4):
    n, d = x.shape
    ff = bias.shape[1]
    tok_rows, dim_rows = n // tok_steps, d // row_steps
    tok = pl.BlockSpec((tok_rows, d), lambda s: (jnp.minimum(s, tok_steps - 1), 0))
    row = pl.BlockSpec((dim_rows, n), lambda s: (jnp.maximum(s - tok_steps, 0), 0))
    wide = pl.BlockSpec((dim_rows, 2 * ff), lambda s: (jnp.maximum(s - tok_steps, 0), 0))
    return mlp_call(
        lambda count, *refs: mlp_whole_body(count, tok_steps, *refs),
        tok_steps + row_steps,
        [tok, tok, row, row] + mlp_weights(d, ff, weights),
        [x, g, xt, gt, *[w for w, _ in weights], bias],
        [
            (tok, (n, d), bf16),
            (tok, (n, d), bf16),
            (pl.BlockSpec((1, ff), lambda s: (0, 0)), (1, ff), f32),
            (wide, (d, 2 * ff), bf16),
        ],
        [pltpu.VMEM((n, ff), bf16), pltpu.VMEM((n, ff), bf16)],
        waits,
        27,
    )


def mlp_first(x, g, weights, bias, waits=(), steps=4):
    n, d = x.shape
    ff = bias.shape[1]
    tok = pl.BlockSpec((n // steps, d), lambda s: (s, 0))
    hid = pl.BlockSpec((n // steps, ff), lambda s: (s, 0))
    return mlp_call(
        mlp_first_body,
        steps,
        [tok, tok] + mlp_weights(d, ff, weights),
        [x, g, *[w for w, _ in weights], bias],
        [
            (tok, (n, d), bf16),
            (tok, (n, d), bf16),
            (pl.BlockSpec((1, ff), lambda s: (0, 0)), (1, ff), f32),
            (hid, (n, ff), bf16),
            (hid, (n, ff), bf16),
        ],
        [],
        waits,
        19,
    )


def mlp_second(xt, gt, act, slope, init, waits=(), steps=4):
    d, n = xt.shape
    ff = act.shape[1]
    row = pl.BlockSpec((d // steps, n), lambda s: (s, 0))
    wide = pl.BlockSpec((d // steps, 2 * ff), lambda s: (s, 0))
    all_hid = pl.BlockSpec((n, ff), lambda s: (0, 0), pipeline_mode=pl.Buffered(1))
    return mlp_call(
        mlp_second_body,
        steps,
        [row, row, all_hid, all_hid, wide],
        [xt, gt, act, slope, init],
        [(wide, (d, 2 * ff), bf16)],
        [],
        waits,
        12,
    )[0]


def attend_fwd_body(heads, lo_ref, hi_ref, x_ref, w_ref, b_ref, sc_ref, sr_ref, *refs):
    qkv_any, att_ref, lse_ref, part_ref, qt_s, k_s, vt_s, ot_s, qkv_ref, sem = refs[-10:]
    n = x_ref.shape[0]
    e = heads * HD
    c = LOG2E / math.sqrt(HD)
    qkv = dot(x_ref[...], w_ref[:, : 3 * e]) + b_ref[...]
    qkv_ref[...] = qkv.astype(bf16)
    save = pltpu.make_async_copy(qkv_ref, qkv_any, sem.at[0])
    save.start()
    qt = qkv[:, :e].T
    vt = qkv[:, 2 * e :].T
    every = range(heads)
    for h in every:
        qt_s[h] = qt[h * HD : (h + 1) * HD].astype(bf16)
        vt_s[h] = vt[h * HD : (h + 1) * HD].astype(bf16)
        k_s[h] = qkv[:, e + h * HD : e + (h + 1) * HD].astype(bf16)

    @pl.loop(0, n // QT)
    def _(i):
        qi = pl.ds(pl.multiple_of(i * QT, QT), QT)
        seg_row = sr_ref[:1, qi]
        first = lo_ref[i]

        def attend(count):
            kk = pl.ds(pl.multiple_of(first * QT, QT), count * QT)
            same = sc_ref[kk, :1] == seg_row
            scores = [
                jnp.where(same, dot(k_s[h, kk, :], qt_s[h, :, qi]), masked_score) for h in every
            ]
            tops = [jnp.max(v, axis=0, keepdims=True) for v in scores]
            probs = [jnp.exp2((v - t) * c) for v, t in zip(scores, tops)]
            totals = [jnp.sum(p, axis=0, keepdims=True) for p in probs]
            mixed = [dot(vt_s[h, :, kk], probs[h].astype(bf16)) for h in every]
            for h in every:
                ot_s[h * HD : (h + 1) * HD, qi] = mixed[h] / totals[h]
                lse_ref[h : h + 1, qi] = tops[h] * c + jnp.log(totals[h]) * LOG2E

        for count in range(1, n // QT + 1):
            pl.when(hi_ref[i] - first == count)(lambda count=count: attend(count))

    att = ot_s[...].T.astype(bf16)
    att_ref[...] = att
    part_ref[...] = dot(att, w_ref[:, 3 * e :], NT).astype(bf16)
    save.wait()


def attend_fwd(x, w, bias, lo, hi, seg_col, seg_row, waits=()):
    n, d = x.shape
    e = bias.shape[1] // 3
    heads = e // HD
    return pl.pallas_call(
        lambda *refs: attend_fwd_body(heads, *refs),
        in_specs=[SMEM_SPEC] * 2
        + [VMEM_SPEC, columns(d, 4 * e, w[1])]
        + [VMEM_SPEC] * 3
        + [ANY_SPEC] * len(waits),
        grid=(1,),
        out_specs=[ANY_SPEC] + [VMEM_SPEC] * 3,
        out_shape=[
            jax.ShapeDtypeStruct((n, 3 * e), bf16),
            jax.ShapeDtypeStruct((n, e), bf16),
            jax.ShapeDtypeStruct((8, n), f32),
            jax.ShapeDtypeStruct((n, d), bf16),
        ],
        scratch_shapes=[
            pltpu.VMEM((heads, HD, n), bf16),
            pltpu.VMEM((heads, n, HD), bf16),
            pltpu.VMEM((heads, HD, n), bf16),
            pltpu.VMEM((e, n), f32),
            pltpu.VMEM((n, 3 * e), bf16),
            pltpu.SemaphoreType.DMA((1,)),
        ],
        compiler_params=compiler_params(),
        cost_estimate=cost(16),
    )(lo, hi, x, w[0], bias, seg_col, seg_row, *waits)


def attend_bwd_body(final, parts, waits, heads, *refs):
    (lo_ref, hi_ref, place_ref, qkv_ref, att_ref, g_ref, gt_any, xt_any, w_ref, lse_ref, sc_ref, sr_ref) = refs[:12]
    init_any = refs[12] if final else None
    refs = refs[12 + final + waits :]
    grads_any, db_ref = refs[:2]
    refs = refs[2:]
    if parts:
        count = 2 * len(parts)
        outs, (stage, sem), refs = refs[:count], refs[-2:], refs[count:-2]
    else:
        stage, refs = refs[0], refs[1:]
    if final:
        init_ref, refs = refs[-1], refs[:-1]
    qt_s, q_s, k_s, kt_s, v_s, do_s, dot_s, delta_s, dqt_s, dk_s, dv_s, xt_ref, gt_ref, grads_ref, own_sem = refs
    loads = [
        pltpu.make_async_copy(xt_any, xt_ref, own_sem.at[0]),
        pltpu.make_async_copy(gt_any, gt_ref, own_sem.at[1]),
    ]
    if final:
        loads.append(pltpu.make_async_copy(init_any, init_ref, own_sem.at[2]))
    for load in loads:
        load.start()
    n = g_ref.shape[0]
    e = heads * HD
    c = LOG2E / math.sqrt(HD)
    scale = 1.0 / math.sqrt(HD)
    every = range(heads)
    out_grad = dot(g_ref[...], w_ref[:, 3 * e :]).astype(bf16).astype(f32)
    out_grad_t = out_grad.T
    qkv = qkv_ref[...].astype(f32)
    qt = qkv[:, :e].T
    kt = qkv[:, e : 2 * e].T
    att = att_ref[...]
    products = out_grad_t * att.astype(f32).T
    for h in every:
        s = slice(h * HD, (h + 1) * HD)
        qt_s[h] = qt[s].astype(bf16)
        kt_s[h] = kt[s].astype(bf16)
        dot_s[h] = out_grad_t[s].astype(bf16)
        delta_s[h] = jnp.sum(products[s], axis=0, keepdims=True)
        q_s[h] = qkv[:, h * HD : (h + 1) * HD].astype(bf16)
        k_s[h] = qkv[:, e + h * HD : e + (h + 1) * HD].astype(bf16)
        v_s[h] = qkv[:, 2 * e + h * HD : 2 * e + (h + 1) * HD].astype(bf16)
        do_s[h] = out_grad[:, s].astype(bf16)
    dk_s[...] = jnp.zeros(dk_s.shape, f32)
    dv_s[...] = jnp.zeros(dv_s.shape, f32)

    @pl.loop(0, n // QT)
    def _(i):
        qi = pl.ds(pl.multiple_of(i * QT, QT), QT)
        seg_row = sr_ref[:1, qi]
        first = lo_ref[i]

        def attend(count):
            kk = pl.ds(pl.multiple_of(first * QT, QT), count * QT)
            same = sc_ref[kk, :1] == seg_row
            scores = [dot(k_s[h, kk, :], qt_s[h, :, qi]) for h in every]
            p_grads = [dot(v_s[h, kk, :], dot_s[h, :, qi]) for h in every]
            probs = [
                jnp.where(same, jnp.exp2(scores[h] * c - lse_ref[h : h + 1, qi]), 0.0) for h in every
            ]
            s_grads = [(probs[h] * (p_grads[h] - delta_s[h, :, qi])).astype(bf16) for h in every]
            dv = [dot(probs[h].astype(bf16), do_s[h, qi, :]) for h in every]
            dk = [dot(s_grads[h], q_s[h, qi, :]) for h in every]
            dq = [dot(kt_s[h, :, kk], s_grads[h]) for h in every]
            for h in every:
                dv_s[h, kk, :] += dv[h]
                dk_s[h, kk, :] += dk[h]
                dqt_s[h, :, qi] = dq[h]

        for count in range(1, n // QT + 1):
            pl.when(hi_ref[i] - first == count)(lambda count=count: attend(count))

    dq = jnp.concatenate([dqt_s[h] for h in every], axis=0).T * scale
    dk = [dk_s[h] * scale for h in every]
    dv = [dv_s[h] for h in every]
    grads = jnp.concatenate([dq] + dk + dv, axis=1).astype(bf16)
    db_ref[...] = jnp.sum(grads.astype(f32), axis=0, keepdims=True)
    grads_ref[...] = grads
    save = pltpu.make_async_copy(grads_ref, grads_any, own_sem.at[3])
    save.start()
    for load in loads:
        load.wait()
    dw = jnp.concatenate([dot(xt_ref[...], grads), dot(gt_ref[...], att)], axis=1)
    if final:
        dw += init_ref[...].astype(f32)
    stage[...] = dw.astype(bf16)
    if parts:
        piece_copies(stage, place_ref, parts, outs, sem, True)
        piece_copies(stage, place_ref, parts, outs, sem, False)
    save.wait()


def attend_bwd(
    qkv, att, g, gt, xt, w, lse, lo, hi, seg_col, seg_row, place, init=None, parts=(), waits=()
):
    n, d = g.shape
    e = att.shape[1]
    heads = e // HD
    final = init is not None
    operands = [lo, hi, place, qkv, att, g, gt, xt, w[0], lse, seg_col, seg_row]
    in_specs = [SMEM_SPEC] * 3 + [VMEM_SPEC] * 3 + [ANY_SPEC] * 2
    in_specs += [columns(d, 4 * e, w[1])] + [VMEM_SPEC] * 3
    out_shape = [jax.ShapeDtypeStruct((n, 3 * e), bf16), jax.ShapeDtypeStruct((1, 3 * e), f32)]
    out_specs = [ANY_SPEC, VMEM_SPEC]
    tall, wide = (heads, n, HD), (heads, HD, n)
    scratch = [pltpu.VMEM(s, bf16) for s in (wide, tall, tall, wide, tall, tall, wide)]
    scratch += [pltpu.VMEM((heads, 1, n), f32)] + [pltpu.VMEM(s, f32) for s in (wide, tall, tall)]
    scratch += [pltpu.VMEM(s, bf16) for s in ((d, n), (d, n), (n, 3 * e))]
    scratch += [pltpu.SemaphoreType.DMA((4,))]
    if final:
        operands.append(init)
        in_specs.append(ANY_SPEC)
        scratch.append(pltpu.VMEM((d, 4 * e), bf16))
    for width in parts:
        out_shape += [jax.ShapeDtypeStruct((4, ROWS, width), bf16)] * 2
        out_specs += [ANY_SPEC] * 2
    if parts:
        scratch += [pltpu.VMEM((d, 4 * e), bf16), pltpu.SemaphoreType.DMA((8 * len(parts),))]
    else:
        out_shape.append(jax.ShapeDtypeStruct((d, 4 * e), bf16))
        out_specs.append(VMEM_SPEC)
    return pl.pallas_call(
        lambda *refs: attend_bwd_body(final, parts, len(waits), heads, *refs),
        grid=(1,),
        in_specs=in_specs + [ANY_SPEC] * len(waits),
        out_specs=out_specs,
        out_shape=out_shape,
        scratch_shapes=scratch,
        compiler_params=compiler_params(),
        cost_estimate=cost(7),
    )(*operands, *waits)


def token_rows(mod_ref, block, sc_ref):
    d = mod_ref.shape[1] // 6
    seg = sc_ref[:, :1]
    rows = mod_ref[:, block * d : (block + 1) * d]
    value = jnp.where(seg == 0, rows[0:1], rows[1:2])
    value = jnp.where(seg == 2, rows[2:3], value)
    return jnp.where(seg == 3, rows[3:4], value)


def normalize(values):
    centred = values - jnp.mean(values, axis=-1, keepdims=True)
    inverse = lax.rsqrt(jnp.mean(centred * centred, axis=-1, keepdims=True) + epsilon)
    return centred * inverse, inverse


def norm_back(normed, inverse, grad):
    mean = jnp.mean(grad, axis=-1, keepdims=True)
    along = jnp.mean(grad * normed, axis=-1, keepdims=True)
    return inverse * (grad - mean - normed * along)


def add_images(acc_ref, first_ref, last_ref, sc_ref, columns):
    step = pl.program_id(0)
    seg = sc_ref[:, :1]

    @pl.when(step == 0)
    def _():
        acc_ref[...] = jnp.zeros(acc_ref.shape, f32)

    @pl.loop(first_ref[step], last_ref[step] + 1)
    def _(image):
        mine = seg == image
        for i, values in enumerate(columns):
            d = values.shape[1]
            part = jnp.sum(jnp.where(mine, values, 0.0), axis=0, keepdims=True)
            acc_ref[pl.ds(image, 1), i * d : (i + 1) * d] += part


def add_rows(acc_ref, values):
    part = jnp.sum(values, axis=0, keepdims=True)

    @pl.when(pl.program_id(0) == 0)
    def _():
        acc_ref[...] = part

    @pl.when(pl.program_id(0) > 0)
    def _():
        acc_ref[...] += part


def enter_body(x_ref, mod_ref, sc_ref, a_ref, at_ref):
    normed, _ = normalize(x_ref[...].astype(f32))
    a = normed * (1.0 + token_rows(mod_ref, 1, sc_ref)) + token_rows(mod_ref, 0, sc_ref)
    a_ref[...] = a.astype(bf16)
    at_ref[...] = a.T.astype(bf16)


def branch_body(g_ref, mod_ref, sc_ref, bg_ref, bgt_ref, sum_ref):
    bg = token_rows(mod_ref, 5, sc_ref) * g_ref[...].astype(f32)
    bg_ref[...] = bg.astype(bf16)
    bgt_ref[...] = bg.T.astype(bf16)
    add_rows(sum_ref, bg)


def middle_body(x_ref, p0, p1, p2, p3, mod_ref, sc_ref, ob_ref, hid_ref, br_ref, m_ref, mt_ref):
    branch = p0[...].astype(f32) + p1[...].astype(f32) + p2[...].astype(f32) + p3[...].astype(f32)
    branch = branch + ob_ref[...]
    br_ref[...] = branch
    hidden = x_ref[...].astype(f32) + token_rows(mod_ref, 2, sc_ref) * branch
    hid_ref[...] = hidden
    normed, _ = normalize(hidden)
    m = normed * (1.0 + token_rows(mod_ref, 4, sc_ref)) + token_rows(mod_ref, 3, sc_ref)
    m_ref[...] = m.astype(bf16)
    mt_ref[...] = m.T.astype(bf16)


def turn_body(
    first_ref, last_ref, hid_ref, br_ref, g_ref, b0, b1, b2, b3, d0, d1, d2, d3, mod_ref, sc_ref, fb_ref,
    out_ref, hg_ref, bg_ref, bgt_ref, sum_ref, img_ref,
):
    hidden, g = hid_ref[...], g_ref[...].astype(f32)
    branch = b0[...].astype(f32) + b1[...].astype(f32) + b2[...].astype(f32) + b3[...].astype(f32)
    branch = branch + fb_ref[...]
    out_ref[...] = (hidden + token_rows(mod_ref, 5, sc_ref) * branch).astype(bf16)
    m_grad = d0[...].astype(f32) + d1[...].astype(f32) + d2[...].astype(f32) + d3[...].astype(f32)
    normed, inverse = normalize(hidden)
    hidden_grad = g + norm_back(normed, inverse, m_grad * (1.0 + token_rows(mod_ref, 4, sc_ref)))
    hg_ref[...] = hidden_grad
    bg = token_rows(mod_ref, 2, sc_ref) * hidden_grad
    bg_ref[...] = bg.astype(bf16)
    bgt_ref[...] = bg.T.astype(bf16)
    add_rows(sum_ref, bg)
    add_images(
        img_ref, first_ref, last_ref, sc_ref,
        (hidden_grad * br_ref[...], m_grad, m_grad * normed, g * branch),
    )


def back_body(q0, q1, q2, q3, w0, w1, w2, w3, *refs):
    out_ref = refs[-1]
    width = q0.shape[1]
    total = dot(q0[...], w0[:, :width], NT)
    for grads, w in ((q1, w1), (q2, w2), (q3, w3)):
        total += dot(grads[...], w[:, :width], NT)
    out_ref[...] = total


def back_to_input(grads, weights, waits, steps=4):
    n, width = grads[0].shape
    d = weights[0][0].shape[0]
    return pl.pallas_call(
        back_body,
        grid=(steps,),
        in_specs=[pl.BlockSpec((n // steps, width), lambda s: (s, 0))] * 4
        + [columns(d, width * 4 // 3, block) for _, block in weights]
        + [ANY_SPEC] * len(waits),
        out_specs=pl.BlockSpec((n // steps, d), lambda s: (s, 0)),
        out_shape=jax.ShapeDtypeStruct((n, d), f32),
        compiler_params=compiler_params(),
        cost_estimate=cost(17),
    )(*grads, *[w for w, _ in weights], *waits)


def leave_body(first_ref, last_ref, x_ref, hg_ref, ag_ref, mod_ref, sc_ref, out_ref, img_ref):
    a_grad = ag_ref[...]
    normed, inverse = normalize(x_ref[...].astype(f32))
    back = norm_back(normed, inverse, a_grad * (1.0 + token_rows(mod_ref, 1, sc_ref)))
    out_ref[...] = (hg_ref[...] + back).astype(bf16)
    add_images(img_ref, first_ref, last_ref, sc_ref, (a_grad, a_grad * normed))


def by_rows(body_fn, micros, scalars, operands, outs, waits=()):
    def spec(kind, shape):
        if kind == "t":
            return pl.BlockSpec((ET, shape[1]), lambda s: (s, 0))
        if kind == "T":
            return pl.BlockSpec((shape[0], ET), lambda s: (0, s))
        return pl.BlockSpec(shape, lambda s: (0, 0))

    n = operands[0][1].shape[0]
    own_in = len(scalars) + len(operands)

    def body(*refs):
        body_fn(*refs[:own_in], *refs[own_in + len(waits) :])

    return pl.pallas_call(
        body,
        grid=(n // ET,),
        in_specs=[SMEM_SPEC] * len(scalars)
        + [spec(k, v.shape) for k, v in operands]
        + [ANY_SPEC] * len(waits),
        out_specs=[spec(k, s) for k, s, _ in outs],
        out_shape=[jax.ShapeDtypeStruct(s, t) for _, s, t in outs],
        compiler_params=compiler_params(),
        cost_estimate=cost(micros),
    )(*scalars, *[v for _, v in operands], *waits)


class Row:
    def __init__(self, values, core):
        self.core = core
        self.own = lax.dynamic_index_in_dim(values, core, 0, keepdims=False)
        self.got = across(lax.dynamic_index_in_dim(values, 1 - core, 0, keepdims=False), CORE)

    def whole(self):
        first = self.core == 0
        return jnp.concatenate(
            [jnp.where(first, self.own, self.got), jnp.where(first, self.got, self.own)]
        )


def trade_back(row, core):
    half = row.shape[0] // 2
    own = lax.dynamic_slice_in_dim(row, core * half, half, 0)
    got = across(lax.dynamic_slice_in_dim(row, (1 - core) * half, half, 0), CORE)
    first = core == 0
    return jnp.stack([jnp.where(first, own, got), jnp.where(first, got, own)])


def add_pieces(*terms):
    return sum(t.astype(f32) for t in terms)


class Scatter:
    def __init__(self, low, high):
        self.low, self.got = low, swap(high, 1, 0)

    def turn(self):
        sums = [add_pieces(self.low[i], self.got[i]) for i in range(4)]
        self.low = sums[0]
        self.got = [swap(sums[i].astype(bf16), 2 * i, 0) for i in range(1, 4)]

    def total(self):
        return add_pieces(self.low, *self.got)


def lanes(values, rows):
    values = values.reshape(rows, -1)
    spare = -values.shape[1] % 128
    return jnp.pad(values.astype(bf16), ((0, 0), (0, spare))).reshape(rows, -1, 128)


def to_owners(grads, pieces, sums):
    count, width = grads.shape
    grads = lanes(grads.reshape(count, 4, width // 4).transpose(1, 0, 2), 4)
    parts = [jnp.concatenate([grads] * 8)]
    if pieces is not None:
        parts.append(lanes(pieces, 32))
    if sums:
        sums = lanes(jnp.concatenate(sums, axis=1), 1)
        parts.append(jnp.broadcast_to(sums, (32,) + sums.shape[1:]))
    return lax.all_to_all(jnp.concatenate(parts, axis=1), AXES, 0, 0, tiled=True)


def taken_apart(got, count, width):
    rows = count * width // 128
    return got[:, :rows].reshape(32 * count, width), got[:, rows:].reshape(32, -1)


def row_body(
    block_input,
    segment_ids,
    conditioning,
    w_qkv,
    qv_bias,
    w_out,
    out_bias,
    w_fc1,
    fc1_bias,
    w_fc2,
    fc2_bias,
    w_ada,
    ada_bias,
    cotangent,
):
    dp_rank, tp_rank = lax.axis_index("dp"), lax.axis_index("tp")
    core, chip = tp_rank & 1, tp_rank >> 1
    d = block_input.shape[2]
    e, ff, mod_dev = w_qkv.shape[2], w_fc1.shape[1], w_ada.shape[1]
    flips = jnp.arange(8, dtype=jnp.int32) ^ dp_rank
    place = (flips & 1) * 4 + (flips >> 1)
    att_shard = jnp.concatenate([w_qkv[0], w_qkv[1], w_qkv[2], w_out.T], axis=1)
    mlp_shard = jnp.concatenate([w_fc1, w_fc2.T], axis=1)
    near_att = lax.all_gather(att_shard, "dp", axis=0, tiled=True)
    x = Row(block_input, core).whole()
    g_row = Row(cotangent, core)
    seg = lax.dynamic_slice(segment_ids, (core, chip * PACK), (1, PACK))[0]
    seg_col = jnp.broadcast_to(seg[:, None], (PACK, 128))
    seg_row = jnp.broadcast_to(seg[None, :], (8, PACK))
    tiles = seg.reshape(-1, QT)
    lo = jnp.sum((tiles[None, :, -1] < tiles[:, None, 0]).astype(jnp.int32), axis=1)
    hi = jnp.sum((tiles[None, :, 0] <= tiles[:, None, -1]).astype(jnp.int32), axis=1)
    small = seg.reshape(-1, ET)
    first, last = small[:, 0], small[:, -1]
    lifted = smooth_gate(conditioning.astype(f32)).astype(bf16).reshape(-1, 8, w_ada.shape[0])
    lifted = lax.all_to_all(lifted.transpose(1, 0, 2), "dp", 0, 0)
    lifted = lifted.reshape(8, 2, 2, IMG_ROW, -1).transpose(0, 2, 1, 3, 4).reshape(32 * IMG_ROW, -1)
    mod_part = dot(lifted, w_ada).reshape(32, IMG_ROW, mod_dev)
    (mlp_shard,) = tie([mlp_shard], (mod_part,))
    peer_shard = across(mlp_shard, CHIP)
    (mod_part,) = tie([lax.all_to_all(mod_part, AXES, 0, 0)], (x,))
    mod_part = mod_part.reshape(8, 4, IMG_ROW, mod_dev)
    modulation = jnp.sum(mod_part, axis=0).transpose(1, 0, 2).reshape(IMG_ROW, -1)
    modulation = modulation + ada_bias.astype(f32)
    (peer_shard,) = tie([peer_shard], (modulation,))
    far_w = lax.all_gather(peer_shard, "dp", axis=0, tiled=True)
    near_w = lax.all_gather(mlp_shard, "dp", axis=0, tiled=True)
    row_f, row_b = ((PACK, d), f32), ((PACK, d), bf16)
    turned = ((d, PACK), bf16)
    a, a_t = by_rows(
        enter_body,
        6,
        (),
        [("t", x), ("w", modulation), ("t", seg_col)],
        [("t", *row_b), ("T", *turned)],
        waits=(peer_shard,),
    )
    qkv_bias = jnp.stack([qv_bias[0], jnp.zeros_like(qv_bias[0]), qv_bias[1]]).astype(f32)
    kept = {}

    def forward(k, waits):
        bias = lax.dynamic_slice_in_dim(qkv_bias, (tp_rank ^ k) * e, e, 1).reshape(1, 3 * e)
        kept[k] = attend_fwd(a, att_w[k], bias, lo, hi, seg_col, seg_row, waits)
        return (kept[k][2],)

    (near_att,) = tie([near_att], (a,))
    att_w = [(v, 0) for v in (near_att, across(near_att, CORE), across(near_att, CHIP))]
    after = forward(1, forward(0, ()))
    (g_row.got,) = tie([g_row.got], after)
    g = g_row.whole()
    bg2, bg2_t, fc2_sum = by_rows(
        branch_body,
        6,
        (),
        [("t", g), ("w", modulation), ("t", seg_col)],
        [("t", *row_b), ("T", *turned), ("w", (1, d), f32)],
        waits=after,
    )
    (far_att,) = tie([att_w[2][0]], (fc2_sum,))
    att_w[2:] = [(far_att, 0), (across(far_att, CORE), 0)]
    after = forward(2, after)
    (far_w,) = tie([far_w], after)
    after = forward(3, after + (far_w,))
    partner_w = across(far_w, CORE)
    hidden, branch1, m, m_t = by_rows(
        middle_body,
        12,
        (),
        [("t", x)]
        + [("t", kept[k][3]) for k in range(4)]
        + [("w", modulation), ("t", seg_col), ("w", out_bias.astype(f32)[None])],
        [("t", *row_f), ("t", *row_f), ("t", *row_b), ("T", *turned)],
    )
    done = {}
    fc1_f = fc1_bias.astype(f32)[None]

    def fc1_part(k):
        return lax.dynamic_slice_in_dim(fc1_f, (tp_rank ^ k) * ff, ff, 1)

    def halves(w):
        return ((w, 0), (w, 1))

    done[3] = mlp_whole(m, bg2, m_t, bg2_t, halves(partner_w), fc1_part(3))
    init = across(done[3][3], CORE)
    done[2] = mlp_first(m, bg2, halves(far_w), fc1_part(2), (done[3][2],))
    (near_w,) = tie([near_w], (done[2][2],))
    partner_w = across(near_w, CORE)
    grad = mlp_second(m_t, bg2_t, *done[2][3:], init, (near_w,))
    far_sum = lax.psum_scatter(grad, "dp", scatter_dimension=0, tiled=True)
    done[1] = mlp_whole(m, bg2, m_t, bg2_t, halves(partner_w), fc1_part(1), (grad,))
    init = across(done[1][3], CORE)
    done[0] = mlp_first(m, bg2, halves(near_w), fc1_part(0), (done[1][2],))
    grad = mlp_second(m_t, bg2_t, *done[0][3:], init)
    near_sum = lax.psum_scatter(grad, "dp", scatter_dimension=0, tiled=True)
    block_output, hidden_grad, bg1, bg1_t, out_sum, img_late = by_rows(
        turn_body,
        5,
        (first, last),
        [("t", hidden), ("t", branch1), ("t", g)]
        + [("t", done[k][0]) for k in range(4)]
        + [("t", done[k][1]) for k in range(4)]
        + [("w", modulation), ("t", seg_col), ("w", fc2_bias.astype(f32)[None])],
        [("t", *row_b), ("t", *row_f), ("t", *row_b), ("T", *turned), ("w", (1, d), f32), ("w", (IMG_ROW, 4 * d), f32)],
        waits=(grad,),
    )
    fc1_sum = jnp.zeros((1, 4 * ff), f32)
    for k in range(4):
        fc1_sum = lax.dynamic_update_slice_in_dim(fc1_sum, done[k][2], (tp_rank ^ k) * ff, 1)
    late = jnp.concatenate([jnp.zeros((IMG_ROW, 2 * d), f32), img_late], axis=1)
    late_sums = [jnp.sum(img_late, axis=0, keepdims=True), fc1_sum, fc2_sum, out_sum]
    late_sums = jnp.concatenate(late_sums, axis=1).reshape(32, -1)
    late = to_owners(late, late_sums, [])
    back = {}

    def backward(k, init, waits, parts=()):
        qkv, att, lse, _ = kept[k]
        back[k] = attend_bwd(
            qkv, att, bg1, bg1_t, a_t, att_w[k], lse, lo, hi, seg_col, seg_row, place, init, parts, waits
        )
        return (back[k][1],)

    block_output = trade_back(block_output, core)
    after = backward(1, None, ())
    init = across(back[1][2], CORE)
    (block_output,) = tie([block_output], after)
    after = backward(3, None, after + (block_output, far_sum))
    init, last_init = across(back[3][2], CORE), init
    after = backward(2, init, after, (4 * e,))
    (late,) = tie([late], after)
    late_grads, late_sums = taken_apart(late, IMG_ROW, mod_dev)
    far = Scatter(*back[2][2:])
    far_peer = across(far_sum, CHIP)
    after = backward(0, last_init, after)
    near_att = lax.psum_scatter(back[0][2], "dp", scatter_dimension=0, tiled=True)
    far.got, far_peer = tie([far.got, far_peer], after)
    far.turn()
    a_grad = back_to_input([back[k][0] for k in range(4)], att_w, (far.low, near_sum))
    far.got = tie(far.got, (a_grad,))
    far_att = across(far.total().astype(bf16), CHIP)
    input_grad, img_early = by_rows(
        leave_body,
        11,
        (first, last),
        [("t", x), ("t", hidden_grad), ("t", a_grad), ("w", modulation), ("t", seg_col)],
        [("t", *row_b), ("w", (IMG_ROW, 2 * d), f32)],
    )
    (far_att,) = tie([far_att], (img_early,))
    att_total = near_att.astype(f32) + far_att.astype(f32)
    near_sum = near_sum.astype(f32)
    fc1_grad = near_sum[:, :ff]
    fc2_grad = near_sum[:, ff:]
    far_peer = far_peer.astype(f32)
    fc1_grad, fc2_grad = fc1_grad + far_peer[:, :ff], fc2_grad + far_peer[:, ff:]
    qv_sum = jnp.zeros((2, 4 * e), f32)
    for k in range(4):
        grads = back[k][1].reshape(3, e)
        qv_sum = lax.dynamic_update_slice_in_dim(
            qv_sum, jnp.stack([grads[0], grads[2]]), (tp_rank ^ k) * e, 1
        )
    early = jnp.concatenate([img_early, jnp.zeros((IMG_ROW, 4 * d), f32)], axis=1)
    late_sums = jnp.sum(late_sums.astype(f32), axis=0, keepdims=True)
    early_sums = [late_sums, jnp.sum(img_early, axis=0, keepdims=True), qv_sum.reshape(1, -1)]
    early = to_owners(early, None, early_sums)
    early_grads, early_sums = taken_apart(early, IMG_ROW, mod_dev)
    share = late_sums.shape[1]
    used = (5 * d + d + 4 * ff) // 32
    late_sums = early_sums[:, :used].astype(f32).reshape(-1)
    late_bias, fc1_total, fc2_total, out_total = jnp.split(
        late_sums, [4 * d, 4 * d + 4 * ff, 5 * d + 4 * ff]
    )
    early_sums = jnp.sum(early_sums[:, share : share + 2 * d + 8 * e].astype(f32), axis=0)
    early_bias, qv_total = jnp.split(early_sums, [2 * d])
    qv_total = qv_total.reshape(2, -1)
    ada_total = jnp.concatenate([early_bias, late_bias])
    mod_grad = late_grads.astype(f32) + early_grads.astype(f32)
    ada_grad = lax.dot_general(
        lifted.astype(f32), mod_grad, (((0,), (0,)), ((), ())), precision=highest
    )
    return (
        block_output,
        trade_back(input_grad, core),
        jnp.stack([att_total[:, i * e : (i + 1) * e] for i in range(3)]),
        qv_total,
        att_total[:, 3 * e :].T,
        out_total,
        fc1_grad,
        fc1_total,
        fc2_grad.T,
        fc2_total,
        ada_grad,
        ada_total,
    )


def body(*arrays):
    block_input, w_qkv, w_fc1 = arrays[0], arrays[3], arrays[7]
    micro, tokens, width = block_input.shape
    heads_dev, rows = w_qkv.shape[2], w_fc1.shape[0]
    if (
        lax.axis_size("dp") == 8
        and lax.axis_size("tp") == 4
        and micro == 2
        and micro * tokens == PACK
        and rows == ROWS
        and rows * 8 == width
        and heads_dev * 4 == width
        and w_fc1.shape[1] % 384 == 0
    ):
        return row_body(*arrays)
    return general_body(*arrays)


def solution(mesh):
    placed = (
        P(None, ("dp", "tp"), None),
        P(None, "dp"),
        P(None, "dp", None),
        P(None, "dp", "tp"),
        P(),
        P("tp", "dp"),
        P(),
        P("dp", "tp"),
        P(),
        P("tp", "dp"),
        P(),
        P("dp", "tp"),
        P(),
        P(None, ("dp", "tp"), None),
    )
    return jax.shard_map(
        body,
        mesh=mesh,
        in_specs=placed,
        out_specs=(
            P(None, ("dp", "tp"), None),
            P(None, ("dp", "tp"), None),
            P(None, "dp", "tp"),
            P(),
            P("tp", "dp"),
            P(),
            P("dp", "tp"),
            P(),
            P("tp", "dp"),
            P(),
            P("dp", "tp"),
            P(),
        ),
        check_vma=False,
    )
```

```python
import math

import jax
import jax.numpy as jnp
from jax import lax
from jax.experimental import pallas as pl
from jax.experimental.pallas import tpu as pltpu
from jax.sharding import PartitionSpec as P

HD = 72
PACK = 1024
IMG_ROW = 4


highest = lax.Precision.HIGHEST
epsilon = 1e-06
masked_score = -1e30


def layer_norm(values):
    centred = values - jnp.mean(values, axis=-1, keepdims=True)
    return centred * lax.rsqrt(jnp.mean(centred * centred, axis=-1, keepdims=True) + epsilon)


def gelu_tanh(values):
    return (
        0.5
        * values
        * (1.0 + jnp.tanh(0.7978845608028654 * (values + 0.044715 * values * values * values)))
    )


def smooth_gate(values):
    return values / (1.0 + jnp.exp(-values))


def to_blocks(values, local_heads):
    shaped = values.reshape(values.shape[0] // PACK, PACK, local_heads, HD)
    return shaped.transpose(0, 2, 1, 3).reshape(-1, PACK, HD)


def from_blocks(blocks, local_heads):
    shaped = blocks.reshape(-1, local_heads, PACK, HD).transpose(0, 2, 1, 3)
    return shaped.reshape(-1, local_heads * HD)


def block_segments(segment_group, local_heads):
    shaped = segment_group.reshape(-1, 1, PACK)
    return jnp.broadcast_to(shaped, (shaped.shape[0], local_heads, PACK)).reshape(-1, PACK)


def project_heads(activations, full_qkv, bias_pair):
    projected = jnp.einsum("gd,cde->cge", activations, full_qkv, preferred_element_type=jnp.float32)
    bias_rows = jnp.stack([bias_pair[0], jnp.zeros_like(bias_pair[0]), bias_pair[1]])
    return (projected + bias_rows[:, None, :]).astype(jnp.bfloat16)


def masked_scores(query_rows, key_rows, segment_row):
    raw_scores = lax.dot_general(
        query_rows, key_rows, (((1,), (1,)), ((), ())), preferred_element_type=jnp.float32
    ) / math.sqrt(HD)
    same_image = segment_row[:, None] == segment_row[None, :]
    return (same_image, jnp.where(same_image, raw_scores, masked_score))


def attend_forward(block_items):
    query_rows, key_rows, value_rows, segment_row = block_items
    same_image, scores = masked_scores(query_rows, key_rows, segment_row)
    row_max = jnp.max(scores, axis=-1, keepdims=True)
    exponents = jnp.exp(scores - row_max)
    row_sums = jnp.sum(exponents, axis=-1, keepdims=True)
    probs_low = (exponents / row_sums).astype(jnp.bfloat16)
    attended = jnp.dot(probs_low, value_rows, preferred_element_type=jnp.float32).astype(
        jnp.bfloat16
    )
    return (attended, (row_max + jnp.log(row_sums))[:, 0])


def attend_backward(block_items):
    query_rows, key_rows, value_rows, segment_row, log_total, attended_grad = block_items
    same_image, scores = masked_scores(query_rows, key_rows, segment_row)
    attn_probs = jnp.where(same_image, jnp.exp(scores - log_total[:, None]), 0.0)
    value_grad = lax.dot_general(
        attn_probs.astype(jnp.bfloat16),
        attended_grad,
        (((0,), (0,)), ((), ())),
        preferred_element_type=jnp.float32,
    )
    probs_grad = lax.dot_general(
        attended_grad, value_rows, (((1,), (1,)), ((), ())), preferred_element_type=jnp.float32
    )
    centred = probs_grad - jnp.sum(attn_probs * probs_grad, axis=-1, keepdims=True)
    scores_grad = (attn_probs * centred).astype(jnp.bfloat16)
    query_grad = jnp.dot(scores_grad, key_rows, preferred_element_type=jnp.float32) / math.sqrt(HD)
    key_grad = lax.dot_general(
        scores_grad, query_rows, (((0,), (0,)), ((), ())), preferred_element_type=jnp.float32
    ) / math.sqrt(HD)
    return (
        query_grad.astype(jnp.bfloat16),
        key_grad.astype(jnp.bfloat16),
        value_grad.astype(jnp.bfloat16),
    )


def general_body(
    block_input,
    segment_ids,
    conditioning,
    w_qkv,
    qv_bias,
    w_out,
    out_bias,
    w_fc1,
    fc1_bias,
    w_fc2,
    fc2_bias,
    w_ada,
    ada_bias,
    cotangent,
):
    micro_count, tok_dev, model_width = block_input.shape
    tp_size = lax.axis_size("tp")
    tp_rank = lax.axis_index("tp")
    heads_dev = w_qkv.shape[2]
    hidden_dev = w_fc1.shape[1]
    mod_dev = w_ada.shape[1]
    cond_width = conditioning.shape[2]
    images = conditioning.shape[1]
    local_heads = heads_dev // HD
    qv_local = lax.dynamic_slice_in_dim(
        qv_bias.astype(jnp.float32), tp_rank * heads_dev, heads_dev, 1
    )
    fc1_local = lax.dynamic_slice_in_dim(
        fc1_bias.astype(jnp.float32), tp_rank * hidden_dev, hidden_dev, 0
    )
    ada_local = lax.dynamic_slice_in_dim(
        ada_bias.astype(jnp.float32), tp_rank * mod_dev, mod_dev, 0
    )
    out_bias_f = out_bias.astype(jnp.float32)
    fc2_bias_f = fc2_bias.astype(jnp.float32)
    positions = tp_rank * tok_dev + jnp.arange(tok_dev, dtype=jnp.int32)
    grad_qkv = jnp.zeros((3, model_width, heads_dev), jnp.float32)
    grad_out_w = jnp.zeros((heads_dev, model_width), jnp.float32)
    grad_fc1 = jnp.zeros((model_width, hidden_dev), jnp.float32)
    grad_fc2 = jnp.zeros((hidden_dev, model_width), jnp.float32)
    grad_ada = jnp.zeros((cond_width, mod_dev), jnp.float32)
    sum_qv = jnp.zeros((2, heads_dev), jnp.float32)
    sum_out_bias = jnp.zeros((model_width,), jnp.float32)
    sum_fc1 = jnp.zeros((hidden_dev,), jnp.float32)
    sum_fc2 = jnp.zeros((model_width,), jnp.float32)
    sum_ada = jnp.zeros((mod_dev,), jnp.float32)
    outputs = []
    input_grads = []
    for micro_step in range(micro_count):
        full_qkv, full_out, full_fc1, full_fc2, full_ada = (
            lax.all_gather(w_qkv, "dp", axis=1, tiled=True),
            lax.all_gather(w_out, "dp", axis=1, tiled=True),
            lax.all_gather(w_fc1, "dp", axis=0, tiled=True),
            lax.all_gather(w_fc2, "dp", axis=1, tiled=True),
            lax.all_gather(w_ada, "dp", axis=0, tiled=True),
        )
        lifted = smooth_gate(conditioning[micro_step].astype(jnp.float32)).astype(jnp.bfloat16)
        mod_part = jnp.dot(lifted, full_ada, preferred_element_type=jnp.float32) + ada_local
        modulation = lax.all_gather(mod_part, "tp", axis=1, tiled=True)
        segment_group = segment_ids[micro_step]
        segment_local = lax.dynamic_slice_in_dim(segment_group, tp_rank * tok_dev, tok_dev, 0)
        image_index = positions // PACK * IMG_ROW + segment_local
        onehot = (image_index[:, None] == jnp.arange(images, dtype=jnp.int32)[None, :]).astype(
            jnp.float32
        )
        token_mod = jnp.dot(onehot, modulation, precision=highest)
        shift_one, scale_one, gate_one, shift_two, scale_two, gate_two = jnp.split(
            token_mod, 6, axis=1
        )
        inputs = block_input[micro_step].astype(jnp.float32)
        normed_one = layer_norm(inputs)
        attn_in = (normed_one * (1.0 + scale_one) + shift_one).astype(jnp.bfloat16)
        attn_full = lax.all_gather(attn_in, "tp", axis=0, tiled=True)
        projected = project_heads(attn_full, full_qkv, qv_local)
        segment_blocks = block_segments(segment_group, local_heads)
        attended_blocks, log_totals = lax.map(
            attend_forward,
            (
                to_blocks(projected[0], local_heads),
                to_blocks(projected[1], local_heads),
                to_blocks(projected[2], local_heads),
                segment_blocks,
            ),
        )
        attended = from_blocks(attended_blocks, local_heads)
        branch_one = lax.psum_scatter(
            jnp.dot(attended, full_out, preferred_element_type=jnp.float32).astype(jnp.bfloat16),
            "tp",
            scatter_dimension=0,
            tiled=True,
        ).astype(jnp.float32)
        hidden = inputs + gate_one * (branch_one + out_bias_f)
        normed_two = layer_norm(hidden)
        mlp_in = (normed_two * (1.0 + scale_two) + shift_two).astype(jnp.bfloat16)
        mlp_full = lax.all_gather(mlp_in, "tp", axis=0, tiled=True)
        pre_act = jnp.dot(mlp_full, full_fc1, preferred_element_type=jnp.float32) + fc1_local
        activated = gelu_tanh(pre_act).astype(jnp.bfloat16)
        branch_two = lax.psum_scatter(
            jnp.dot(activated, full_fc2, preferred_element_type=jnp.float32).astype(jnp.bfloat16),
            "tp",
            scatter_dimension=0,
            tiled=True,
        ).astype(jnp.float32)
        outputs.append((hidden + gate_two * (branch_two + fc2_bias_f)).astype(jnp.bfloat16))
        grad_y = cotangent[micro_step].astype(jnp.float32)
        sum_fc2 = sum_fc2 + jnp.sum(gate_two * grad_y, axis=0)
        grad_gate_two = grad_y * (branch_two + fc2_bias_f)
        grad_branch_two = (gate_two * grad_y).astype(jnp.bfloat16)
        grad_two_full = lax.all_gather(grad_branch_two, "tp", axis=0, tiled=True)
        attn_back, mlp_back = (
            lax.all_gather(attn_in, "tp", axis=0, tiled=True),
            lax.all_gather(mlp_in, "tp", axis=0, tiled=True),
        )
        proj_back = project_heads(attn_back, full_qkv, qv_local)
        pre_back = jnp.dot(mlp_back, full_fc1, preferred_element_type=jnp.float32) + fc1_local
        act_back, gelu_pull = jax.vjp(gelu_tanh, pre_back)
        grad_fc2 = grad_fc2 + lax.dot_general(
            act_back.astype(jnp.bfloat16),
            grad_two_full,
            (((0,), (0,)), ((), ())),
            preferred_element_type=jnp.float32,
        )
        grad_act = lax.dot_general(
            grad_two_full, full_fc2, (((1,), (1,)), ((), ())), preferred_element_type=jnp.float32
        )
        grad_pre = gelu_pull(grad_act)[0].astype(jnp.bfloat16)
        sum_fc1 = sum_fc1 + jnp.sum(grad_pre.astype(jnp.float32), axis=0)
        grad_fc1 = grad_fc1 + lax.dot_general(
            mlp_back, grad_pre, (((0,), (0,)), ((), ())), preferred_element_type=jnp.float32
        )
        grad_mlp_in = lax.psum_scatter(
            lax.dot_general(
                grad_pre, full_fc1, (((1,), (1,)), ((), ())), preferred_element_type=jnp.float32
            ).astype(jnp.bfloat16),
            "tp",
            scatter_dimension=0,
            tiled=True,
        ).astype(jnp.float32)
        norm_two_pull = jax.vjp(layer_norm, hidden)[1]
        grad_hidden = grad_y + norm_two_pull(grad_mlp_in * (1.0 + scale_two))[0]
        sum_out_bias = sum_out_bias + jnp.sum(gate_one * grad_hidden, axis=0)
        grad_gate_one = grad_hidden * (branch_one + out_bias_f)
        grad_branch_one = (gate_one * grad_hidden).astype(jnp.bfloat16)
        grad_one_full = lax.all_gather(grad_branch_one, "tp", axis=0, tiled=True)
        grad_out_w = grad_out_w + lax.dot_general(
            attended, grad_one_full, (((0,), (0,)), ((), ())), preferred_element_type=jnp.float32
        )
        grad_attended = lax.dot_general(
            grad_one_full, full_out, (((1,), (1,)), ((), ())), preferred_element_type=jnp.float32
        ).astype(jnp.bfloat16)
        query_blocks, key_blocks, value_blocks = lax.map(
            attend_backward,
            (
                to_blocks(proj_back[0], local_heads),
                to_blocks(proj_back[1], local_heads),
                to_blocks(proj_back[2], local_heads),
                segment_blocks,
                log_totals,
                to_blocks(grad_attended, local_heads),
            ),
        )
        grad_proj = jnp.stack(
            [
                from_blocks(query_blocks, local_heads),
                from_blocks(key_blocks, local_heads),
                from_blocks(value_blocks, local_heads),
            ]
        )
        sum_qv = sum_qv + jnp.stack(
            [
                jnp.sum(grad_proj[0].astype(jnp.float32), axis=0),
                jnp.sum(grad_proj[2].astype(jnp.float32), axis=0),
            ]
        )
        grad_qkv = grad_qkv + jnp.einsum(
            "gd,cge->cde", attn_back, grad_proj, preferred_element_type=jnp.float32
        )
        grad_attn_in = lax.psum_scatter(
            jnp.einsum(
                "cge,cde->gd", grad_proj, full_qkv, preferred_element_type=jnp.float32
            ).astype(jnp.bfloat16),
            "tp",
            scatter_dimension=0,
            tiled=True,
        ).astype(jnp.float32)
        norm_one_pull = jax.vjp(layer_norm, inputs)[1]
        input_grads.append(
            (grad_hidden + norm_one_pull(grad_attn_in * (1.0 + scale_one))[0]).astype(jnp.bfloat16)
        )
        grad_token_mod = jnp.concatenate(
            [
                grad_attn_in,
                grad_attn_in * normed_one,
                grad_gate_one,
                grad_mlp_in,
                grad_mlp_in * normed_two,
                grad_gate_two,
            ],
            axis=1,
        )
        mod_grad_part = lax.dot_general(
            onehot, grad_token_mod, (((0,), (0,)), ((), ())), precision=highest
        )
        grad_mod = lax.psum_scatter(
            mod_grad_part.astype(jnp.bfloat16), "tp", scatter_dimension=1, tiled=True
        ).astype(jnp.float32)
        sum_ada = sum_ada + jnp.sum(grad_mod, axis=0)
        grad_ada = grad_ada + lax.dot_general(
            lifted.astype(jnp.float32), grad_mod, (((0,), (0,)), ((), ())), precision=highest
        )
    qkv_shard, out_shard, fc1_shard, fc2_shard, ada_shard = (
        lax.psum_scatter(
            grad_qkv.astype(jnp.bfloat16), "dp", scatter_dimension=1, tiled=True
        ).astype(jnp.float32),
        lax.psum_scatter(
            grad_out_w.astype(jnp.bfloat16), "dp", scatter_dimension=1, tiled=True
        ).astype(jnp.float32),
        lax.psum_scatter(
            grad_fc1.astype(jnp.bfloat16), "dp", scatter_dimension=0, tiled=True
        ).astype(jnp.float32),
        lax.psum_scatter(
            grad_fc2.astype(jnp.bfloat16), "dp", scatter_dimension=1, tiled=True
        ).astype(jnp.float32),
        lax.psum_scatter(
            grad_ada.astype(jnp.bfloat16), "dp", scatter_dimension=0, tiled=True
        ).astype(jnp.float32),
    )
    qv_full = lax.dynamic_update_slice_in_dim(
        jnp.zeros((2, model_width), jnp.float32), sum_qv, tp_rank * heads_dev, 1
    )
    fc1_full = lax.dynamic_update_slice_in_dim(
        jnp.zeros((hidden_dev * tp_size,), jnp.float32), sum_fc1, tp_rank * hidden_dev, 0
    )
    ada_full = lax.dynamic_update_slice_in_dim(
        jnp.zeros((mod_dev * tp_size,), jnp.float32), sum_ada, tp_rank * mod_dev, 0
    )
    qv_total, out_total, fc1_total, fc2_total, ada_total = lax.psum(
        (qv_full, sum_out_bias, fc1_full, sum_fc2, ada_full), ("dp", "tp")
    )
    return (
        jnp.stack(outputs),
        jnp.stack(input_grads),
        qkv_shard,
        qv_total,
        out_shard,
        out_total,
        fc1_shard,
        fc1_total,
        fc2_shard,
        fc2_total,
        ada_shard,
        ada_total,
    )


f32, bf16 = jnp.float32, jnp.bfloat16
AXES = ("dp", "tp")
CORE, CHIP = 1, 2
ROWS = 144
QT = 256
ET = 128
LOG2E = 1.4426950408889634
GELU_A = 0.7978845608028654
GELU_B = 0.7978845608028654 * 0.044715
VMEM_BYTES = 56 * 2**20
NN = (((1,), (0,)), ((), ()))
NT = (((1,), (1,)), ((), ()))
SMEM_SPEC = pl.BlockSpec(memory_space=pltpu.SMEM)
VMEM_SPEC = pl.BlockSpec(memory_space=pltpu.VMEM)
ANY_SPEC = pl.BlockSpec(memory_space=pl.ANY)


def cost(micros):
    return pl.CostEstimate(flops=int(4 * micros * 1.15e9), bytes_accessed=0, transcendentals=0)


def dot(left, right, dims=NN):
    return lax.dot_general(left, right, dims, preferred_element_type=f32)


def compiler_params():
    return pltpu.CompilerParams(vmem_limit_bytes=VMEM_BYTES)


def swap(values, dp_mask, tp_mask):
    pairs = [(d * 4 + t, (d ^ dp_mask) * 4 + (t ^ tp_mask)) for d in range(8) for t in range(4)]
    return lax.ppermute(values, AXES, pairs)


def across(values, tp_mask):
    return swap(values, 0, tp_mask)


def tie(values, after):
    count = len(values)
    return pl.pallas_call(
        lambda *refs: None,
        in_specs=[ANY_SPEC] * (count + len(after)),
        out_specs=[ANY_SPEC] * count,
        out_shape=[jax.ShapeDtypeStruct(v.shape, v.dtype) for v in values],
        input_output_aliases={i: i for i in range(count)},
    )(*values, *after)


def piece_copies(stage, place_ref, parts, outs, sem, start):
    for q in range(8):
        column = 0
        for i, width in enumerate(parts):
            source = stage.at[pl.ds(q * ROWS, ROWS), pl.ds(column, width)]
            column += width
            low, high, done = outs[2 * i], outs[2 * i + 1], sem.at[len(parts) * q + i]
            if not start:
                pltpu.make_async_copy(source, low.at[0], done).wait()
                continue
            spot = place_ref[q]

            @pl.when(spot < 4)
            def _():
                pltpu.make_async_copy(source, low.at[spot], done).start()

            @pl.when(spot >= 4)
            def _():
                pltpu.make_async_copy(source, high.at[spot - 4], done).start()


def mlp_tokens(x_ref, g_ref, w1_ref, w2_ref, b_ref, b2_ref, dm_ref, db_ref):
    pre = dot(x_ref[...], w1_ref[...]) + b_ref[...]
    act_grad = dot(g_ref[...], w2_ref[...])
    square = pre * pre
    bend = jnp.tanh(pre * (GELU_A + GELU_B * square))
    half = 0.5 + 0.5 * bend
    act = (pre * half).astype(bf16)
    slope = half + pre * (half * (1.0 - bend)) * (GELU_A + (3 * GELU_B) * square)
    pre_grad = (act_grad * slope).astype(bf16)
    b2_ref[...] = dot(act, w2_ref[...], NT).astype(bf16)
    dm_ref[...] = dot(pre_grad, w1_ref[...], NT).astype(bf16)
    add_rows(db_ref, pre_grad.astype(f32))
    return act, pre_grad


def mlp_whole_body(waits, tok_steps, x_ref, g_ref, xt_ref, gt_ref, w1_ref, w2_ref, b_ref, *refs):
    b2_ref, dm_ref, db_ref, dw_ref, act_s, slope_s = refs[waits:]
    step = pl.program_id(0)
    rows = x_ref.shape[0]
    ff = w1_ref.shape[1]

    @pl.when(step < tok_steps)
    def _():
        act, pre_grad = mlp_tokens(x_ref, g_ref, w1_ref, w2_ref, b_ref, b2_ref, dm_ref, db_ref)
        here = pl.ds(pl.multiple_of(step * rows, rows), rows)
        act_s[here, :] = act
        slope_s[here, :] = pre_grad

    @pl.when(step >= tok_steps)
    def _():
        dw_ref[:, :ff] = dot(xt_ref[...], slope_s[...]).astype(bf16)
        dw_ref[:, ff:] = dot(gt_ref[...], act_s[...]).astype(bf16)


def mlp_first_body(waits, x_ref, g_ref, w1_ref, w2_ref, b_ref, *refs):
    b2_ref, dm_ref, db_ref, act_ref, slope_ref = refs[waits:]
    act, pre_grad = mlp_tokens(x_ref, g_ref, w1_ref, w2_ref, b_ref, b2_ref, dm_ref, db_ref)
    act_ref[...] = act
    slope_ref[...] = pre_grad


def mlp_second_body(waits, xt_ref, gt_ref, act_ref, slope_ref, init_ref, *refs):
    (dw_ref,) = refs[waits:]
    ff = act_ref.shape[1]
    grad1 = dot(xt_ref[...], slope_ref[...]) + init_ref[:, :ff].astype(f32)
    dw_ref[:, :ff] = grad1.astype(bf16)
    grad2 = dot(gt_ref[...], act_ref[...]) + init_ref[:, ff:].astype(f32)
    dw_ref[:, ff:] = grad2.astype(bf16)


def mlp_call(body, steps, in_specs, operands, outs, scratch, waits, micros):
    n, d = operands[0].shape
    return pl.pallas_call(
        lambda *refs: body(len(waits), *refs),
        grid=(steps,),
        in_specs=in_specs + [ANY_SPEC] * len(waits),
        out_specs=[spec for spec, _, _ in outs],
        out_shape=[jax.ShapeDtypeStruct(shape, kind) for _, shape, kind in outs],
        scratch_shapes=scratch,
        compiler_params=compiler_params(),
        cost_estimate=cost(micros),
    )(*operands, *waits)


def columns(d, ff, block):
    return pl.BlockSpec((d, ff), lambda s: (0, block), pipeline_mode=pl.Buffered(1))


def mlp_weights(d, ff, weights):
    return [columns(d, ff, block) for _, block in weights] + [
        pl.BlockSpec((1, ff), lambda s: (0, 0))
    ]


def mlp_whole(x, g, xt, gt, weights, bias, waits=(), tok_steps=4, row_steps=4):
    n, d = x.shape
    ff = bias.shape[1]
    tok_rows, dim_rows = n // tok_steps, d // row_steps
    tok = pl.BlockSpec((tok_rows, d), lambda s: (jnp.minimum(s, tok_steps - 1), 0))
    row = pl.BlockSpec((dim_rows, n), lambda s: (jnp.maximum(s - tok_steps, 0), 0))
    wide = pl.BlockSpec((dim_rows, 2 * ff), lambda s: (jnp.maximum(s - tok_steps, 0), 0))
    return mlp_call(
        lambda count, *refs: mlp_whole_body(count, tok_steps, *refs),
        tok_steps + row_steps,
        [tok, tok, row, row] + mlp_weights(d, ff, weights),
        [x, g, xt, gt, *[w for w, _ in weights], bias],
        [
            (tok, (n, d), bf16),
            (tok, (n, d), bf16),
            (pl.BlockSpec((1, ff), lambda s: (0, 0)), (1, ff), f32),
            (wide, (d, 2 * ff), bf16),
        ],
        [pltpu.VMEM((n, ff), bf16), pltpu.VMEM((n, ff), bf16)],
        waits,
        27,
    )


def mlp_first(x, g, weights, bias, waits=(), steps=4):
    n, d = x.shape
    ff = bias.shape[1]
    tok = pl.BlockSpec((n // steps, d), lambda s: (s, 0))
    hid = pl.BlockSpec((n // steps, ff), lambda s: (s, 0))
    return mlp_call(
        mlp_first_body,
        steps,
        [tok, tok] + mlp_weights(d, ff, weights),
        [x, g, *[w for w, _ in weights], bias],
        [
            (tok, (n, d), bf16),
            (tok, (n, d), bf16),
            (pl.BlockSpec((1, ff), lambda s: (0, 0)), (1, ff), f32),
            (hid, (n, ff), bf16),
            (hid, (n, ff), bf16),
        ],
        [],
        waits,
        19,
    )


def mlp_second(xt, gt, act, slope, init, waits=(), steps=4):
    d, n = xt.shape
    ff = act.shape[1]
    row = pl.BlockSpec((d // steps, n), lambda s: (s, 0))
    wide = pl.BlockSpec((d // steps, 2 * ff), lambda s: (s, 0))
    all_hid = pl.BlockSpec((n, ff), lambda s: (0, 0), pipeline_mode=pl.Buffered(1))
    return mlp_call(
        mlp_second_body,
        steps,
        [row, row, all_hid, all_hid, wide],
        [xt, gt, act, slope, init],
        [(wide, (d, 2 * ff), bf16)],
        [],
        waits,
        12,
    )[0]


def attend_fwd_body(heads, lo_ref, hi_ref, x_ref, w_ref, b_ref, sc_ref, sr_ref, *refs):
    qkv_any, att_ref, lse_ref, part_ref, qt_s, k_s, vt_s, ot_s, qkv_ref, sem = refs[-10:]
    n = x_ref.shape[0]
    e = heads * HD
    c = LOG2E / math.sqrt(HD)
    qkv = dot(x_ref[...], w_ref[:, : 3 * e]) + b_ref[...]
    qkv_ref[...] = qkv.astype(bf16)
    save = pltpu.make_async_copy(qkv_ref, qkv_any, sem.at[0])
    save.start()
    qt = qkv[:, :e].T
    vt = qkv[:, 2 * e :].T
    every = range(heads)
    for h in every:
        qt_s[h] = qt[h * HD : (h + 1) * HD].astype(bf16)
        vt_s[h] = vt[h * HD : (h + 1) * HD].astype(bf16)
        k_s[h] = qkv[:, e + h * HD : e + (h + 1) * HD].astype(bf16)

    @pl.loop(0, n // QT)
    def _(i):
        qi = pl.ds(pl.multiple_of(i * QT, QT), QT)
        seg_row = sr_ref[:1, qi]
        first = lo_ref[i]

        def attend(count):
            kk = pl.ds(pl.multiple_of(first * QT, QT), count * QT)
            same = sc_ref[kk, :1] == seg_row
            scores = [
                jnp.where(same, dot(k_s[h, kk, :], qt_s[h, :, qi]), masked_score) for h in every
            ]
            tops = [jnp.max(v, axis=0, keepdims=True) for v in scores]
            probs = [jnp.exp2((v - t) * c) for v, t in zip(scores, tops)]
            totals = [jnp.sum(p, axis=0, keepdims=True) for p in probs]
            mixed = [dot(vt_s[h, :, kk], probs[h].astype(bf16)) for h in every]
            for h in every:
                ot_s[h * HD : (h + 1) * HD, qi] = mixed[h] / totals[h]
                lse_ref[h : h + 1, qi] = tops[h] * c + jnp.log(totals[h]) * LOG2E

        for count in range(1, n // QT + 1):
            pl.when(hi_ref[i] - first == count)(lambda count=count: attend(count))

    att = ot_s[...].T.astype(bf16)
    att_ref[...] = att
    part_ref[...] = dot(att, w_ref[:, 3 * e :], NT).astype(bf16)
    save.wait()


def attend_fwd(x, w, bias, lo, hi, seg_col, seg_row, waits=()):
    n, d = x.shape
    e = bias.shape[1] // 3
    heads = e // HD
    return pl.pallas_call(
        lambda *refs: attend_fwd_body(heads, *refs),
        in_specs=[SMEM_SPEC] * 2
        + [VMEM_SPEC, columns(d, 4 * e, w[1])]
        + [VMEM_SPEC] * 3
        + [ANY_SPEC] * len(waits),
        grid=(1,),
        out_specs=[ANY_SPEC] + [VMEM_SPEC] * 3,
        out_shape=[
            jax.ShapeDtypeStruct((n, 3 * e), bf16),
            jax.ShapeDtypeStruct((n, e), bf16),
            jax.ShapeDtypeStruct((8, n), f32),
            jax.ShapeDtypeStruct((n, d), bf16),
        ],
        scratch_shapes=[
            pltpu.VMEM((heads, HD, n), bf16),
            pltpu.VMEM((heads, n, HD), bf16),
            pltpu.VMEM((heads, HD, n), bf16),
            pltpu.VMEM((e, n), f32),
            pltpu.VMEM((n, 3 * e), bf16),
            pltpu.SemaphoreType.DMA((1,)),
        ],
        compiler_params=compiler_params(),
        cost_estimate=cost(16),
    )(lo, hi, x, w[0], bias, seg_col, seg_row, *waits)


def attend_bwd_body(final, parts, waits, heads, *refs):
    (lo_ref, hi_ref, place_ref, qkv_ref, att_ref, g_ref, gt_any, xt_any, w_ref, lse_ref, sc_ref, sr_ref) = refs[:12]
    init_any = refs[12] if final else None
    refs = refs[12 + final + waits :]
    grads_any, db_ref = refs[:2]
    refs = refs[2:]
    if parts:
        count = 2 * len(parts)
        outs, (stage, sem), refs = refs[:count], refs[-2:], refs[count:-2]
    else:
        stage, refs = refs[0], refs[1:]
    if final:
        init_ref, refs = refs[-1], refs[:-1]
    qt_s, q_s, k_s, kt_s, v_s, do_s, dot_s, delta_s, dqt_s, dk_s, dv_s, xt_ref, gt_ref, grads_ref, own_sem = refs
    loads = [
        pltpu.make_async_copy(xt_any, xt_ref, own_sem.at[0]),
        pltpu.make_async_copy(gt_any, gt_ref, own_sem.at[1]),
    ]
    if final:
        loads.append(pltpu.make_async_copy(init_any, init_ref, own_sem.at[2]))
    for load in loads:
        load.start()
    n = g_ref.shape[0]
    e = heads * HD
    c = LOG2E / math.sqrt(HD)
    scale = 1.0 / math.sqrt(HD)
    every = range(heads)
    out_grad = dot(g_ref[...], w_ref[:, 3 * e :]).astype(bf16).astype(f32)
    out_grad_t = out_grad.T
    qkv = qkv_ref[...].astype(f32)
    qt = qkv[:, :e].T
    kt = qkv[:, e : 2 * e].T
    att = att_ref[...]
    products = out_grad_t * att.astype(f32).T
    for h in every:
        s = slice(h * HD, (h + 1) * HD)
        qt_s[h] = qt[s].astype(bf16)
        kt_s[h] = kt[s].astype(bf16)
        dot_s[h] = out_grad_t[s].astype(bf16)
        delta_s[h] = jnp.sum(products[s], axis=0, keepdims=True)
        q_s[h] = qkv[:, h * HD : (h + 1) * HD].astype(bf16)
        k_s[h] = qkv[:, e + h * HD : e + (h + 1) * HD].astype(bf16)
        v_s[h] = qkv[:, 2 * e + h * HD : 2 * e + (h + 1) * HD].astype(bf16)
        do_s[h] = out_grad[:, s].astype(bf16)
    dk_s[...] = jnp.zeros(dk_s.shape, f32)
    dv_s[...] = jnp.zeros(dv_s.shape, f32)

    @pl.loop(0, n // QT)
    def _(i):
        qi = pl.ds(pl.multiple_of(i * QT, QT), QT)
        seg_row = sr_ref[:1, qi]
        first = lo_ref[i]

        def attend(count):
            kk = pl.ds(pl.multiple_of(first * QT, QT), count * QT)
            same = sc_ref[kk, :1] == seg_row
            scores = [dot(k_s[h, kk, :], qt_s[h, :, qi]) for h in every]
            p_grads = [dot(v_s[h, kk, :], dot_s[h, :, qi]) for h in every]
            probs = [
                jnp.where(same, jnp.exp2(scores[h] * c - lse_ref[h : h + 1, qi]), 0.0) for h in every
            ]
            s_grads = [(probs[h] * (p_grads[h] - delta_s[h, :, qi])).astype(bf16) for h in every]
            dv = [dot(probs[h].astype(bf16), do_s[h, qi, :]) for h in every]
            dk = [dot(s_grads[h], q_s[h, qi, :]) for h in every]
            dq = [dot(kt_s[h, :, kk], s_grads[h]) for h in every]
            for h in every:
                dv_s[h, kk, :] += dv[h]
                dk_s[h, kk, :] += dk[h]
                dqt_s[h, :, qi] = dq[h]

        for count in range(1, n // QT + 1):
            pl.when(hi_ref[i] - first == count)(lambda count=count: attend(count))

    dq = jnp.concatenate([dqt_s[h] for h in every], axis=0).T * scale
    dk = [dk_s[h] * scale for h in every]
    dv = [dv_s[h] for h in every]
    grads = jnp.concatenate([dq] + dk + dv, axis=1).astype(bf16)
    db_ref[...] = jnp.sum(grads.astype(f32), axis=0, keepdims=True)
    grads_ref[...] = grads
    save = pltpu.make_async_copy(grads_ref, grads_any, own_sem.at[3])
    save.start()
    for load in loads:
        load.wait()
    dw = jnp.concatenate([dot(xt_ref[...], grads), dot(gt_ref[...], att)], axis=1)
    if final:
        dw += init_ref[...].astype(f32)
    stage[...] = dw.astype(bf16)
    if parts:
        piece_copies(stage, place_ref, parts, outs, sem, True)
        piece_copies(stage, place_ref, parts, outs, sem, False)
    save.wait()


def attend_bwd(
    qkv, att, g, gt, xt, w, lse, lo, hi, seg_col, seg_row, place, init=None, parts=(), waits=()
):
    n, d = g.shape
    e = att.shape[1]
    heads = e // HD
    final = init is not None
    operands = [lo, hi, place, qkv, att, g, gt, xt, w[0], lse, seg_col, seg_row]
    in_specs = [SMEM_SPEC] * 3 + [VMEM_SPEC] * 3 + [ANY_SPEC] * 2
    in_specs += [columns(d, 4 * e, w[1])] + [VMEM_SPEC] * 3
    out_shape = [jax.ShapeDtypeStruct((n, 3 * e), bf16), jax.ShapeDtypeStruct((1, 3 * e), f32)]
    out_specs = [ANY_SPEC, VMEM_SPEC]
    tall, wide = (heads, n, HD), (heads, HD, n)
    scratch = [pltpu.VMEM(s, bf16) for s in (wide, tall, tall, wide, tall, tall, wide)]
    scratch += [pltpu.VMEM((heads, 1, n), f32)] + [pltpu.VMEM(s, f32) for s in (wide, tall, tall)]
    scratch += [pltpu.VMEM(s, bf16) for s in ((d, n), (d, n), (n, 3 * e))]
    scratch += [pltpu.SemaphoreType.DMA((4,))]
    if final:
        operands.append(init)
        in_specs.append(ANY_SPEC)
        scratch.append(pltpu.VMEM((d, 4 * e), bf16))
    for width in parts:
        out_shape += [jax.ShapeDtypeStruct((4, ROWS, width), bf16)] * 2
        out_specs += [ANY_SPEC] * 2
    if parts:
        scratch += [pltpu.VMEM((d, 4 * e), bf16), pltpu.SemaphoreType.DMA((8 * len(parts),))]
    else:
        out_shape.append(jax.ShapeDtypeStruct((d, 4 * e), bf16))
        out_specs.append(VMEM_SPEC)
    return pl.pallas_call(
        lambda *refs: attend_bwd_body(final, parts, len(waits), heads, *refs),
        grid=(1,),
        in_specs=in_specs + [ANY_SPEC] * len(waits),
        out_specs=out_specs,
        out_shape=out_shape,
        scratch_shapes=scratch,
        compiler_params=compiler_params(),
        cost_estimate=cost(7),
    )(*operands, *waits)


def token_rows(mod_ref, block, sc_ref):
    d = mod_ref.shape[1] // 6
    seg = sc_ref[:, :1]
    rows = mod_ref[:, block * d : (block + 1) * d]
    value = jnp.where(seg == 0, rows[0:1], rows[1:2])
    value = jnp.where(seg == 2, rows[2:3], value)
    return jnp.where(seg == 3, rows[3:4], value)


def normalize(values):
    centred = values - jnp.mean(values, axis=-1, keepdims=True)
    inverse = lax.rsqrt(jnp.mean(centred * centred, axis=-1, keepdims=True) + epsilon)
    return centred * inverse, inverse


def norm_back(normed, inverse, grad):
    mean = jnp.mean(grad, axis=-1, keepdims=True)
    along = jnp.mean(grad * normed, axis=-1, keepdims=True)
    return inverse * (grad - mean - normed * along)


def add_images(acc_ref, first_ref, last_ref, sc_ref, columns):
    step = pl.program_id(0)
    seg = sc_ref[:, :1]

    @pl.when(step == 0)
    def _():
        acc_ref[...] = jnp.zeros(acc_ref.shape, f32)

    @pl.loop(first_ref[step], last_ref[step] + 1)
    def _(image):
        mine = seg == image
        for i, values in enumerate(columns):
            d = values.shape[1]
            part = jnp.sum(jnp.where(mine, values, 0.0), axis=0, keepdims=True)
            acc_ref[pl.ds(image, 1), i * d : (i + 1) * d] += part


def add_rows(acc_ref, values):
    part = jnp.sum(values, axis=0, keepdims=True)

    @pl.when(pl.program_id(0) == 0)
    def _():
        acc_ref[...] = part

    @pl.when(pl.program_id(0) > 0)
    def _():
        acc_ref[...] += part


def enter_body(x_ref, mod_ref, sc_ref, a_ref, at_ref):
    normed, _ = normalize(x_ref[...].astype(f32))
    a = normed * (1.0 + token_rows(mod_ref, 1, sc_ref)) + token_rows(mod_ref, 0, sc_ref)
    a_ref[...] = a.astype(bf16)
    at_ref[...] = a.T.astype(bf16)


def branch_body(g_ref, mod_ref, sc_ref, bg_ref, bgt_ref, sum_ref):
    bg = token_rows(mod_ref, 5, sc_ref) * g_ref[...].astype(f32)
    bg_ref[...] = bg.astype(bf16)
    bgt_ref[...] = bg.T.astype(bf16)
    add_rows(sum_ref, bg)


def middle_body(x_ref, p0, p1, p2, p3, mod_ref, sc_ref, ob_ref, hid_ref, br_ref, m_ref, mt_ref):
    branch = p0[...].astype(f32) + p1[...].astype(f32) + p2[...].astype(f32) + p3[...].astype(f32)
    branch = branch + ob_ref[...]
    br_ref[...] = branch
    hidden = x_ref[...].astype(f32) + token_rows(mod_ref, 2, sc_ref) * branch
    hid_ref[...] = hidden
    normed, _ = normalize(hidden)
    m = normed * (1.0 + token_rows(mod_ref, 4, sc_ref)) + token_rows(mod_ref, 3, sc_ref)
    m_ref[...] = m.astype(bf16)
    mt_ref[...] = m.T.astype(bf16)


def turn_body(
    first_ref, last_ref, hid_ref, br_ref, g_ref, b0, b1, b2, b3, d0, d1, d2, d3, mod_ref, sc_ref, fb_ref,
    out_ref, hg_ref, bg_ref, bgt_ref, sum_ref, img_ref,
):
    hidden, g = hid_ref[...], g_ref[...].astype(f32)
    branch = b0[...].astype(f32) + b1[...].astype(f32) + b2[...].astype(f32) + b3[...].astype(f32)
    branch = branch + fb_ref[...]
    out_ref[...] = (hidden + token_rows(mod_ref, 5, sc_ref) * branch).astype(bf16)
    m_grad = d0[...].astype(f32) + d1[...].astype(f32) + d2[...].astype(f32) + d3[...].astype(f32)
    normed, inverse = normalize(hidden)
    hidden_grad = g + norm_back(normed, inverse, m_grad * (1.0 + token_rows(mod_ref, 4, sc_ref)))
    hg_ref[...] = hidden_grad
    bg = token_rows(mod_ref, 2, sc_ref) * hidden_grad
    bg_ref[...] = bg.astype(bf16)
    bgt_ref[...] = bg.T.astype(bf16)
    add_rows(sum_ref, bg)
    add_images(
        img_ref, first_ref, last_ref, sc_ref,
        (hidden_grad * br_ref[...], m_grad, m_grad * normed, g * branch),
    )


def back_body(q0, q1, q2, q3, w0, w1, w2, w3, *refs):
    out_ref = refs[-1]
    width = q0.shape[1]
    total = dot(q0[...], w0[:, :width], NT)
    for grads, w in ((q1, w1), (q2, w2), (q3, w3)):
        total += dot(grads[...], w[:, :width], NT)
    out_ref[...] = total


def back_to_input(grads, weights, waits, steps=4):
    n, width = grads[0].shape
    d = weights[0][0].shape[0]
    return pl.pallas_call(
        back_body,
        grid=(steps,),
        in_specs=[pl.BlockSpec((n // steps, width), lambda s: (s, 0))] * 4
        + [columns(d, width * 4 // 3, block) for _, block in weights]
        + [ANY_SPEC] * len(waits),
        out_specs=pl.BlockSpec((n // steps, d), lambda s: (s, 0)),
        out_shape=jax.ShapeDtypeStruct((n, d), f32),
        compiler_params=compiler_params(),
        cost_estimate=cost(1),
    )(*grads, *[w for w, _ in weights], *waits)


def leave_body(first_ref, last_ref, x_ref, hg_ref, ag_ref, mod_ref, sc_ref, out_ref, img_ref):
    a_grad = ag_ref[...]
    normed, inverse = normalize(x_ref[...].astype(f32))
    back = norm_back(normed, inverse, a_grad * (1.0 + token_rows(mod_ref, 1, sc_ref)))
    out_ref[...] = (hg_ref[...] + back).astype(bf16)
    add_images(img_ref, first_ref, last_ref, sc_ref, (a_grad, a_grad * normed))


def by_rows(body_fn, micros, scalars, operands, outs, waits=()):
    def spec(kind, shape):
        if kind == "t":
            return pl.BlockSpec((ET, shape[1]), lambda s: (s, 0))
        if kind == "T":
            return pl.BlockSpec((shape[0], ET), lambda s: (0, s))
        return pl.BlockSpec(shape, lambda s: (0, 0))

    n = operands[0][1].shape[0]
    own_in = len(scalars) + len(operands)

    def body(*refs):
        body_fn(*refs[:own_in], *refs[own_in + len(waits) :])

    return pl.pallas_call(
        body,
        grid=(n // ET,),
        in_specs=[SMEM_SPEC] * len(scalars)
        + [spec(k, v.shape) for k, v in operands]
        + [ANY_SPEC] * len(waits),
        out_specs=[spec(k, s) for k, s, _ in outs],
        out_shape=[jax.ShapeDtypeStruct(s, t) for _, s, t in outs],
        compiler_params=compiler_params(),
        cost_estimate=cost(micros),
    )(*scalars, *[v for _, v in operands], *waits)


class Row:
    def __init__(self, values, core):
        self.core = core
        self.own = lax.dynamic_index_in_dim(values, core, 0, keepdims=False)
        self.got = across(lax.dynamic_index_in_dim(values, 1 - core, 0, keepdims=False), CORE)

    def whole(self):
        first = self.core == 0
        return jnp.concatenate(
            [jnp.where(first, self.own, self.got), jnp.where(first, self.got, self.own)]
        )


def trade_back(row, core):
    half = row.shape[0] // 2
    own = lax.dynamic_slice_in_dim(row, core * half, half, 0)
    got = across(lax.dynamic_slice_in_dim(row, (1 - core) * half, half, 0), CORE)
    first = core == 0
    return jnp.stack([jnp.where(first, own, got), jnp.where(first, got, own)])


def add_pieces(*terms):
    return sum(t.astype(f32) for t in terms)


class Scatter:
    def __init__(self, low, high):
        self.low, self.got = low, swap(high, 1, 0)

    def turn(self):
        sums = [add_pieces(self.low[i], self.got[i]) for i in range(4)]
        self.low = sums[0]
        self.got = [swap(sums[i].astype(bf16), 2 * i, 0) for i in range(1, 4)]

    def total(self):
        return add_pieces(self.low, *self.got)


def lanes(values, rows):
    values = values.reshape(rows, -1)
    spare = -values.shape[1] % 128
    return jnp.pad(values.astype(bf16), ((0, 0), (0, spare))).reshape(rows, -1, 128)


def to_owners(grads, pieces, sums):
    count, width = grads.shape
    grads = lanes(grads.reshape(count, 4, width // 4).transpose(1, 0, 2), 4)
    parts = [jnp.concatenate([grads] * 8)]
    if pieces is not None:
        parts.append(lanes(pieces, 32))
    if sums:
        sums = lanes(jnp.concatenate(sums, axis=1), 1)
        parts.append(jnp.broadcast_to(sums, (32,) + sums.shape[1:]))
    return lax.all_to_all(jnp.concatenate(parts, axis=1), AXES, 0, 0, tiled=True)


def taken_apart(got, count, width):
    rows = count * width // 128
    return got[:, :rows].reshape(32 * count, width), got[:, rows:].reshape(32, -1)


def row_body(
    block_input,
    segment_ids,
    conditioning,
    w_qkv,
    qv_bias,
    w_out,
    out_bias,
    w_fc1,
    fc1_bias,
    w_fc2,
    fc2_bias,
    w_ada,
    ada_bias,
    cotangent,
):
    dp_rank, tp_rank = lax.axis_index("dp"), lax.axis_index("tp")
    core, chip = tp_rank & 1, tp_rank >> 1
    d = block_input.shape[2]
    e, ff, mod_dev = w_qkv.shape[2], w_fc1.shape[1], w_ada.shape[1]
    flips = jnp.arange(8, dtype=jnp.int32) ^ dp_rank
    place = (flips & 1) * 4 + (flips >> 1)
    att_shard = jnp.concatenate([w_qkv[0], w_qkv[1], w_qkv[2], w_out.T], axis=1)
    mlp_shard = jnp.concatenate([w_fc1, w_fc2.T], axis=1)
    near_att = lax.all_gather(att_shard, "dp", axis=0, tiled=True)
    x = Row(block_input, core).whole()
    g_row = Row(cotangent, core)
    seg = lax.dynamic_slice(segment_ids, (core, chip * PACK), (1, PACK))[0]
    seg_col = jnp.broadcast_to(seg[:, None], (PACK, 128))
    seg_row = jnp.broadcast_to(seg[None, :], (8, PACK))
    tiles = seg.reshape(-1, QT)
    lo = jnp.sum((tiles[None, :, -1] < tiles[:, None, 0]).astype(jnp.int32), axis=1)
    hi = jnp.sum((tiles[None, :, 0] <= tiles[:, None, -1]).astype(jnp.int32), axis=1)
    small = seg.reshape(-1, ET)
    first, last = small[:, 0], small[:, -1]
    lifted = smooth_gate(conditioning.astype(f32)).astype(bf16).reshape(-1, 8, w_ada.shape[0])
    (lifted,) = tie([lifted.transpose(1, 0, 2)], (att_shard,))
    lifted = lax.all_to_all(lifted, "dp", 0, 0)
    lifted = lifted.reshape(8, 2, 2, IMG_ROW, -1).transpose(0, 2, 1, 3, 4).reshape(32 * IMG_ROW, -1)
    mod_part = dot(lifted, w_ada).reshape(32, IMG_ROW, mod_dev)
    (mlp_shard,) = tie([mlp_shard], (mod_part,))
    peer_shard = across(mlp_shard, CHIP)
    qkv_bias = jnp.stack([qv_bias[0], jnp.zeros_like(qv_bias[0]), qv_bias[1]]).astype(f32)
    qkv_bias = [
        lax.dynamic_slice_in_dim(qkv_bias, (tp_rank ^ k) * e, e, 1).reshape(1, 3 * e)
        for k in range(4)
    ]
    fc1_part = [
        lax.dynamic_slice_in_dim(fc1_bias.astype(f32)[None], (tp_rank ^ k) * ff, ff, 1)
        for k in range(4)
    ]
    out_bias_row, fc2_bias_row = out_bias.astype(f32)[None], fc2_bias.astype(f32)[None]
    ready = (x, seg_col, seg_row, lo, hi, first, last, g_row.own, out_bias_row, fc2_bias_row)
    ready += tuple(qkv_bias) + tuple(fc1_part)
    (mod_part,) = tie([lax.all_to_all(mod_part, AXES, 0, 0)], ready)
    mod_part = mod_part.reshape(8, 4, IMG_ROW, mod_dev)
    modulation = jnp.sum(mod_part, axis=0).transpose(1, 0, 2).reshape(IMG_ROW, -1)
    modulation = modulation + ada_bias.astype(f32)
    (peer_shard,) = tie([peer_shard], (modulation,))
    far_w = lax.all_gather(peer_shard, "dp", axis=0, tiled=True)
    near_w = lax.all_gather(mlp_shard, "dp", axis=0, tiled=True)
    row_f, row_b = ((PACK, d), f32), ((PACK, d), bf16)
    turned = ((d, PACK), bf16)
    a, a_t = by_rows(
        enter_body,
        6,
        (),
        [("t", x), ("w", modulation), ("t", seg_col)],
        [("t", *row_b), ("T", *turned)],
        waits=(peer_shard,),
    )
    kept = {}

    def forward(k, waits):
        kept[k] = attend_fwd(a, att_w[k], qkv_bias[k], lo, hi, seg_col, seg_row, waits)
        return (kept[k][2],)

    (near_att,) = tie([near_att], (modulation,))
    att_w = [(v, 0) for v in (near_att, across(near_att, CORE), across(near_att, CHIP))]
    after = forward(1, forward(0, ()))
    (g_row.got,) = tie([g_row.got], after)
    g = g_row.whole()
    bg2, bg2_t, fc2_sum = by_rows(
        branch_body,
        6,
        (),
        [("t", g), ("w", modulation), ("t", seg_col)],
        [("t", *row_b), ("T", *turned), ("w", (1, d), f32)],
        waits=after,
    )
    (far_att,) = tie([att_w[2][0]], (fc2_sum,))
    att_w[2:] = [(far_att, 0), (across(far_att, CORE), 0)]
    after = forward(2, after)
    (far_w,) = tie([far_w], after)
    after = forward(3, after + (far_w,))
    partner_w = across(far_w, CORE)
    hidden, branch1, m, m_t = by_rows(
        middle_body,
        12,
        (),
        [("t", x)]
        + [("t", kept[k][3]) for k in range(4)]
        + [("w", modulation), ("t", seg_col), ("w", out_bias_row)],
        [("t", *row_f), ("t", *row_f), ("t", *row_b), ("T", *turned)],
    )
    done = {}
    def halves(w):
        return ((w, 0), (w, 1))

    done[3] = mlp_whole(m, bg2, m_t, bg2_t, halves(partner_w), fc1_part[3])
    init = across(done[3][3], CORE)
    done[2] = mlp_first(m, bg2, halves(far_w), fc1_part[2], (done[3][2],))
    (near_w,) = tie([near_w], (done[2][2],))
    partner_w = across(near_w, CORE)
    grad = mlp_second(m_t, bg2_t, *done[2][3:], init, (near_w,))
    far_sum = lax.psum_scatter(grad, "dp", scatter_dimension=0, tiled=True)
    done[1] = mlp_whole(m, bg2, m_t, bg2_t, halves(partner_w), fc1_part[1], (grad,))
    init = across(done[1][3], CORE)
    done[0] = mlp_first(m, bg2, halves(near_w), fc1_part[0], (done[1][2],))
    grad = mlp_second(m_t, bg2_t, *done[0][3:], init)
    near_sum = lax.psum_scatter(grad, "dp", scatter_dimension=0, tiled=True)
    block_output, hidden_grad, bg1, bg1_t, out_sum, img_late = by_rows(
        turn_body,
        5,
        (first, last),
        [("t", hidden), ("t", branch1), ("t", g)]
        + [("t", done[k][0]) for k in range(4)]
        + [("t", done[k][1]) for k in range(4)]
        + [("w", modulation), ("t", seg_col), ("w", fc2_bias_row)],
        [("t", *row_b), ("t", *row_f), ("t", *row_b), ("T", *turned), ("w", (1, d), f32), ("w", (IMG_ROW, 4 * d), f32)],
        waits=(grad,),
    )
    fc1_sum = jnp.zeros((1, 4 * ff), f32)
    for k in range(4):
        fc1_sum = lax.dynamic_update_slice_in_dim(fc1_sum, done[k][2], (tp_rank ^ k) * ff, 1)
    late = jnp.concatenate([jnp.zeros((IMG_ROW, 2 * d), f32), img_late], axis=1)
    late_sums = [jnp.sum(img_late, axis=0, keepdims=True), fc1_sum, fc2_sum, out_sum]
    late_sums = jnp.concatenate(late_sums, axis=1).reshape(32, -1)
    late = to_owners(late, late_sums, [])
    back = {}

    def backward(k, init, waits, parts=()):
        qkv, att, lse, _ = kept[k]
        back[k] = attend_bwd(
            qkv, att, bg1, bg1_t, a_t, att_w[k], lse, lo, hi, seg_col, seg_row, place, init, parts, waits
        )
        return (back[k][1],)

    block_output = trade_back(block_output, core)
    after = backward(1, None, ())
    init = across(back[1][2], CORE)
    (block_output,) = tie([block_output], after)
    after = backward(3, None, after + (block_output, far_sum))
    init, last_init = across(back[3][2], CORE), init
    after = backward(2, init, after, (4 * e,))
    (late,) = tie([late], after)
    late_grads, late_sums = taken_apart(late, IMG_ROW, mod_dev)
    far = Scatter(*back[2][2:])
    far_peer = across(far_sum, CHIP)
    after = backward(0, last_init, after, (4 * e,))
    far.got, far_peer = tie([far.got, far_peer], after)
    far.turn()
    near = Scatter(*back[0][2:])
    a_grad = back_to_input([back[k][0] for k in range(4)], att_w, (far.low,))
    (near.got,) = tie([near.got], (a_grad,))
    near.turn()
    input_grad, img_early = by_rows(
        leave_body,
        1,
        (first, last),
        [("t", x), ("t", hidden_grad), ("t", a_grad), ("w", modulation), ("t", seg_col)],
        [("t", *row_b), ("w", (IMG_ROW, 2 * d), f32)],
        waits=(near.low, near_sum),
    )
    far.got = tie(far.got, (img_early,))
    far_att = across(far.total().astype(bf16), CHIP)
    att_total = near.total() + far_att.astype(f32)
    near_sum = near_sum.astype(f32)
    fc1_grad = near_sum[:, :ff]
    fc2_grad = near_sum[:, ff:]
    far_peer = far_peer.astype(f32)
    fc1_grad, fc2_grad = fc1_grad + far_peer[:, :ff], fc2_grad + far_peer[:, ff:]
    qv_sum = jnp.zeros((2, 4 * e), f32)
    for k in range(4):
        grads = back[k][1].reshape(3, e)
        qv_sum = lax.dynamic_update_slice_in_dim(
            qv_sum, jnp.stack([grads[0], grads[2]]), (tp_rank ^ k) * e, 1
        )
    early = jnp.concatenate([img_early, jnp.zeros((IMG_ROW, 4 * d), f32)], axis=1)
    late_sums = jnp.sum(late_sums.astype(f32), axis=0, keepdims=True)
    early_sums = [late_sums, jnp.sum(img_early, axis=0, keepdims=True), qv_sum.reshape(1, -1)]
    early = to_owners(early, None, early_sums)
    early_grads, early_sums = taken_apart(early, IMG_ROW, mod_dev)
    share = late_sums.shape[1]
    used = (5 * d + d + 4 * ff) // 32
    late_sums = early_sums[:, :used].astype(f32).reshape(-1)
    late_bias, fc1_total, fc2_total, out_total = jnp.split(
        late_sums, [4 * d, 4 * d + 4 * ff, 5 * d + 4 * ff]
    )
    early_sums = jnp.sum(early_sums[:, share : share + 2 * d + 8 * e].astype(f32), axis=0)
    early_bias, qv_total = jnp.split(early_sums, [2 * d])
    qv_total = qv_total.reshape(2, -1)
    ada_total = jnp.concatenate([early_bias, late_bias])
    mod_grad = late_grads.astype(f32) + early_grads.astype(f32)
    ada_grad = lax.dot_general(
        lifted.astype(f32), mod_grad, (((0,), (0,)), ((), ())), precision=highest
    )
    return (
        block_output,
        trade_back(input_grad, core),
        jnp.stack([att_total[:, i * e : (i + 1) * e] for i in range(3)]),
        qv_total,
        att_total[:, 3 * e :].T,
        out_total,
        fc1_grad,
        fc1_total,
        fc2_grad.T,
        fc2_total,
        ada_grad,
        ada_total,
    )


def body(*arrays):
    block_input, w_qkv, w_fc1 = arrays[0], arrays[3], arrays[7]
    micro, tokens, width = block_input.shape
    heads_dev, rows = w_qkv.shape[2], w_fc1.shape[0]
    if (
        lax.axis_size("dp") == 8
        and lax.axis_size("tp") == 4
        and micro == 2
        and micro * tokens == PACK
        and rows == ROWS
        and rows * 8 == width
        and heads_dev * 4 == width
        and w_fc1.shape[1] % 384 == 0
    ):
        return row_body(*arrays)
    return general_body(*arrays)


def solution(mesh):
    placed = (
        P(None, ("dp", "tp"), None),
        P(None, "dp"),
        P(None, "dp", None),
        P(None, "dp", "tp"),
        P(),
        P("tp", "dp"),
        P(),
        P("dp", "tp"),
        P(),
        P("tp", "dp"),
        P(),
        P("dp", "tp"),
        P(),
        P(None, ("dp", "tp"), None),
    )
    return jax.shard_map(
        body,
        mesh=mesh,
        in_specs=placed,
        out_specs=(
            P(None, ("dp", "tp"), None),
            P(None, ("dp", "tp"), None),
            P(None, "dp", "tp"),
            P(),
            P("tp", "dp"),
            P(),
            P("dp", "tp"),
            P(),
            P("tp", "dp"),
            P(),
            P("dp", "tp"),
            P(),
        ),
        check_vma=False,
    )
```

```python
import math

import jax
import jax.numpy as jnp
from jax import lax
from jax.experimental import pallas as pl
from jax.experimental.pallas import tpu as pltpu
from jax.sharding import PartitionSpec as P

HD = 72
PACK = 1024
IMG_ROW = 4


highest = lax.Precision.HIGHEST
epsilon = 1e-06
masked_score = -1e30


def layer_norm(values):
    centred = values - jnp.mean(values, axis=-1, keepdims=True)
    return centred * lax.rsqrt(jnp.mean(centred * centred, axis=-1, keepdims=True) + epsilon)


def gelu_tanh(values):
    return (
        0.5
        * values
        * (1.0 + jnp.tanh(0.7978845608028654 * (values + 0.044715 * values * values * values)))
    )


def smooth_gate(values):
    return values / (1.0 + jnp.exp(-values))


def to_blocks(values, local_heads):
    shaped = values.reshape(values.shape[0] // PACK, PACK, local_heads, HD)
    return shaped.transpose(0, 2, 1, 3).reshape(-1, PACK, HD)


def from_blocks(blocks, local_heads):
    shaped = blocks.reshape(-1, local_heads, PACK, HD).transpose(0, 2, 1, 3)
    return shaped.reshape(-1, local_heads * HD)


def block_segments(segment_group, local_heads):
    shaped = segment_group.reshape(-1, 1, PACK)
    return jnp.broadcast_to(shaped, (shaped.shape[0], local_heads, PACK)).reshape(-1, PACK)


def project_heads(activations, full_qkv, bias_pair):
    projected = jnp.einsum("gd,cde->cge", activations, full_qkv, preferred_element_type=jnp.float32)
    bias_rows = jnp.stack([bias_pair[0], jnp.zeros_like(bias_pair[0]), bias_pair[1]])
    return (projected + bias_rows[:, None, :]).astype(jnp.bfloat16)


def masked_scores(query_rows, key_rows, segment_row):
    raw_scores = lax.dot_general(
        query_rows, key_rows, (((1,), (1,)), ((), ())), preferred_element_type=jnp.float32
    ) / math.sqrt(HD)
    same_image = segment_row[:, None] == segment_row[None, :]
    return (same_image, jnp.where(same_image, raw_scores, masked_score))


def attend_forward(block_items):
    query_rows, key_rows, value_rows, segment_row = block_items
    same_image, scores = masked_scores(query_rows, key_rows, segment_row)
    row_max = jnp.max(scores, axis=-1, keepdims=True)
    exponents = jnp.exp(scores - row_max)
    row_sums = jnp.sum(exponents, axis=-1, keepdims=True)
    probs_low = (exponents / row_sums).astype(jnp.bfloat16)
    attended = jnp.dot(probs_low, value_rows, preferred_element_type=jnp.float32).astype(
        jnp.bfloat16
    )
    return (attended, (row_max + jnp.log(row_sums))[:, 0])


def attend_backward(block_items):
    query_rows, key_rows, value_rows, segment_row, log_total, attended_grad = block_items
    same_image, scores = masked_scores(query_rows, key_rows, segment_row)
    attn_probs = jnp.where(same_image, jnp.exp(scores - log_total[:, None]), 0.0)
    value_grad = lax.dot_general(
        attn_probs.astype(jnp.bfloat16),
        attended_grad,
        (((0,), (0,)), ((), ())),
        preferred_element_type=jnp.float32,
    )
    probs_grad = lax.dot_general(
        attended_grad, value_rows, (((1,), (1,)), ((), ())), preferred_element_type=jnp.float32
    )
    centred = probs_grad - jnp.sum(attn_probs * probs_grad, axis=-1, keepdims=True)
    scores_grad = (attn_probs * centred).astype(jnp.bfloat16)
    query_grad = jnp.dot(scores_grad, key_rows, preferred_element_type=jnp.float32) / math.sqrt(HD)
    key_grad = lax.dot_general(
        scores_grad, query_rows, (((0,), (0,)), ((), ())), preferred_element_type=jnp.float32
    ) / math.sqrt(HD)
    return (
        query_grad.astype(jnp.bfloat16),
        key_grad.astype(jnp.bfloat16),
        value_grad.astype(jnp.bfloat16),
    )


def general_body(
    block_input,
    segment_ids,
    conditioning,
    w_qkv,
    qv_bias,
    w_out,
    out_bias,
    w_fc1,
    fc1_bias,
    w_fc2,
    fc2_bias,
    w_ada,
    ada_bias,
    cotangent,
):
    micro_count, tok_dev, model_width = block_input.shape
    tp_size = lax.axis_size("tp")
    tp_rank = lax.axis_index("tp")
    heads_dev = w_qkv.shape[2]
    hidden_dev = w_fc1.shape[1]
    mod_dev = w_ada.shape[1]
    cond_width = conditioning.shape[2]
    images = conditioning.shape[1]
    local_heads = heads_dev // HD
    qv_local = lax.dynamic_slice_in_dim(
        qv_bias.astype(jnp.float32), tp_rank * heads_dev, heads_dev, 1
    )
    fc1_local = lax.dynamic_slice_in_dim(
        fc1_bias.astype(jnp.float32), tp_rank * hidden_dev, hidden_dev, 0
    )
    ada_local = lax.dynamic_slice_in_dim(
        ada_bias.astype(jnp.float32), tp_rank * mod_dev, mod_dev, 0
    )
    out_bias_f = out_bias.astype(jnp.float32)
    fc2_bias_f = fc2_bias.astype(jnp.float32)
    positions = tp_rank * tok_dev + jnp.arange(tok_dev, dtype=jnp.int32)
    grad_qkv = jnp.zeros((3, model_width, heads_dev), jnp.float32)
    grad_out_w = jnp.zeros((heads_dev, model_width), jnp.float32)
    grad_fc1 = jnp.zeros((model_width, hidden_dev), jnp.float32)
    grad_fc2 = jnp.zeros((hidden_dev, model_width), jnp.float32)
    grad_ada = jnp.zeros((cond_width, mod_dev), jnp.float32)
    sum_qv = jnp.zeros((2, heads_dev), jnp.float32)
    sum_out_bias = jnp.zeros((model_width,), jnp.float32)
    sum_fc1 = jnp.zeros((hidden_dev,), jnp.float32)
    sum_fc2 = jnp.zeros((model_width,), jnp.float32)
    sum_ada = jnp.zeros((mod_dev,), jnp.float32)
    outputs = []
    input_grads = []
    for micro_step in range(micro_count):
        full_qkv, full_out, full_fc1, full_fc2, full_ada = (
            lax.all_gather(w_qkv, "dp", axis=1, tiled=True),
            lax.all_gather(w_out, "dp", axis=1, tiled=True),
            lax.all_gather(w_fc1, "dp", axis=0, tiled=True),
            lax.all_gather(w_fc2, "dp", axis=1, tiled=True),
            lax.all_gather(w_ada, "dp", axis=0, tiled=True),
        )
        lifted = smooth_gate(conditioning[micro_step].astype(jnp.float32)).astype(jnp.bfloat16)
        mod_part = jnp.dot(lifted, full_ada, preferred_element_type=jnp.float32) + ada_local
        modulation = lax.all_gather(mod_part, "tp", axis=1, tiled=True)
        segment_group = segment_ids[micro_step]
        segment_local = lax.dynamic_slice_in_dim(segment_group, tp_rank * tok_dev, tok_dev, 0)
        image_index = positions // PACK * IMG_ROW + segment_local
        onehot = (image_index[:, None] == jnp.arange(images, dtype=jnp.int32)[None, :]).astype(
            jnp.float32
        )
        token_mod = jnp.dot(onehot, modulation, precision=highest)
        shift_one, scale_one, gate_one, shift_two, scale_two, gate_two = jnp.split(
            token_mod, 6, axis=1
        )
        inputs = block_input[micro_step].astype(jnp.float32)
        normed_one = layer_norm(inputs)
        attn_in = (normed_one * (1.0 + scale_one) + shift_one).astype(jnp.bfloat16)
        attn_full = lax.all_gather(attn_in, "tp", axis=0, tiled=True)
        projected = project_heads(attn_full, full_qkv, qv_local)
        segment_blocks = block_segments(segment_group, local_heads)
        attended_blocks, log_totals = lax.map(
            attend_forward,
            (
                to_blocks(projected[0], local_heads),
                to_blocks(projected[1], local_heads),
                to_blocks(projected[2], local_heads),
                segment_blocks,
            ),
        )
        attended = from_blocks(attended_blocks, local_heads)
        branch_one = lax.psum_scatter(
            jnp.dot(attended, full_out, preferred_element_type=jnp.float32).astype(jnp.bfloat16),
            "tp",
            scatter_dimension=0,
            tiled=True,
        ).astype(jnp.float32)
        hidden = inputs + gate_one * (branch_one + out_bias_f)
        normed_two = layer_norm(hidden)
        mlp_in = (normed_two * (1.0 + scale_two) + shift_two).astype(jnp.bfloat16)
        mlp_full = lax.all_gather(mlp_in, "tp", axis=0, tiled=True)
        pre_act = jnp.dot(mlp_full, full_fc1, preferred_element_type=jnp.float32) + fc1_local
        activated = gelu_tanh(pre_act).astype(jnp.bfloat16)
        branch_two = lax.psum_scatter(
            jnp.dot(activated, full_fc2, preferred_element_type=jnp.float32).astype(jnp.bfloat16),
            "tp",
            scatter_dimension=0,
            tiled=True,
        ).astype(jnp.float32)
        outputs.append((hidden + gate_two * (branch_two + fc2_bias_f)).astype(jnp.bfloat16))
        grad_y = cotangent[micro_step].astype(jnp.float32)
        sum_fc2 = sum_fc2 + jnp.sum(gate_two * grad_y, axis=0)
        grad_gate_two = grad_y * (branch_two + fc2_bias_f)
        grad_branch_two = (gate_two * grad_y).astype(jnp.bfloat16)
        grad_two_full = lax.all_gather(grad_branch_two, "tp", axis=0, tiled=True)
        attn_back, mlp_back = (
            lax.all_gather(attn_in, "tp", axis=0, tiled=True),
            lax.all_gather(mlp_in, "tp", axis=0, tiled=True),
        )
        proj_back = project_heads(attn_back, full_qkv, qv_local)
        pre_back = jnp.dot(mlp_back, full_fc1, preferred_element_type=jnp.float32) + fc1_local
        act_back, gelu_pull = jax.vjp(gelu_tanh, pre_back)
        grad_fc2 = grad_fc2 + lax.dot_general(
            act_back.astype(jnp.bfloat16),
            grad_two_full,
            (((0,), (0,)), ((), ())),
            preferred_element_type=jnp.float32,
        )
        grad_act = lax.dot_general(
            grad_two_full, full_fc2, (((1,), (1,)), ((), ())), preferred_element_type=jnp.float32
        )
        grad_pre = gelu_pull(grad_act)[0].astype(jnp.bfloat16)
        sum_fc1 = sum_fc1 + jnp.sum(grad_pre.astype(jnp.float32), axis=0)
        grad_fc1 = grad_fc1 + lax.dot_general(
            mlp_back, grad_pre, (((0,), (0,)), ((), ())), preferred_element_type=jnp.float32
        )
        grad_mlp_in = lax.psum_scatter(
            lax.dot_general(
                grad_pre, full_fc1, (((1,), (1,)), ((), ())), preferred_element_type=jnp.float32
            ).astype(jnp.bfloat16),
            "tp",
            scatter_dimension=0,
            tiled=True,
        ).astype(jnp.float32)
        norm_two_pull = jax.vjp(layer_norm, hidden)[1]
        grad_hidden = grad_y + norm_two_pull(grad_mlp_in * (1.0 + scale_two))[0]
        sum_out_bias = sum_out_bias + jnp.sum(gate_one * grad_hidden, axis=0)
        grad_gate_one = grad_hidden * (branch_one + out_bias_f)
        grad_branch_one = (gate_one * grad_hidden).astype(jnp.bfloat16)
        grad_one_full = lax.all_gather(grad_branch_one, "tp", axis=0, tiled=True)
        grad_out_w = grad_out_w + lax.dot_general(
            attended, grad_one_full, (((0,), (0,)), ((), ())), preferred_element_type=jnp.float32
        )
        grad_attended = lax.dot_general(
            grad_one_full, full_out, (((1,), (1,)), ((), ())), preferred_element_type=jnp.float32
        ).astype(jnp.bfloat16)
        query_blocks, key_blocks, value_blocks = lax.map(
            attend_backward,
            (
                to_blocks(proj_back[0], local_heads),
                to_blocks(proj_back[1], local_heads),
                to_blocks(proj_back[2], local_heads),
                segment_blocks,
                log_totals,
                to_blocks(grad_attended, local_heads),
            ),
        )
        grad_proj = jnp.stack(
            [
                from_blocks(query_blocks, local_heads),
                from_blocks(key_blocks, local_heads),
                from_blocks(value_blocks, local_heads),
            ]
        )
        sum_qv = sum_qv + jnp.stack(
            [
                jnp.sum(grad_proj[0].astype(jnp.float32), axis=0),
                jnp.sum(grad_proj[2].astype(jnp.float32), axis=0),
            ]
        )
        grad_qkv = grad_qkv + jnp.einsum(
            "gd,cge->cde", attn_back, grad_proj, preferred_element_type=jnp.float32
        )
        grad_attn_in = lax.psum_scatter(
            jnp.einsum(
                "cge,cde->gd", grad_proj, full_qkv, preferred_element_type=jnp.float32
            ).astype(jnp.bfloat16),
            "tp",
            scatter_dimension=0,
            tiled=True,
        ).astype(jnp.float32)
        norm_one_pull = jax.vjp(layer_norm, inputs)[1]
        input_grads.append(
            (grad_hidden + norm_one_pull(grad_attn_in * (1.0 + scale_one))[0]).astype(jnp.bfloat16)
        )
        grad_token_mod = jnp.concatenate(
            [
                grad_attn_in,
                grad_attn_in * normed_one,
                grad_gate_one,
                grad_mlp_in,
                grad_mlp_in * normed_two,
                grad_gate_two,
            ],
            axis=1,
        )
        mod_grad_part = lax.dot_general(
            onehot, grad_token_mod, (((0,), (0,)), ((), ())), precision=highest
        )
        grad_mod = lax.psum_scatter(
            mod_grad_part.astype(jnp.bfloat16), "tp", scatter_dimension=1, tiled=True
        ).astype(jnp.float32)
        sum_ada = sum_ada + jnp.sum(grad_mod, axis=0)
        grad_ada = grad_ada + lax.dot_general(
            lifted.astype(jnp.float32), grad_mod, (((0,), (0,)), ((), ())), precision=highest
        )
    qkv_shard, out_shard, fc1_shard, fc2_shard, ada_shard = (
        lax.psum_scatter(
            grad_qkv.astype(jnp.bfloat16), "dp", scatter_dimension=1, tiled=True
        ).astype(jnp.float32),
        lax.psum_scatter(
            grad_out_w.astype(jnp.bfloat16), "dp", scatter_dimension=1, tiled=True
        ).astype(jnp.float32),
        lax.psum_scatter(
            grad_fc1.astype(jnp.bfloat16), "dp", scatter_dimension=0, tiled=True
        ).astype(jnp.float32),
        lax.psum_scatter(
            grad_fc2.astype(jnp.bfloat16), "dp", scatter_dimension=1, tiled=True
        ).astype(jnp.float32),
        lax.psum_scatter(
            grad_ada.astype(jnp.bfloat16), "dp", scatter_dimension=0, tiled=True
        ).astype(jnp.float32),
    )
    qv_full = lax.dynamic_update_slice_in_dim(
        jnp.zeros((2, model_width), jnp.float32), sum_qv, tp_rank * heads_dev, 1
    )
    fc1_full = lax.dynamic_update_slice_in_dim(
        jnp.zeros((hidden_dev * tp_size,), jnp.float32), sum_fc1, tp_rank * hidden_dev, 0
    )
    ada_full = lax.dynamic_update_slice_in_dim(
        jnp.zeros((mod_dev * tp_size,), jnp.float32), sum_ada, tp_rank * mod_dev, 0
    )
    qv_total, out_total, fc1_total, fc2_total, ada_total = lax.psum(
        (qv_full, sum_out_bias, fc1_full, sum_fc2, ada_full), ("dp", "tp")
    )
    return (
        jnp.stack(outputs),
        jnp.stack(input_grads),
        qkv_shard,
        qv_total,
        out_shard,
        out_total,
        fc1_shard,
        fc1_total,
        fc2_shard,
        fc2_total,
        ada_shard,
        ada_total,
    )


f32, bf16 = jnp.float32, jnp.bfloat16
AXES = ("dp", "tp")
CORE, CHIP = 1, 2
ROWS = 144
QT = 256
ET = 128
LOG2E = 1.4426950408889634
GELU_A = 0.7978845608028654
GELU_B = 0.7978845608028654 * 0.044715
VMEM_BYTES = 56 * 2**20
NN = (((1,), (0,)), ((), ()))
NT = (((1,), (1,)), ((), ()))
SMEM_SPEC = pl.BlockSpec(memory_space=pltpu.SMEM)
VMEM_SPEC = pl.BlockSpec(memory_space=pltpu.VMEM)
ANY_SPEC = pl.BlockSpec(memory_space=pl.ANY)


def cost(micros):
    return pl.CostEstimate(flops=int(4 * micros * 1.15e9), bytes_accessed=0, transcendentals=0)


def dot(left, right, dims=NN):
    return lax.dot_general(left, right, dims, preferred_element_type=f32)


def compiler_params():
    return pltpu.CompilerParams(vmem_limit_bytes=VMEM_BYTES)


def swap(values, dp_mask, tp_mask):
    pairs = [(d * 4 + t, (d ^ dp_mask) * 4 + (t ^ tp_mask)) for d in range(8) for t in range(4)]
    return lax.ppermute(values, AXES, pairs)


def across(values, tp_mask):
    return swap(values, 0, tp_mask)


def tie(values, after):
    count = len(values)
    return pl.pallas_call(
        lambda *refs: None,
        in_specs=[ANY_SPEC] * (count + len(after)),
        out_specs=[ANY_SPEC] * count,
        out_shape=[jax.ShapeDtypeStruct(v.shape, v.dtype) for v in values],
        input_output_aliases={i: i for i in range(count)},
    )(*values, *after)


def piece_copies(stage, place_ref, parts, outs, sem, start):
    for q in range(8):
        column = 0
        for i, width in enumerate(parts):
            source = stage.at[pl.ds(q * ROWS, ROWS), pl.ds(column, width)]
            column += width
            low, high, done = outs[2 * i], outs[2 * i + 1], sem.at[len(parts) * q + i]
            if not start:
                pltpu.make_async_copy(source, low.at[0], done).wait()
                continue
            spot = place_ref[q]

            @pl.when(spot < 4)
            def _():
                pltpu.make_async_copy(source, low.at[spot], done).start()

            @pl.when(spot >= 4)
            def _():
                pltpu.make_async_copy(source, high.at[spot - 4], done).start()


def mlp_tokens(x_ref, g_ref, w1_ref, w2_ref, b_ref, b2_ref, dm_ref, db_ref):
    pre = dot(x_ref[...], w1_ref[...]) + b_ref[...]
    act_grad = dot(g_ref[...], w2_ref[...])
    square = pre * pre
    bend = jnp.tanh(pre * (GELU_A + GELU_B * square))
    half = 0.5 + 0.5 * bend
    act = (pre * half).astype(bf16)
    slope = half + pre * (half * (1.0 - bend)) * (GELU_A + (3 * GELU_B) * square)
    pre_grad = (act_grad * slope).astype(bf16)
    b2_ref[...] = dot(act, w2_ref[...], NT).astype(bf16)
    dm_ref[...] = dot(pre_grad, w1_ref[...], NT).astype(bf16)
    add_rows(db_ref, pre_grad.astype(f32))
    return act, pre_grad


def mlp_whole_body(waits, tok_steps, x_ref, g_ref, xt_ref, gt_ref, w1_ref, w2_ref, b_ref, *refs):
    b2_ref, dm_ref, db_ref, dw_ref, act_s, slope_s = refs[waits:]
    step = pl.program_id(0)
    rows = x_ref.shape[0]
    ff = w1_ref.shape[1]

    @pl.when(step < tok_steps)
    def _():
        act, pre_grad = mlp_tokens(x_ref, g_ref, w1_ref, w2_ref, b_ref, b2_ref, dm_ref, db_ref)
        here = pl.ds(pl.multiple_of(step * rows, rows), rows)
        act_s[here, :] = act
        slope_s[here, :] = pre_grad

    @pl.when(step >= tok_steps)
    def _():
        dw_ref[:, :ff] = dot(xt_ref[...], slope_s[...]).astype(bf16)
        dw_ref[:, ff:] = dot(gt_ref[...], act_s[...]).astype(bf16)


def mlp_first_body(waits, x_ref, g_ref, w1_ref, w2_ref, b_ref, *refs):
    b2_ref, dm_ref, db_ref, act_ref, slope_ref = refs[waits:]
    act, pre_grad = mlp_tokens(x_ref, g_ref, w1_ref, w2_ref, b_ref, b2_ref, dm_ref, db_ref)
    act_ref[...] = act
    slope_ref[...] = pre_grad


def mlp_second_body(waits, xt_ref, gt_ref, act_ref, slope_ref, init_ref, *refs):
    (dw_ref,) = refs[waits:]
    ff = act_ref.shape[1]
    grad1 = dot(xt_ref[...], slope_ref[...]) + init_ref[:, :ff].astype(f32)
    dw_ref[:, :ff] = grad1.astype(bf16)
    grad2 = dot(gt_ref[...], act_ref[...]) + init_ref[:, ff:].astype(f32)
    dw_ref[:, ff:] = grad2.astype(bf16)


def mlp_call(body, steps, in_specs, operands, outs, scratch, waits, micros):
    n, d = operands[0].shape
    return pl.pallas_call(
        lambda *refs: body(len(waits), *refs),
        grid=(steps,),
        in_specs=in_specs + [ANY_SPEC] * len(waits),
        out_specs=[spec for spec, _, _ in outs],
        out_shape=[jax.ShapeDtypeStruct(shape, kind) for _, shape, kind in outs],
        scratch_shapes=scratch,
        compiler_params=compiler_params(),
        cost_estimate=cost(micros),
    )(*operands, *waits)


def columns(d, ff, block):
    return pl.BlockSpec((d, ff), lambda s: (0, block), pipeline_mode=pl.Buffered(1))


def mlp_weights(d, ff, weights):
    return [columns(d, ff, block) for _, block in weights] + [
        pl.BlockSpec((1, ff), lambda s: (0, 0))
    ]


def mlp_whole(x, g, xt, gt, weights, bias, waits=(), tok_steps=4, row_steps=4):
    n, d = x.shape
    ff = bias.shape[1]
    tok_rows, dim_rows = n // tok_steps, d // row_steps
    tok = pl.BlockSpec((tok_rows, d), lambda s: (jnp.minimum(s, tok_steps - 1), 0))
    row = pl.BlockSpec((dim_rows, n), lambda s: (jnp.maximum(s - tok_steps, 0), 0))
    wide = pl.BlockSpec((dim_rows, 2 * ff), lambda s: (jnp.maximum(s - tok_steps, 0), 0))
    return mlp_call(
        lambda count, *refs: mlp_whole_body(count, tok_steps, *refs),
        tok_steps + row_steps,
        [tok, tok, row, row] + mlp_weights(d, ff, weights),
        [x, g, xt, gt, *[w for w, _ in weights], bias],
        [
            (tok, (n, d), bf16),
            (tok, (n, d), bf16),
            (pl.BlockSpec((1, ff), lambda s: (0, 0)), (1, ff), f32),
            (wide, (d, 2 * ff), bf16),
        ],
        [pltpu.VMEM((n, ff), bf16), pltpu.VMEM((n, ff), bf16)],
        waits,
        27,
    )


def mlp_first(x, g, weights, bias, waits=(), steps=4):
    n, d = x.shape
    ff = bias.shape[1]
    tok = pl.BlockSpec((n // steps, d), lambda s: (s, 0))
    hid = pl.BlockSpec((n // steps, ff), lambda s: (s, 0))
    return mlp_call(
        mlp_first_body,
        steps,
        [tok, tok] + mlp_weights(d, ff, weights),
        [x, g, *[w for w, _ in weights], bias],
        [
            (tok, (n, d), bf16),
            (tok, (n, d), bf16),
            (pl.BlockSpec((1, ff), lambda s: (0, 0)), (1, ff), f32),
            (hid, (n, ff), bf16),
            (hid, (n, ff), bf16),
        ],
        [],
        waits,
        19,
    )


def mlp_second(xt, gt, act, slope, init, waits=(), steps=4):
    d, n = xt.shape
    ff = act.shape[1]
    row = pl.BlockSpec((d // steps, n), lambda s: (s, 0))
    wide = pl.BlockSpec((d // steps, 2 * ff), lambda s: (s, 0))
    all_hid = pl.BlockSpec((n, ff), lambda s: (0, 0), pipeline_mode=pl.Buffered(1))
    return mlp_call(
        mlp_second_body,
        steps,
        [row, row, all_hid, all_hid, wide],
        [xt, gt, act, slope, init],
        [(wide, (d, 2 * ff), bf16)],
        [],
        waits,
        12,
    )[0]


def attend_fwd_body(heads, lo_ref, hi_ref, x_ref, w_ref, b_ref, sc_ref, sr_ref, *refs):
    qkv_any, att_ref, lse_ref, part_ref, qt_s, k_s, vt_s, ot_s, qkv_ref, sem = refs[-10:]
    n = x_ref.shape[0]
    e = heads * HD
    c = LOG2E / math.sqrt(HD)
    qkv = dot(x_ref[...], w_ref[:, : 3 * e]) + b_ref[...]
    qkv_ref[...] = qkv.astype(bf16)
    save = pltpu.make_async_copy(qkv_ref, qkv_any, sem.at[0])
    save.start()
    qt = qkv[:, :e].T
    vt = qkv[:, 2 * e :].T
    every = range(heads)
    for h in every:
        qt_s[h] = qt[h * HD : (h + 1) * HD].astype(bf16)
        vt_s[h] = vt[h * HD : (h + 1) * HD].astype(bf16)
        k_s[h] = qkv[:, e + h * HD : e + (h + 1) * HD].astype(bf16)

    @pl.loop(0, n // QT)
    def _(i):
        qi = pl.ds(pl.multiple_of(i * QT, QT), QT)
        seg_row = sr_ref[:1, qi]
        first = lo_ref[i]

        def attend(count):
            kk = pl.ds(pl.multiple_of(first * QT, QT), count * QT)
            same = sc_ref[kk, :1] == seg_row
            scores = [
                jnp.where(same, dot(k_s[h, kk, :], qt_s[h, :, qi]), masked_score) for h in every
            ]
            tops = [jnp.max(v, axis=0, keepdims=True) for v in scores]
            probs = [jnp.exp2((v - t) * c) for v, t in zip(scores, tops)]
            totals = [jnp.sum(p, axis=0, keepdims=True) for p in probs]
            mixed = [dot(vt_s[h, :, kk], probs[h].astype(bf16)) for h in every]
            for h in every:
                ot_s[h * HD : (h + 1) * HD, qi] = mixed[h] / totals[h]
                lse_ref[h : h + 1, qi] = tops[h] * c + jnp.log(totals[h]) * LOG2E

        for count in range(1, n // QT + 1):
            pl.when(hi_ref[i] - first == count)(lambda count=count: attend(count))

    att = ot_s[...].T.astype(bf16)
    att_ref[...] = att
    part_ref[...] = dot(att, w_ref[:, 3 * e :], NT).astype(bf16)
    save.wait()


def attend_fwd(x, w, bias, lo, hi, seg_col, seg_row, waits=()):
    n, d = x.shape
    e = bias.shape[1] // 3
    heads = e // HD
    return pl.pallas_call(
        lambda *refs: attend_fwd_body(heads, *refs),
        in_specs=[SMEM_SPEC] * 2
        + [VMEM_SPEC, columns(d, 4 * e, w[1])]
        + [VMEM_SPEC] * 3
        + [ANY_SPEC] * len(waits),
        grid=(1,),
        out_specs=[ANY_SPEC] + [VMEM_SPEC] * 3,
        out_shape=[
            jax.ShapeDtypeStruct((n, 3 * e), bf16),
            jax.ShapeDtypeStruct((n, e), bf16),
            jax.ShapeDtypeStruct((8, n), f32),
            jax.ShapeDtypeStruct((n, d), bf16),
        ],
        scratch_shapes=[
            pltpu.VMEM((heads, HD, n), bf16),
            pltpu.VMEM((heads, n, HD), bf16),
            pltpu.VMEM((heads, HD, n), bf16),
            pltpu.VMEM((e, n), f32),
            pltpu.VMEM((n, 3 * e), bf16),
            pltpu.SemaphoreType.DMA((1,)),
        ],
        compiler_params=compiler_params(),
        cost_estimate=cost(16),
    )(lo, hi, x, w[0], bias, seg_col, seg_row, *waits)


def attend_bwd_body(final, parts, waits, heads, *refs):
    (lo_ref, hi_ref, place_ref, qkv_ref, att_ref, g_ref, gt_any, xt_any, w_ref, lse_ref, sc_ref, sr_ref) = refs[:12]
    init_any = refs[12] if final else None
    refs = refs[12 + final + waits :]
    grads_any, db_ref = refs[:2]
    refs = refs[2:]
    if parts:
        count = 2 * len(parts)
        outs, (stage, sem), refs = refs[:count], refs[-2:], refs[count:-2]
    else:
        stage, refs = refs[0], refs[1:]
    if final:
        init_ref, refs = refs[-1], refs[:-1]
    qt_s, q_s, k_s, kt_s, v_s, do_s, dot_s, delta_s, dqt_s, dk_s, dv_s, xt_ref, gt_ref, grads_ref, own_sem = refs
    loads = [
        pltpu.make_async_copy(xt_any, xt_ref, own_sem.at[0]),
        pltpu.make_async_copy(gt_any, gt_ref, own_sem.at[1]),
    ]
    if final:
        loads.append(pltpu.make_async_copy(init_any, init_ref, own_sem.at[2]))
    for load in loads:
        load.start()
    n = g_ref.shape[0]
    e = heads * HD
    c = LOG2E / math.sqrt(HD)
    scale = 1.0 / math.sqrt(HD)
    every = range(heads)
    out_grad = dot(g_ref[...], w_ref[:, 3 * e :]).astype(bf16).astype(f32)
    out_grad_t = out_grad.T
    qkv = qkv_ref[...].astype(f32)
    qt = qkv[:, :e].T
    kt = qkv[:, e : 2 * e].T
    att = att_ref[...]
    products = out_grad_t * att.astype(f32).T
    for h in every:
        s = slice(h * HD, (h + 1) * HD)
        qt_s[h] = qt[s].astype(bf16)
        kt_s[h] = kt[s].astype(bf16)
        dot_s[h] = out_grad_t[s].astype(bf16)
        delta_s[h] = jnp.sum(products[s], axis=0, keepdims=True)
        q_s[h] = qkv[:, h * HD : (h + 1) * HD].astype(bf16)
        k_s[h] = qkv[:, e + h * HD : e + (h + 1) * HD].astype(bf16)
        v_s[h] = qkv[:, 2 * e + h * HD : 2 * e + (h + 1) * HD].astype(bf16)
        do_s[h] = out_grad[:, s].astype(bf16)
    dk_s[...] = jnp.zeros(dk_s.shape, f32)
    dv_s[...] = jnp.zeros(dv_s.shape, f32)

    @pl.loop(0, n // QT)
    def _(i):
        qi = pl.ds(pl.multiple_of(i * QT, QT), QT)
        seg_row = sr_ref[:1, qi]
        first = lo_ref[i]

        def attend(count):
            kk = pl.ds(pl.multiple_of(first * QT, QT), count * QT)
            same = sc_ref[kk, :1] == seg_row
            scores = [dot(k_s[h, kk, :], qt_s[h, :, qi]) for h in every]
            p_grads = [dot(v_s[h, kk, :], dot_s[h, :, qi]) for h in every]
            probs = [
                jnp.where(same, jnp.exp2(scores[h] * c - lse_ref[h : h + 1, qi]), 0.0) for h in every
            ]
            s_grads = [(probs[h] * (p_grads[h] - delta_s[h, :, qi])).astype(bf16) for h in every]
            dv = [dot(probs[h].astype(bf16), do_s[h, qi, :]) for h in every]
            dk = [dot(s_grads[h], q_s[h, qi, :]) for h in every]
            dq = [dot(kt_s[h, :, kk], s_grads[h]) for h in every]
            for h in every:
                dv_s[h, kk, :] += dv[h]
                dk_s[h, kk, :] += dk[h]
                dqt_s[h, :, qi] = dq[h]

        for count in range(1, n // QT + 1):
            pl.when(hi_ref[i] - first == count)(lambda count=count: attend(count))

    dq = jnp.concatenate([dqt_s[h] for h in every], axis=0).T * scale
    dk = [dk_s[h] * scale for h in every]
    dv = [dv_s[h] for h in every]
    grads = jnp.concatenate([dq] + dk + dv, axis=1).astype(bf16)
    db_ref[...] = jnp.sum(grads.astype(f32), axis=0, keepdims=True)
    grads_ref[...] = grads
    save = pltpu.make_async_copy(grads_ref, grads_any, own_sem.at[3])
    save.start()
    for load in loads:
        load.wait()
    dw = jnp.concatenate([dot(xt_ref[...], grads), dot(gt_ref[...], att)], axis=1)
    if final:
        dw += init_ref[...].astype(f32)
    stage[...] = dw.astype(bf16)
    if parts:
        piece_copies(stage, place_ref, parts, outs, sem, True)
        piece_copies(stage, place_ref, parts, outs, sem, False)
    save.wait()


def attend_bwd(
    qkv, att, g, gt, xt, w, lse, lo, hi, seg_col, seg_row, place, init=None, parts=(), waits=()
):
    n, d = g.shape
    e = att.shape[1]
    heads = e // HD
    final = init is not None
    operands = [lo, hi, place, qkv, att, g, gt, xt, w[0], lse, seg_col, seg_row]
    in_specs = [SMEM_SPEC] * 3 + [VMEM_SPEC] * 3 + [ANY_SPEC] * 2
    in_specs += [columns(d, 4 * e, w[1])] + [VMEM_SPEC] * 3
    out_shape = [jax.ShapeDtypeStruct((n, 3 * e), bf16), jax.ShapeDtypeStruct((1, 3 * e), f32)]
    out_specs = [ANY_SPEC, VMEM_SPEC]
    tall, wide = (heads, n, HD), (heads, HD, n)
    scratch = [pltpu.VMEM(s, bf16) for s in (wide, tall, tall, wide, tall, tall, wide)]
    scratch += [pltpu.VMEM((heads, 1, n), f32)] + [pltpu.VMEM(s, f32) for s in (wide, tall, tall)]
    scratch += [pltpu.VMEM(s, bf16) for s in ((d, n), (d, n), (n, 3 * e))]
    scratch += [pltpu.SemaphoreType.DMA((4,))]
    if final:
        operands.append(init)
        in_specs.append(ANY_SPEC)
        scratch.append(pltpu.VMEM((d, 4 * e), bf16))
    for width in parts:
        out_shape += [jax.ShapeDtypeStruct((4, ROWS, width), bf16)] * 2
        out_specs += [ANY_SPEC] * 2
    if parts:
        scratch += [pltpu.VMEM((d, 4 * e), bf16), pltpu.SemaphoreType.DMA((8 * len(parts),))]
    else:
        out_shape.append(jax.ShapeDtypeStruct((d, 4 * e), bf16))
        out_specs.append(VMEM_SPEC)
    return pl.pallas_call(
        lambda *refs: attend_bwd_body(final, parts, len(waits), heads, *refs),
        grid=(1,),
        in_specs=in_specs + [ANY_SPEC] * len(waits),
        out_specs=out_specs,
        out_shape=out_shape,
        scratch_shapes=scratch,
        compiler_params=compiler_params(),
        cost_estimate=cost(1),
    )(*operands, *waits)


def token_rows(mod_ref, block, sc_ref):
    d = mod_ref.shape[1] // 6
    seg = sc_ref[:, :1]
    rows = mod_ref[:, block * d : (block + 1) * d]
    value = jnp.where(seg == 0, rows[0:1], rows[1:2])
    value = jnp.where(seg == 2, rows[2:3], value)
    return jnp.where(seg == 3, rows[3:4], value)


def normalize(values):
    centred = values - jnp.mean(values, axis=-1, keepdims=True)
    inverse = lax.rsqrt(jnp.mean(centred * centred, axis=-1, keepdims=True) + epsilon)
    return centred * inverse, inverse


def norm_back(normed, inverse, grad):
    mean = jnp.mean(grad, axis=-1, keepdims=True)
    along = jnp.mean(grad * normed, axis=-1, keepdims=True)
    return inverse * (grad - mean - normed * along)


def add_images(acc_ref, first_ref, last_ref, sc_ref, columns):
    step = pl.program_id(0)
    seg = sc_ref[:, :1]

    @pl.when(step == 0)
    def _():
        acc_ref[...] = jnp.zeros(acc_ref.shape, f32)

    @pl.loop(first_ref[step], last_ref[step] + 1)
    def _(image):
        mine = seg == image
        for i, values in enumerate(columns):
            d = values.shape[1]
            part = jnp.sum(jnp.where(mine, values, 0.0), axis=0, keepdims=True)
            acc_ref[pl.ds(image, 1), i * d : (i + 1) * d] += part


def add_rows(acc_ref, values):
    part = jnp.sum(values, axis=0, keepdims=True)

    @pl.when(pl.program_id(0) == 0)
    def _():
        acc_ref[...] = part

    @pl.when(pl.program_id(0) > 0)
    def _():
        acc_ref[...] += part


def enter_body(x_ref, mod_ref, sc_ref, a_ref, at_ref):
    normed, _ = normalize(x_ref[...].astype(f32))
    a = normed * (1.0 + token_rows(mod_ref, 1, sc_ref)) + token_rows(mod_ref, 0, sc_ref)
    a_ref[...] = a.astype(bf16)
    at_ref[...] = a.T.astype(bf16)


def branch_body(g_ref, mod_ref, sc_ref, bg_ref, bgt_ref, sum_ref):
    bg = token_rows(mod_ref, 5, sc_ref) * g_ref[...].astype(f32)
    bg_ref[...] = bg.astype(bf16)
    bgt_ref[...] = bg.T.astype(bf16)
    add_rows(sum_ref, bg)


def middle_body(x_ref, p0, p1, p2, p3, mod_ref, sc_ref, ob_ref, hid_ref, br_ref, m_ref, mt_ref):
    branch = p0[...].astype(f32) + p1[...].astype(f32) + p2[...].astype(f32) + p3[...].astype(f32)
    branch = branch + ob_ref[...]
    br_ref[...] = branch
    hidden = x_ref[...].astype(f32) + token_rows(mod_ref, 2, sc_ref) * branch
    hid_ref[...] = hidden
    normed, _ = normalize(hidden)
    m = normed * (1.0 + token_rows(mod_ref, 4, sc_ref)) + token_rows(mod_ref, 3, sc_ref)
    m_ref[...] = m.astype(bf16)
    mt_ref[...] = m.T.astype(bf16)


def turn_body(
    first_ref, last_ref, hid_ref, br_ref, g_ref, b0, b1, b2, b3, d0, d1, d2, d3, mod_ref, sc_ref, fb_ref,
    out_ref, hg_ref, bg_ref, bgt_ref, sum_ref, img_ref,
):
    hidden, g = hid_ref[...], g_ref[...].astype(f32)
    branch = b0[...].astype(f32) + b1[...].astype(f32) + b2[...].astype(f32) + b3[...].astype(f32)
    branch = branch + fb_ref[...]
    out_ref[...] = (hidden + token_rows(mod_ref, 5, sc_ref) * branch).astype(bf16)
    m_grad = d0[...].astype(f32) + d1[...].astype(f32) + d2[...].astype(f32) + d3[...].astype(f32)
    normed, inverse = normalize(hidden)
    hidden_grad = g + norm_back(normed, inverse, m_grad * (1.0 + token_rows(mod_ref, 4, sc_ref)))
    hg_ref[...] = hidden_grad
    bg = token_rows(mod_ref, 2, sc_ref) * hidden_grad
    bg_ref[...] = bg.astype(bf16)
    bgt_ref[...] = bg.T.astype(bf16)
    add_rows(sum_ref, bg)
    add_images(
        img_ref, first_ref, last_ref, sc_ref,
        (hidden_grad * br_ref[...], m_grad, m_grad * normed, g * branch),
    )


def back_body(q0, q1, q2, q3, w0, w1, w2, w3, *refs):
    out_ref = refs[-1]
    width = q0.shape[1]
    total = dot(q0[...], w0[:, :width], NT)
    for grads, w in ((q1, w1), (q2, w2), (q3, w3)):
        total += dot(grads[...], w[:, :width], NT)
    out_ref[...] = total


def back_to_input(grads, weights, waits, steps=4):
    n, width = grads[0].shape
    d = weights[0][0].shape[0]
    return pl.pallas_call(
        back_body,
        grid=(steps,),
        in_specs=[pl.BlockSpec((n // steps, width), lambda s: (s, 0))] * 4
        + [columns(d, width * 4 // 3, block) for _, block in weights]
        + [ANY_SPEC] * len(waits),
        out_specs=pl.BlockSpec((n // steps, d), lambda s: (s, 0)),
        out_shape=jax.ShapeDtypeStruct((n, d), f32),
        compiler_params=compiler_params(),
        cost_estimate=cost(1),
    )(*grads, *[w for w, _ in weights], *waits)


def leave_body(first_ref, last_ref, x_ref, hg_ref, ag_ref, mod_ref, sc_ref, out_ref, img_ref):
    a_grad = ag_ref[...]
    normed, inverse = normalize(x_ref[...].astype(f32))
    back = norm_back(normed, inverse, a_grad * (1.0 + token_rows(mod_ref, 1, sc_ref)))
    out_ref[...] = (hg_ref[...] + back).astype(bf16)
    add_images(img_ref, first_ref, last_ref, sc_ref, (a_grad, a_grad * normed))


def by_rows(body_fn, micros, scalars, operands, outs, waits=()):
    def spec(kind, shape):
        if kind == "t":
            return pl.BlockSpec((ET, shape[1]), lambda s: (s, 0))
        if kind == "T":
            return pl.BlockSpec((shape[0], ET), lambda s: (0, s))
        return pl.BlockSpec(shape, lambda s: (0, 0))

    n = operands[0][1].shape[0]
    own_in = len(scalars) + len(operands)

    def body(*refs):
        body_fn(*refs[:own_in], *refs[own_in + len(waits) :])

    return pl.pallas_call(
        body,
        grid=(n // ET,),
        in_specs=[SMEM_SPEC] * len(scalars)
        + [spec(k, v.shape) for k, v in operands]
        + [ANY_SPEC] * len(waits),
        out_specs=[spec(k, s) for k, s, _ in outs],
        out_shape=[jax.ShapeDtypeStruct(s, t) for _, s, t in outs],
        compiler_params=compiler_params(),
        cost_estimate=cost(micros),
    )(*scalars, *[v for _, v in operands], *waits)


class Row:
    def __init__(self, values, core):
        self.core = core
        self.own = lax.dynamic_index_in_dim(values, core, 0, keepdims=False)
        self.got = across(lax.dynamic_index_in_dim(values, 1 - core, 0, keepdims=False), CORE)

    def whole(self):
        first = self.core == 0
        return jnp.concatenate(
            [jnp.where(first, self.own, self.got), jnp.where(first, self.got, self.own)]
        )


def trade_back(row, core):
    half = row.shape[0] // 2
    own = lax.dynamic_slice_in_dim(row, core * half, half, 0)
    got = across(lax.dynamic_slice_in_dim(row, (1 - core) * half, half, 0), CORE)
    first = core == 0
    return jnp.stack([jnp.where(first, own, got), jnp.where(first, got, own)])


def add_pieces(*terms):
    return sum(t.astype(f32) for t in terms)


class Scatter:
    def __init__(self, low, high):
        self.low, self.got = low, swap(high, 1, 0)

    def turn(self):
        sums = [add_pieces(self.low[i], self.got[i]) for i in range(4)]
        self.low = sums[0]
        self.got = [swap(sums[i].astype(bf16), 2 * i, 0) for i in range(1, 4)]

    def total(self):
        return add_pieces(self.low, *self.got)


def lanes(values, rows):
    values = values.reshape(rows, -1)
    spare = -values.shape[1] % 128
    return jnp.pad(values.astype(bf16), ((0, 0), (0, spare))).reshape(rows, -1, 128)


def to_owners(grads, pieces, sums):
    count, width = grads.shape
    grads = lanes(grads.reshape(count, 4, width // 4).transpose(1, 0, 2), 4)
    parts = [jnp.concatenate([grads] * 8)]
    if pieces is not None:
        parts.append(lanes(pieces, 32))
    if sums:
        sums = lanes(jnp.concatenate(sums, axis=1), 1)
        parts.append(jnp.broadcast_to(sums, (32,) + sums.shape[1:]))
    return lax.all_to_all(jnp.concatenate(parts, axis=1), AXES, 0, 0, tiled=True)


def taken_apart(got, count, width):
    rows = count * width // 128
    return got[:, :rows].reshape(32 * count, width), got[:, rows:].reshape(32, -1)


def row_body(
    block_input,
    segment_ids,
    conditioning,
    w_qkv,
    qv_bias,
    w_out,
    out_bias,
    w_fc1,
    fc1_bias,
    w_fc2,
    fc2_bias,
    w_ada,
    ada_bias,
    cotangent,
):
    dp_rank, tp_rank = lax.axis_index("dp"), lax.axis_index("tp")
    core, chip = tp_rank & 1, tp_rank >> 1
    d = block_input.shape[2]
    e, ff, mod_dev = w_qkv.shape[2], w_fc1.shape[1], w_ada.shape[1]
    flips = jnp.arange(8, dtype=jnp.int32) ^ dp_rank
    place = (flips & 1) * 4 + (flips >> 1)
    att_shard = jnp.concatenate([w_qkv[0], w_qkv[1], w_qkv[2], w_out.T], axis=1)
    mlp_shard = jnp.concatenate([w_fc1, w_fc2.T], axis=1)
    near_att = lax.all_gather(att_shard, "dp", axis=0, tiled=True)
    x = Row(block_input, core).whole()
    g_row = Row(cotangent, core)
    seg = lax.dynamic_slice(segment_ids, (core, chip * PACK), (1, PACK))[0]
    seg_col = jnp.broadcast_to(seg[:, None], (PACK, 128))
    seg_row = jnp.broadcast_to(seg[None, :], (8, PACK))
    tiles = seg.reshape(-1, QT)
    lo = jnp.sum((tiles[None, :, -1] < tiles[:, None, 0]).astype(jnp.int32), axis=1)
    hi = jnp.sum((tiles[None, :, 0] <= tiles[:, None, -1]).astype(jnp.int32), axis=1)
    small = seg.reshape(-1, ET)
    first, last = small[:, 0], small[:, -1]
    lifted = smooth_gate(conditioning.astype(f32)).astype(bf16).reshape(-1, 8, w_ada.shape[0])
    (lifted,) = tie([lifted.transpose(1, 0, 2)], (att_shard,))
    lifted = lax.all_to_all(lifted, "dp", 0, 0)
    lifted = lifted.reshape(8, 2, 2, IMG_ROW, -1).transpose(0, 2, 1, 3, 4).reshape(32 * IMG_ROW, -1)
    mod_part = dot(lifted, w_ada).reshape(32, IMG_ROW, mod_dev)
    (mlp_shard,) = tie([mlp_shard], (mod_part,))
    peer_shard = across(mlp_shard, CHIP)
    qkv_bias = jnp.stack([qv_bias[0], jnp.zeros_like(qv_bias[0]), qv_bias[1]]).astype(f32)
    qkv_bias = [
        lax.dynamic_slice_in_dim(qkv_bias, (tp_rank ^ k) * e, e, 1).reshape(1, 3 * e)
        for k in range(4)
    ]
    fc1_part = [
        lax.dynamic_slice_in_dim(fc1_bias.astype(f32)[None], (tp_rank ^ k) * ff, ff, 1)
        for k in range(4)
    ]
    out_bias_row, fc2_bias_row = out_bias.astype(f32)[None], fc2_bias.astype(f32)[None]
    ready = (x, seg_col, seg_row, lo, hi, first, last, g_row.own, out_bias_row, fc2_bias_row)
    ready += tuple(qkv_bias) + tuple(fc1_part)
    (mod_part,) = tie([lax.all_to_all(mod_part, AXES, 0, 0)], ready)
    mod_part = mod_part.reshape(8, 4, IMG_ROW, mod_dev)
    modulation = jnp.sum(mod_part, axis=0).transpose(1, 0, 2).reshape(IMG_ROW, -1)
    modulation = modulation + ada_bias.astype(f32)
    (peer_shard,) = tie([peer_shard], (modulation,))
    far_w = lax.all_gather(peer_shard, "dp", axis=0, tiled=True)
    near_w = lax.all_gather(mlp_shard, "dp", axis=0, tiled=True)
    row_f, row_b = ((PACK, d), f32), ((PACK, d), bf16)
    turned = ((d, PACK), bf16)
    a, a_t = by_rows(
        enter_body,
        6,
        (),
        [("t", x), ("w", modulation), ("t", seg_col)],
        [("t", *row_b), ("T", *turned)],
        waits=(peer_shard,),
    )
    kept = {}

    def forward(k, waits):
        kept[k] = attend_fwd(a, att_w[k], qkv_bias[k], lo, hi, seg_col, seg_row, waits)
        return (kept[k][2],)

    (near_att,) = tie([near_att], (modulation,))
    att_w = [(v, 0) for v in (near_att, across(near_att, CORE), across(near_att, CHIP))]
    after = forward(1, forward(0, ()))
    (g_row.got,) = tie([g_row.got], after)
    g = g_row.whole()
    bg2, bg2_t, fc2_sum = by_rows(
        branch_body,
        6,
        (),
        [("t", g), ("w", modulation), ("t", seg_col)],
        [("t", *row_b), ("T", *turned), ("w", (1, d), f32)],
        waits=after,
    )
    (far_att,) = tie([att_w[2][0]], (fc2_sum,))
    att_w[2:] = [(far_att, 0), (across(far_att, CORE), 0)]
    after = forward(2, after)
    (far_w,) = tie([far_w], after)
    after = forward(3, after + (far_w,))
    partner_w = across(far_w, CORE)
    hidden, branch1, m, m_t = by_rows(
        middle_body,
        12,
        (),
        [("t", x)]
        + [("t", kept[k][3]) for k in range(4)]
        + [("w", modulation), ("t", seg_col), ("w", out_bias_row)],
        [("t", *row_f), ("t", *row_f), ("t", *row_b), ("T", *turned)],
    )
    done = {}
    def halves(w):
        return ((w, 0), (w, 1))

    done[3] = mlp_whole(m, bg2, m_t, bg2_t, halves(partner_w), fc1_part[3])
    init = across(done[3][3], CORE)
    done[2] = mlp_first(m, bg2, halves(far_w), fc1_part[2], (done[3][2],))
    (near_w,) = tie([near_w], (done[2][2],))
    partner_w = across(near_w, CORE)
    grad = mlp_second(m_t, bg2_t, *done[2][3:], init, (near_w,))
    far_sum = lax.psum_scatter(grad, "dp", scatter_dimension=0, tiled=True)
    done[1] = mlp_whole(m, bg2, m_t, bg2_t, halves(partner_w), fc1_part[1], (grad,))
    init = across(done[1][3], CORE)
    done[0] = mlp_first(m, bg2, halves(near_w), fc1_part[0], (done[1][2],))
    grad = mlp_second(m_t, bg2_t, *done[0][3:], init)
    near_sum = lax.psum_scatter(grad, "dp", scatter_dimension=0, tiled=True)
    block_output, hidden_grad, bg1, bg1_t, out_sum, img_late = by_rows(
        turn_body,
        5,
        (first, last),
        [("t", hidden), ("t", branch1), ("t", g)]
        + [("t", done[k][0]) for k in range(4)]
        + [("t", done[k][1]) for k in range(4)]
        + [("w", modulation), ("t", seg_col), ("w", fc2_bias_row)],
        [("t", *row_b), ("t", *row_f), ("t", *row_b), ("T", *turned), ("w", (1, d), f32), ("w", (IMG_ROW, 4 * d), f32)],
        waits=(grad,),
    )
    fc1_sum = jnp.zeros((1, 4 * ff), f32)
    for k in range(4):
        fc1_sum = lax.dynamic_update_slice_in_dim(fc1_sum, done[k][2], (tp_rank ^ k) * ff, 1)
    late = jnp.concatenate([jnp.zeros((IMG_ROW, 2 * d), f32), img_late], axis=1)
    late_sums = [jnp.sum(img_late, axis=0, keepdims=True), fc1_sum, fc2_sum, out_sum]
    late_sums = jnp.concatenate(late_sums, axis=1).reshape(32, -1)
    late = to_owners(late, late_sums, [])
    back = {}

    def backward(k, init, waits, parts=()):
        qkv, att, lse, _ = kept[k]
        back[k] = attend_bwd(
            qkv, att, bg1, bg1_t, a_t, att_w[k], lse, lo, hi, seg_col, seg_row, place, init, parts, waits
        )
        return (back[k][1],)

    block_output = trade_back(block_output, core)
    after = backward(1, None, ())
    init = across(back[1][2], CORE)
    (block_output,) = tie([block_output], after)
    after = backward(3, None, after + (block_output, far_sum))
    init, last_init = across(back[3][2], CORE), init
    after = backward(2, init, after, (4 * e,))
    (late,) = tie([late], after)
    late_grads, late_sums = taken_apart(late, IMG_ROW, mod_dev)
    far = Scatter(*back[2][2:])
    far_peer = across(far_sum, CHIP)
    after = backward(0, last_init, after, (4 * e,))
    far.got, far_peer = tie([far.got, far_peer], after)
    far.turn()
    near = Scatter(*back[0][2:])
    a_grad = back_to_input([back[k][0] for k in range(4)], att_w, (far.low,))
    (near.got,) = tie([near.got], (a_grad,))
    near.turn()
    input_grad, img_early = by_rows(
        leave_body,
        1,
        (first, last),
        [("t", x), ("t", hidden_grad), ("t", a_grad), ("w", modulation), ("t", seg_col)],
        [("t", *row_b), ("w", (IMG_ROW, 2 * d), f32)],
        waits=(near.low, near_sum),
    )
    far.got = tie(far.got, (img_early,))
    far_att = across(far.total().astype(bf16), CHIP)
    att_total = near.total() + far_att.astype(f32)
    near_sum = near_sum.astype(f32)
    fc1_grad = near_sum[:, :ff]
    fc2_grad = near_sum[:, ff:]
    far_peer = far_peer.astype(f32)
    fc1_grad, fc2_grad = fc1_grad + far_peer[:, :ff], fc2_grad + far_peer[:, ff:]
    qv_sum = jnp.zeros((2, 4 * e), f32)
    for k in range(4):
        grads = back[k][1].reshape(3, e)
        qv_sum = lax.dynamic_update_slice_in_dim(
            qv_sum, jnp.stack([grads[0], grads[2]]), (tp_rank ^ k) * e, 1
        )
    early = jnp.concatenate([img_early, jnp.zeros((IMG_ROW, 4 * d), f32)], axis=1)
    late_sums = jnp.sum(late_sums.astype(f32), axis=0, keepdims=True)
    early_sums = [late_sums, jnp.sum(img_early, axis=0, keepdims=True), qv_sum.reshape(1, -1)]
    early = to_owners(early, None, early_sums)
    early_grads, early_sums = taken_apart(early, IMG_ROW, mod_dev)
    share = late_sums.shape[1]
    used = (5 * d + d + 4 * ff) // 32
    late_sums = early_sums[:, :used].astype(f32).reshape(-1)
    late_bias, fc1_total, fc2_total, out_total = jnp.split(
        late_sums, [4 * d, 4 * d + 4 * ff, 5 * d + 4 * ff]
    )
    early_sums = jnp.sum(early_sums[:, share : share + 2 * d + 8 * e].astype(f32), axis=0)
    early_bias, qv_total = jnp.split(early_sums, [2 * d])
    qv_total = qv_total.reshape(2, -1)
    ada_total = jnp.concatenate([early_bias, late_bias])
    mod_grad = late_grads.astype(f32) + early_grads.astype(f32)
    ada_grad = lax.dot_general(
        lifted.astype(f32), mod_grad, (((0,), (0,)), ((), ())), precision=highest
    )
    return (
        block_output,
        trade_back(input_grad, core),
        jnp.stack([att_total[:, i * e : (i + 1) * e] for i in range(3)]),
        qv_total,
        att_total[:, 3 * e :].T,
        out_total,
        fc1_grad,
        fc1_total,
        fc2_grad.T,
        fc2_total,
        ada_grad,
        ada_total,
    )


def body(*arrays):
    block_input, w_qkv, w_fc1 = arrays[0], arrays[3], arrays[7]
    micro, tokens, width = block_input.shape
    heads_dev, rows = w_qkv.shape[2], w_fc1.shape[0]
    if (
        lax.axis_size("dp") == 8
        and lax.axis_size("tp") == 4
        and micro == 2
        and micro * tokens == PACK
        and rows == ROWS
        and rows * 8 == width
        and heads_dev * 4 == width
        and w_fc1.shape[1] % 384 == 0
    ):
        return row_body(*arrays)
    return general_body(*arrays)


def solution(mesh):
    placed = (
        P(None, ("dp", "tp"), None),
        P(None, "dp"),
        P(None, "dp", None),
        P(None, "dp", "tp"),
        P(),
        P("tp", "dp"),
        P(),
        P("dp", "tp"),
        P(),
        P("tp", "dp"),
        P(),
        P("dp", "tp"),
        P(),
        P(None, ("dp", "tp"), None),
    )
    return jax.shard_map(
        body,
        mesh=mesh,
        in_specs=placed,
        out_specs=(
            P(None, ("dp", "tp"), None),
            P(None, ("dp", "tp"), None),
            P(None, "dp", "tp"),
            P(),
            P("tp", "dp"),
            P(),
            P("dp", "tp"),
            P(),
            P("tp", "dp"),
            P(),
            P("dp", "tp"),
            P(),
        ),
        check_vma=False,
    )
```
